512 devices in a mesh: pos: 64 (over y, z_lo, core), off: 8 (over z_hi, x).
Axes of the slice: x: 4, y: 8, z: 8 (z_hi: 2, z_lo: 4; z = z_hi * 4 + z_lo), core: 2. Of those that a mesh axis runs over, the one named last changes fastest.
Arguments:
- counts: float32 [16384, 8192], P('pos', 'off'), as said below
- bin_mask: int32 [16384], P('pos'), may hold values 0 or 1
Outputs:
- donut_enrich: float32 [16384, 8192], P('pos', 'off')
- lower_enrich: float32 [16384, 8192], P('pos', 'off')
The draws below stay inside these ranges and needn't reach their ends.
Inputs may be any that keep to these rules, and one draw needn't show every extreme that they name: `counts`: every entry is a nonnegative whole number.
All inputs are finite; a program needn't handle non-finite values. No bound on the sum of `bin_mask` on one device may be relied on, other than what follows from the above.
Results may differ from the reference program's by a relative error of at most 0.00075.
Values sent between devices are 32-bit elements; how exact they have to be, the bound alone decides.
A program may use at most 64 MiB of HBM per device.

```python
import jax
import jax.numpy as jnp
from jax import lax

K = 8192
W = 20
P_SIZE = 8
NTOT = 16384


def draw_counts(key, part):
    row_key, noise_key = jax.random.split(key, 2)
    row_pos = jnp.arange(NTOT, dtype=jnp.float32) / NTOT
    off_pos = jnp.arange(K, dtype=jnp.float32)
    off_decay = 200.0 / (1.0 + off_pos / 16.0) ** 0.7
    row_scale = jnp.exp(jax.random.uniform(row_key, (NTOT,), jnp.float32, 0.0, jnp.log(10.0)))
    roughness = jnp.exp(jax.random.uniform(noise_key, (NTOT, K), jnp.float32, -0.7, 0.7))
    row_level = row_scale * 3.0 ** row_pos
    return jnp.floor(row_level[:, None] * off_decay[None, :] * roughness) + 1.0


def with_ends(entries, stream_key, least, top_value):
    dims = entries.shape
    index_at = [jax.random.randint(jax.random.fold_in(stream_key, axis), (), 0, dims[axis]) for axis in range(len(dims))]
    entries = entries.at[tuple(index_at)].set(least)
    longest = dims.index(max(dims))
    index_at[longest] = (index_at[longest] + 1) % dims[longest]
    return entries.at[tuple(index_at)].set(top_value)


def setup_inputs(seed: int = 0) -> dict:
    seeds = jax.random.split(jax.random.key(seed), 3)
    return {
        "counts": draw_counts(jax.random.fold_in(seeds[2], 71), 0),
        "bin_mask": with_ends((jax.random.randint(seeds[1], (NTOT,), 0, 10) < 9).astype(jnp.int32), jax.random.fold_in(seeds[1], 1), 0, 1),
    }


def reference(counts, bin_mask):
    total_bins, band_width = counts.shape
    row_index = jnp.arange(total_bins, dtype=jnp.int32)[:, None]
    off_index = jnp.arange(band_width, dtype=jnp.int32)[None, :]
    partner = row_index + off_index
    inside = partner < total_bins
    kept_counts = jnp.where(inside, counts, jnp.zeros_like(counts))
    coverage = lax.optimization_barrier(jnp.sum(kept_counts, axis=1))
    weight = bin_mask.astype(jnp.float32) / jnp.sqrt(coverage)
    weight_ext = jnp.concatenate([weight, jnp.zeros((band_width,), jnp.float32)])
    col_weight = jnp.take(weight_ext, partner)
    normed = kept_counts * weight[:, None] * col_weight
    live_pairs = ((weight[:, None] > 0) & (col_weight > 0)).astype(jnp.float32)
    pair_count = lax.optimization_barrier(jnp.sum(live_pairs, axis=0))
    expected = lax.optimization_barrier(jnp.sum(normed, axis=0))
    ratios = normed * (pair_count / jnp.where(expected > 0, expected, jnp.ones_like(expected)))[None, :]
    padded_ratio = jnp.pad(ratios, ((W, W), (2 * W, 2 * W)))
    prefix = jnp.concatenate([jnp.zeros((padded_ratio.shape[0], 1), jnp.float32), jnp.cumsum(padded_ratio, axis=1)], axis=1)

    def box_sum(displace, lowest, highest):
        anchor = 2 * W - displace
        upper = prefix[W + displace:W + displace + total_bins, anchor + highest + 1:anchor + highest + 1 + band_width]
        under = prefix[W + displace:W + displace + total_bins, anchor + lowest:anchor + lowest + band_width]
        return upper - under

    def center(displace):
        anchor = 2 * W - displace
        return padded_ratio[W + displace:W + displace + total_bins, anchor:anchor + band_width]
    donut_sum = jnp.zeros_like(ratios)
    lower_sum = jnp.zeros_like(ratios)
    for displace in range(-W, W + 1):
        if displace != 0:
            if abs(displace) <= P_SIZE:
                donut_sum = donut_sum + (box_sum(displace, -W, W) - box_sum(displace, -P_SIZE, P_SIZE))
            else:
                donut_sum = donut_sum + (box_sum(displace, -W, W) - center(displace))
        if displace > 0:
            addend = box_sum(displace, -W, -1)
            if displace <= P_SIZE:
                addend = addend - box_sum(displace, -P_SIZE, -1)
            lower_sum = lower_sum + addend
    donut_cells = (2 * W + 1) ** 2 - (2 * P_SIZE + 1) ** 2 - 4 * (W - P_SIZE)
    lower_cells = W * W - P_SIZE * P_SIZE
    donut_enrich = ratios / jnp.maximum(donut_sum / donut_cells, 0.25)
    lower_enrich = ratios / jnp.maximum(lower_sum / lower_cells, 0.25)
    return (donut_enrich, lower_enrich)
```

```python
import functools

import jax
import jax.numpy as jnp
from jax import lax
from jax.experimental import pallas as pl
from jax.experimental.pallas import tpu as pltpu
from jax.sharding import PartitionSpec as P

W = 20
P_SIZE = 8
TOP = 24
LANE = 128
SIDE = 64
STEP = 64
SPAN = STEP + 2 * TOP
MESH = pl.DeviceIdType.MESH


def comm_kernel(
    sizes, counts_ref, mask_ref, normed_ref, factor_ref, cells, cov, own, wts, row_w, tables, part, group,
    load_sem, cov_send, cov_recv, halo_send, halo_recv, wts_send, wts_recv, part_send, part_recv, group_send, group_recv,
):
    n_pos, n_off = sizes
    rows, cols = counts_ref.shape
    width = cols + LANE
    blocks = cols // LANE
    ratio = cols // rows
    inner = part.shape[0]
    outer = group.shape[0]
    pos = lax.axis_index("pos")
    off = lax.axis_index("off")
    total_bins = rows * n_pos
    band = cols * n_off
    row_halves = rows // LANE

    def at_pos(k):
        return lax.rem(pos + (k + n_pos), n_pos)

    def at_off(k):
        return lax.rem(off + (k + n_off), n_off)

    first = ratio * off
    quot = pos // inner
    rank = pos - quot * inner
    off_peers = [(pos, at_off(r)) for r in range(1, n_off)]
    halo_peers = [(at_pos(a), at_off(b)) for a in (-1, 1) for b in (-1, 0, 1)]
    steps = list(range(-1, ratio + 2))
    to_wts = [(lax.rem(pos - first - d + n_pos, n_pos), off) for d in steps]
    from_wts = [(lax.rem(pos + first + d + n_pos, n_pos), off) for d in steps]
    part_peers = [(quot * inner + lax.rem(rank + r, inner), off) for r in range(1, inner)]
    group_peers = [(lax.rem(quot + r, outer) * inner + rank, off) for r in range(1, outer)]

    barrier = pltpu.get_barrier_semaphore()

    def greet(device):
        pl.semaphore_signal(barrier, inc=1, device_id=device, device_id_type=MESH)

    for device in off_peers + halo_peers + part_peers + group_peers:
        greet(device)
    for d, there, here in zip(steps, to_wts, from_wts):
        if d == 0:

            @pl.when(off > 0)
            def _():
                greet(there)
                greet(here)
        else:
            greet(there)
            greet(here)

    load = pltpu.make_async_copy(counts_ref, cells.at[pl.ds(TOP, rows), pl.ds(0, cols)], load_sem)
    load.start()
    load.wait()

    base = pos * rows + off * cols
    acc = None
    for b in range(blocks):
        row_i = lax.broadcasted_iota(jnp.int32, (rows, LANE), 0)
        col_i = lax.broadcasted_iota(jnp.int32, (rows, LANE), 1)
        piece = cells[TOP : TOP + rows, b * LANE : (b + 1) * LANE]
        piece = jnp.where(row_i + col_i < total_bins - base - b * LANE, piece, 0.0)
        acc = piece if acc is None else acc + piece
    for h in range(row_halves):
        turned = acc[h * LANE : (h + 1) * LANE, :].T
        cov[0, h : h + 1, :] = jnp.sum(turned, axis=0, keepdims=True)

    n_greet = len(off_peers) + len(halo_peers) + len(part_peers) + len(group_peers) + 2 * (len(steps) - 1)
    pl.semaphore_wait(barrier, n_greet + jnp.where(off > 0, 2, 0))

    def remote(src, dst, send, recv, device):
        return pltpu.make_async_remote_copy(
            src_ref=src, dst_ref=dst, send_sem=send, recv_sem=recv, device_id=device, device_id_type=MESH
        )

    cov_copies = [
        remote(cov.at[0], cov.at[r], cov_send.at[r], cov_recv.at[r], off_peers[r - 1]) for r in range(1, n_off)
    ]
    for copy in cov_copies:
        copy.start()

    spans = {-1: (pl.ds(0, TOP), pl.ds(TOP + rows, TOP)), 1: (pl.ds(rows - TOP, TOP), pl.ds(0, TOP)), 0: (pl.ds(0, rows), pl.ds(TOP, rows))}
    strips = {
        -1: (pl.ds(0, LANE), pl.ds(cols, LANE)),
        1: (pl.ds(cols - LANE, LANE), pl.ds(cols + LANE, LANE)),
        0: (pl.ds(0, cols), pl.ds(0, cols)),
    }
    halo_copies = []
    for a, b in ((0, -1), (0, 1), (-1, 0), (1, 0), (-1, -1), (-1, 1), (1, -1), (1, 1)):
        k = len(halo_copies)
        halo_copies.append(
            remote(
                counts_ref.at[spans[a][0], strips[b][0]],
                cells.at[spans[a][1], strips[b][1]],
                halo_send.at[k],
                halo_recv.at[k],
                (at_pos(a), at_off(b)),
            )
        )
    for copy in halo_copies:
        copy.start()

    for copy in cov_copies:
        copy.wait_recv()
    coverage = cov[0]
    for r in range(1, n_off):
        coverage = coverage + cov[r]
    own[...] = mask_ref[...].astype(jnp.float32) / jnp.sqrt(coverage)

    n_steps = len(steps)
    wts_copies = [
        remote(own, wts.at[k], wts_send.at[k], wts_recv.at[k], to_wts[k]) for k in range(n_steps)
    ]
    for side, a in ((0, 1), (1, -1)):
        k = n_steps + side
        wts_copies.append(remote(own, wts.at[k], wts_send.at[k], wts_recv.at[k], (at_pos(a), off)))
    self_step = steps.index(0)
    for k, copy in enumerate(wts_copies):
        if k == self_step:
            pl.when(off > 0)(copy.start)
        else:
            copy.start()

    @pl.when(off == 0)
    def _():
        wts[self_step] = own[...]

    def down(vector):
        return jnp.broadcast_to(vector, (LANE, LANE)).T

    for h in range(row_halves):
        row_w[TOP + h * LANE : TOP + (h + 1) * LANE, :] = down(own[h : h + 1, :])

    for k, copy in enumerate(wts_copies):
        if k == self_step:
            pl.when(off > 0)(copy.wait_recv)
        else:
            copy.wait_recv()

    pieces = []
    for k, d in enumerate(steps):
        block = pos + first + d
        inside = (block >= 0) & (block < n_pos)
        for h in range(row_halves):
            pieces.append(jnp.where(inside, wts[k, h : h + 1, :], 0.0))
    line = jnp.concatenate(pieces, axis=1)
    reach = line.shape[1]
    line = jnp.broadcast_to(line, (8, reach))
    line = pltpu.roll(line, reach - 7, 1, stride=1, stride_axis=0)
    flip = 7 - lax.broadcasted_iota(jnp.int32, (8, reach), 0)
    line = jnp.take_along_axis(line, flip, axis=0)
    phases = LANE // 8
    for h in range(phases):
        tables[h] = line if h == 0 else pltpu.roll(line, reach - 8 * h, 1)

    low_lanes = lax.broadcasted_iota(jnp.int32, (8, LANE), 1) < SIDE

    def row_group(g):
        rows_g = slice(8 * g, 8 * g + 8)
        place = 8 * g + rows - TOP
        h, shift = (place % LANE) // 8, place // LANE * LANE
        weight = row_w[rows_g, :]
        outs = []
        for b in range(blocks + 1):
            if b < blocks:
                count = cells[rows_g, b * LANE : (b + 1) * LANE]
                col = tables[h, :, shift + b * LANE : shift + (b + 1) * LANE]
            else:
                count = jnp.where(
                    low_lanes, cells[rows_g, cols : cols + LANE], cells[rows_g, cols + LANE : cols + 2 * LANE]
                )
                col = jnp.where(
                    low_lanes,
                    tables[h, :, shift + cols : shift + cols + LANE],
                    tables[h, :, shift - LANE : shift],
                )
            value = count * weight * col
            normed_ref[rows_g, b * LANE : (b + 1) * LANE] = value
            outs.append((value, jnp.where((weight > 0) & (col > 0), 1.0, 0.0)))
        return outs

    halo_copies[0].wait_recv()
    halo_copies[1].wait_recv()
    sums = [None] * (2 * (blocks + 1))
    for g in range(TOP // 8, (TOP + rows) // 8):
        for b, (value, live) in enumerate(row_group(g)):
            for k, term in ((b, value), (blocks + 1 + b, live)):
                sums[k] = term if sums[k] is None else sums[k] + term
    for k, total in enumerate(sums):
        part[0, k : k + 1, :] = jnp.sum(total, axis=0, keepdims=True)

    part_copies = [
        remote(part.at[0], part.at[r], part_send.at[r], part_recv.at[r], part_peers[r - 1]) for r in range(1, inner)
    ]
    for copy in part_copies:
        copy.start()

    for copy in halo_copies[2:]:
        copy.wait_recv()
    for side, h, low, place in ((0, row_halves - 1, LANE - TOP, 0), (1, 0, 0, TOP + rows)):
        block = pos + (1 if side else -1)
        inside = (block >= 0) & (block < n_pos)
        weight = jnp.where(inside, wts[n_steps + side, h : h + 1, :], 0.0)
        row_w[place : place + TOP, :] = down(weight)[low : low + TOP, :]
    for g in list(range(TOP // 8)) + list(range((TOP + rows) // 8, (2 * TOP + rows) // 8)):
        row_group(g)

    for copy in part_copies:
        copy.wait_recv()
    total = part[0]
    for r in range(1, inner):
        total = total + part[r]
    group[0] = total
    group_copies = [
        remote(group.at[0], group.at[r], group_send.at[r], group_recv.at[r], group_peers[r - 1])
        for r in range(1, outer)
    ]
    for copy in group_copies:
        copy.start()
    for copy in group_copies:
        copy.wait_recv()
    total = group[0]
    for r in range(1, outer):
        total = total + group[r]
    expected = total[: blocks + 1, :]
    pairs = total[blocks + 1 :, :]
    lane = lax.broadcasted_iota(jnp.int32, expected.shape, 1)
    place = lax.broadcasted_iota(jnp.int32, expected.shape, 0) * LANE + lane
    place = off * cols + jnp.where(place < cols + SIDE, place, place - width)
    factor = pairs / jnp.where(expected > 0, expected, 1.0)
    factor_ref[...] = jnp.where((place >= 0) & (place < band), factor, 0.0)

    for copy in cov_copies + halo_copies + part_copies + group_copies:
        copy.wait_send()
    for k, copy in enumerate(wts_copies):
        if k == self_step:
            pl.when(off > 0)(copy.wait_send)
        else:
            copy.wait_send()


def near(distance, lowest, highest):
    return (distance >= lowest) & (distance <= highest)


def both(mask_a, mask_b):
    return jnp.where(mask_a | mask_b, 1.0, 0.0).astype(jnp.bfloat16)


def halves(values):
    high = values.astype(jnp.bfloat16)
    return high, (values - high.astype(jnp.float32)).astype(jnp.bfloat16)


def window_kernel(normed_ref, factor_ref, donut_ref, lower_ref, down_table, side_table):
    step = pl.program_id(0)
    width = normed_ref.shape[1]
    cols = donut_ref.shape[1]
    blocks = width // LANE

    @pl.when(step == 0)
    def _():
        out_row = lax.broadcasted_iota(jnp.int32, (STEP, 2 * SPAN), 0)
        out_row = (out_row // 8) * 8 + 7 - lax.rem(out_row, 8)
        in_row = lax.broadcasted_iota(jnp.int32, (STEP, 2 * SPAN), 1)
        in_row = jnp.where(in_row < SPAN, in_row, in_row - SPAN)
        a = in_row - TOP - out_row
        down_table[0:STEP, :] = both(near(a, P_SIZE + 1, W), near(a, -W, -P_SIZE - 1))
        down_table[STEP : 2 * STEP, :] = both(near(a, 1, P_SIZE), near(a, -P_SIZE, -1))
        down_table[2 * STEP : 3 * STEP, :] = both(near(a, P_SIZE + 1, W), near(a, P_SIZE + 1, W))
        down_table[3 * STEP :, :] = both(near(a, 1, P_SIZE), near(a, 1, P_SIZE))
        shape = (2 * LANE, LANE)
        b = lax.broadcasted_iota(jnp.int32, shape, 0) - SIDE - lax.broadcasted_iota(jnp.int32, shape, 1)
        side_table[0] = both(near(b, 1, W), near(b, -W, -1))
        side_table[1] = both(near(b, P_SIZE + 1, W), near(b, -W, -P_SIZE - 1))
        side_table[2] = both(near(b, -W, -1), near(b, -W, -1))
        side_table[3] = both(near(b, -W, -P_SIZE - 1), near(b, -W, -P_SIZE - 1))

    start = pl.multiple_of(step * STEP, STEP)
    factor = jnp.concatenate([factor_ref[b : b + 1, :] for b in range(blocks)], axis=1)
    ratios = normed_ref[pl.ds(start, SPAN), :] * factor
    level = pltpu.roll(ratios, SIDE, 1, stride=1, stride_axis=0)
    stacked = jnp.concatenate(halves(level), axis=0)
    summed = jnp.dot(down_table[...], stacked, preferred_element_type=jnp.float32)

    def sideways(k):
        parts = []
        for half in halves(summed[k * STEP : (k + 1) * STEP, :]):
            around = jnp.concatenate([half, half[:, :LANE]], axis=1)
            parts.append(jnp.concatenate([around[:, b * LANE : (b + 2) * LANE] for b in range(blocks)], axis=0))
        table = side_table[k]
        result = jnp.dot(parts[0], table, preferred_element_type=jnp.float32)
        return result + jnp.dot(parts[1], table, preferred_element_type=jnp.float32)

    flip = 7 - lax.broadcasted_iota(jnp.int32, (8, cols), 0)
    here = ratios[TOP : TOP + STEP, :cols]
    cells_donut = (2 * W + 1) ** 2 - (2 * P_SIZE + 1) ** 2 - 4 * (W - P_SIZE)
    cells_lower = W * W - P_SIZE * P_SIZE
    for out_ref, k, cell_count in ((donut_ref, 0, cells_donut), (lower_ref, 2, cells_lower)):
        tall = sideways(k) + sideways(k + 1)
        flat = jnp.concatenate([tall[b * STEP : (b + 1) * STEP, :] for b in range(blocks)], axis=1)
        for g in range(STEP // 8):
            rows_g = slice(8 * g, 8 * g + 8)
            back = pltpu.roll(flat[rows_g, :], width - TOP - 8 * g - 7, 1, stride=1, stride_axis=0)[:, :cols]
            back = jnp.take_along_axis(back, flip, axis=0)
            out_ref[rows_g, :] = here[rows_g, :] / jnp.maximum(back / cell_count, 0.25)


def local(counts, bin_mask):
    rows, cols = counts.shape
    n_pos = lax.axis_size("pos")
    n_off = lax.axis_size("off")
    inner = 8
    outer = n_pos // inner
    width = cols + LANE
    vecs = 2 * (cols // LANE + 1)
    n_wts = cols // rows + 5
    reach = (cols // rows + 3) * rows
    dma = pltpu.SemaphoreType.DMA
    normed, factor = pl.pallas_call(
        functools.partial(comm_kernel, (n_pos, n_off)),
        out_shape=(
            pltpu.VMEM((rows + 2 * TOP, width), jnp.float32),
            pltpu.VMEM((vecs // 2, LANE), jnp.float32),
        ),
        in_specs=[pl.BlockSpec(memory_space=pl.ANY), pl.BlockSpec(memory_space=pltpu.VMEM)],
        out_specs=(pl.BlockSpec(memory_space=pltpu.VMEM), pl.BlockSpec(memory_space=pltpu.VMEM)),
        scratch_shapes=[
            pltpu.VMEM((rows + 2 * TOP, cols + 2 * LANE), jnp.float32),
            pltpu.VMEM((n_off, rows // LANE, LANE), jnp.float32),
            pltpu.VMEM((rows // LANE, LANE), jnp.float32),
            pltpu.VMEM((n_wts, rows // LANE, LANE), jnp.float32),
            pltpu.VMEM((rows + 2 * TOP, LANE), jnp.float32),
            pltpu.VMEM((LANE // 8, 8, reach), jnp.float32),
            pltpu.VMEM((inner, vecs, LANE), jnp.float32),
            pltpu.VMEM((outer, vecs, LANE), jnp.float32),
            dma,
            dma((n_off,)),
            dma((n_off,)),
            dma((8,)),
            dma((8,)),
            dma((n_wts,)),
            dma((n_wts,)),
            dma((inner,)),
            dma((inner,)),
            dma((outer,)),
            dma((outer,)),
        ],
        compiler_params=pltpu.CompilerParams(
            collective_id=0, has_side_effects=True, vmem_limit_bytes=24 * 1024 * 1024
        ),
        name="comm",
    )(counts, bin_mask.reshape(rows // LANE, LANE))
    out = jax.ShapeDtypeStruct((rows, cols), jnp.float32)
    return pl.pallas_call(
        window_kernel,
        grid=(rows // STEP,),
        out_shape=(out, out),
        in_specs=[pl.BlockSpec(memory_space=pltpu.VMEM), pl.BlockSpec(memory_space=pltpu.VMEM)],
        out_specs=(pl.BlockSpec((STEP, cols), lambda i: (i, 0)), pl.BlockSpec((STEP, cols), lambda i: (i, 0))),
        scratch_shapes=[
            pltpu.VMEM((4 * STEP, 2 * SPAN), jnp.bfloat16),
            pltpu.VMEM((4, 2 * LANE, LANE), jnp.bfloat16),
        ],
        compiler_params=pltpu.CompilerParams(vmem_limit_bytes=24 * 1024 * 1024),
        name="windows",
    )(normed, factor)


def solution(mesh):
    placed = (P("pos", "off"), P("pos"))
    return jax.shard_map(
        local,
        mesh=mesh,
        in_specs=placed,
        out_specs=(P("pos", "off"), P("pos", "off")),
        check_vma=False,
    )
```

```python
import functools

import jax
import jax.numpy as jnp
from jax import lax
from jax.experimental import pallas as pl
from jax.experimental.pallas import tpu as pltpu
from jax.sharding import PartitionSpec as P

W = 20
P_SIZE = 8
TOP = 24
LANE = 128
SIDE = 64
STEP = 64
SPAN = STEP + 2 * TOP
MESH = pl.DeviceIdType.MESH


def comm_kernel(
    sizes, counts_ref, mask_ref, normed_ref, factor_ref,
    cells, strips_out, strips_in, mask, cov, own, wts, lines, row_w, tables, part, group,
    load_sem, mask_sem, cov_send, cov_recv, halo_send, halo_recv, wts_send, wts_recv, part_send, part_recv, group_send, group_recv,
):
    n_pos, n_off = sizes
    rows, cols = counts_ref.shape
    width = cols + LANE
    blocks = cols // LANE
    ratio = cols // rows
    near_offs = cov.shape[0]
    far_offs = n_off // near_offs
    inner = part.shape[0]
    outer = group.shape[0]
    pos = lax.axis_index("pos")
    off = lax.axis_index("off")
    total_bins = rows * n_pos
    band = cols * n_off
    row_halves = rows // LANE
    third = strips_in.shape[1]

    def at_pos(k):
        return lax.rem(pos + (k + n_pos), n_pos)

    def at_off(k):
        return lax.rem(off + (k + n_off), n_off)

    first = ratio * off
    far = off // near_offs
    near = off - far * near_offs
    quot = pos // inner
    rank = pos - quot * inner
    cov_peers = [(pos, far * near_offs + lax.rem(near + r, near_offs)) for r in range(1, near_offs)]
    halo_moves = [(0, -1), (0, 1), (-1, 0), (1, 0), (-1, -1), (-1, 1), (1, -1), (1, 1)]
    steps = list(range(-1, ratio + 2))
    n_steps = len(steps)
    self_step = steps.index(0)
    n_slots = n_steps + 3
    part_peers = [(quot * inner + lax.rem(rank + r, inner), off) for r in range(1, inner)]
    group_peers = [(lax.rem(quot + r, outer) * inner + rank, off) for r in range(1, outer)]

    def wts_target(t, slot):
        there = lax.rem(far + t, far_offs) * near_offs + near
        if slot < n_steps:
            return (lax.rem(pos - ratio * there - steps[slot] + n_pos, n_pos), there)
        return (at_pos((1, -1, 0)[slot - n_steps]), there)

    def wts_source(t, slot):
        there = lax.rem(far - t + far_offs, far_offs) * near_offs + near
        if slot < n_steps:
            return (lax.rem(pos + first + steps[slot] + n_pos, n_pos), there)
        return (at_pos((-1, 1, 0)[slot - n_steps]), there)

    moves = []
    for t in list(range(1, far_offs)) + [0]:
        for slot in range(n_slots):
            if t or slot != n_slots - 1:
                moves.append((t, slot, t == 0 and slot == self_step))

    barrier = pltpu.get_barrier_semaphore()

    def greet(device):
        pl.semaphore_signal(barrier, inc=1, device_id=device, device_id_type=MESH)

    for device in cov_peers:
        greet(device)
    for t, slot, selfish in moves:
        if selfish:
            pl.when(off > 0)(functools.partial(greet, wts_source(t, slot)))
        else:
            greet(wts_source(t, slot))
    for a, b in halo_moves:
        greet((at_pos(-a), at_off(-b)))
    for device in part_peers + group_peers:
        greet(device)

    load = pltpu.make_async_copy(counts_ref, cells.at[pl.ds(TOP, rows), pl.ds(0, cols)], load_sem)
    load.start()
    load_mask = pltpu.make_async_copy(mask_ref, mask, mask_sem)
    load_mask.start()

    @pl.when(off == 0)
    def _():
        strips_in[1] = jnp.zeros(strips_in.shape[1:], jnp.float32)
        for place in (0, TOP + rows):
            cells[place : place + TOP, cols + LANE :] = jnp.zeros((TOP, LANE), jnp.float32)

    @pl.when(off == n_off - 1)
    def _():
        strips_in[0] = jnp.zeros(strips_in.shape[1:], jnp.float32)
        for place in (0, TOP + rows):
            cells[place : place + TOP, cols : cols + LANE] = jnp.zeros((TOP, LANE), jnp.float32)

    load.wait()

    base = pos * rows + off * cols
    acc = None
    for b in range(blocks):
        row_i = lax.broadcasted_iota(jnp.int32, (rows, LANE), 0)
        col_i = lax.broadcasted_iota(jnp.int32, (rows, LANE), 1)
        piece = cells[TOP : TOP + rows, b * LANE : (b + 1) * LANE]
        piece = jnp.where(row_i + col_i < total_bins - base - b * LANE, piece, 0.0)
        acc = piece if acc is None else acc + piece
    for h in range(row_halves):
        turned = acc[h * LANE : (h + 1) * LANE, :].T
        cov[0, h : h + 1, :] = jnp.sum(turned, axis=0, keepdims=True)
    load_mask.wait()

    n_greet = len(cov_peers) + len(moves) - 1 + len(halo_moves) + len(part_peers) + len(group_peers)
    pl.semaphore_wait(barrier, n_greet + jnp.where(off > 0, 1, 0))

    def remote(src, dst, send, recv, device):
        return pltpu.make_async_remote_copy(
            src_ref=src, dst_ref=dst, send_sem=send, recv_sem=recv, device_id=device, device_id_type=MESH
        )

    cov_copies = [
        remote(cov.at[0], cov.at[r], cov_send.at[r], cov_recv.at[r], cov_peers[r - 1]) for r in range(1, near_offs)
    ]
    for copy in cov_copies:
        copy.start()

    spare = LANE // 3
    lane_t = lax.broadcasted_iota(jnp.int32, (third, LANE), 1)
    for side in (0, 1):
        packed = None
        for k in range(3):
            low = TOP + k * third
            high = min(low + third, TOP + rows)
            piece = cells[low:high, 0:LANE] if side == 0 else cells[low:high, cols - LANE : cols]
            if high - low < third:
                piece = jnp.concatenate([piece, jnp.zeros((third - high + low, LANE), jnp.float32)], axis=0)
            if side == 0:
                piece = pltpu.roll(piece, k * spare, 1) if k else piece
                here = (lane_t >= k * spare) & (lane_t < (k + 1) * spare)
            else:
                piece = pltpu.roll(piece, LANE - k * spare, 1) if k else piece
                here = (lane_t < LANE - k * spare) & (lane_t >= LANE - (k + 1) * spare)
            packed = jnp.where(here, piece, 0.0 if packed is None else packed)
        strips_out[side] = packed

    spans = {-1: (pl.ds(0, TOP), pl.ds(TOP + rows, TOP)), 1: (pl.ds(rows - TOP, TOP), pl.ds(0, TOP))}
    strips = {
        -1: (pl.ds(0, LANE), pl.ds(cols, LANE)),
        1: (pl.ds(cols - LANE, LANE), pl.ds(cols + LANE, LANE)),
        0: (pl.ds(0, cols), pl.ds(0, cols)),
    }
    halo_copies = []
    for k, (a, b) in enumerate(halo_moves):
        if a == 0:
            side = 0 if b < 0 else 1
            ends = strips_out.at[side], strips_in.at[side]
        else:
            ends = counts_ref.at[spans[a][0], strips[b][0]], cells.at[spans[a][1], strips[b][1]]
        halo_copies.append(remote(*ends, halo_send.at[k], halo_recv.at[k], (at_pos(a), at_off(b))))

    def sends(b):
        return off > 0 if b < 0 else off < n_off - 1

    def each_halo(copies, act):
        for (a, b), copy in copies:
            if b == 0:
                getattr(copy, act)()
            elif act == "wait_recv":
                pl.when(sends(-b))(copy.wait_recv)
            else:
                pl.when(sends(b))(getattr(copy, act))

    halos = list(zip(halo_moves, halo_copies))
    each_halo(halos, "start")

    for copy in cov_copies:
        copy.wait_recv()
    coverage = cov[0]
    for r in range(1, near_offs):
        coverage = coverage + cov[r]
    own[0:row_halves, :] = coverage
    own[row_halves:, :] = mask[...].astype(jnp.float32)

    wts_copies = [
        remote(own, wts.at[t, slot], wts_send.at[t, slot], wts_recv.at[t, slot], wts_target(t, slot))
        for t, slot, _ in moves
    ]

    def each_wts(act):
        for (_, _, selfish), copy in zip(moves, wts_copies):
            if selfish:
                pl.when(off > 0)(getattr(copy, act))
            else:
                getattr(copy, act)()

    each_wts("start")
    wts[0, n_slots - 1] = own[...]

    @pl.when(off == 0)
    def _():
        wts[0, self_step] = own[...]

    each_wts("wait_recv")

    gathered = wts[0, :, 0:row_halves, :]
    for t in range(1, far_offs):
        gathered = gathered + wts[t, :, 0:row_halves, :]
    lines[...] = wts[0, :, row_halves:, :] / jnp.sqrt(gathered)

    def down(vector):
        return jnp.broadcast_to(vector, (LANE, LANE)).T

    for h in range(row_halves):
        row_w[TOP + h * LANE : TOP + (h + 1) * LANE, :] = down(lines[n_slots - 1, h : h + 1, :])

    pieces = []
    for k, d in enumerate(steps):
        block = pos + first + d
        inside = (block >= 0) & (block < n_pos)
        for h in range(row_halves):
            pieces.append(jnp.where(inside, lines[k, h : h + 1, :], 0.0))
    line = jnp.concatenate(pieces, axis=1)
    reach = line.shape[1]
    line = jnp.broadcast_to(line, (8, reach))
    line = pltpu.roll(line, reach - 7, 1, stride=1, stride_axis=0)
    flip = 7 - lax.broadcasted_iota(jnp.int32, (8, reach), 0)
    line = jnp.take_along_axis(line, flip, axis=0)
    phases = LANE // 8
    for h in range(phases):
        tables[h] = line if h == 0 else pltpu.roll(line, reach - 8 * h, 1)

    lane_8 = lax.broadcasted_iota(jnp.int32, (8, LANE), 1)
    low_lanes = lane_8 < SIDE

    def row_group(g):
        rows_g = slice(8 * g, 8 * g + 8)
        place = 8 * g + rows - TOP
        h, shift = (place % LANE) // 8, place // LANE * LANE
        weight = row_w[rows_g, :]
        outs = []
        for b in range(blocks + 1):
            if b < blocks:
                count = cells[rows_g, b * LANE : (b + 1) * LANE]
                col = tables[h, :, shift + b * LANE : shift + (b + 1) * LANE]
            else:
                own_row = 8 * g - TOP
                if 0 <= own_row < rows:
                    k, at = own_row // third, own_row % third
                    after, before = strips_in[0, at : at + 8, :], strips_in[1, at : at + 8, :]
                    if k:
                        after = pltpu.roll(after, LANE - k * spare, 1)
                        before = pltpu.roll(before, k * spare, 1)
                else:
                    after, before = cells[rows_g, cols : cols + LANE], cells[rows_g, cols + LANE : cols + 2 * LANE]
                count = jnp.where(low_lanes, after, before)
                col = jnp.where(
                    low_lanes,
                    tables[h, :, shift + cols : shift + cols + LANE],
                    tables[h, :, shift - LANE : shift],
                )
            value = count * weight * col
            normed_ref[rows_g, b * LANE : (b + 1) * LANE] = value
            outs.append((value, jnp.where((weight > 0) & (col > 0), 1.0, 0.0)))
        return outs

    each_halo(halos[:2], "wait_recv")
    sums = [None] * (2 * (blocks + 1))
    for g in range(TOP // 8, (TOP + rows) // 8):
        for b, (value, live) in enumerate(row_group(g)):
            for k, term in ((b, value), (blocks + 1 + b, live)):
                sums[k] = term if sums[k] is None else sums[k] + term
    for k, total in enumerate(sums):
        part[0, k : k + 1, :] = jnp.sum(total, axis=0, keepdims=True)

    part_copies = [
        remote(part.at[0], part.at[r], part_send.at[r], part_recv.at[r], part_peers[r - 1]) for r in range(1, inner)
    ]
    for copy in part_copies:
        copy.start()

    each_halo(halos[2:], "wait_recv")
    for side, h, low, place in ((0, row_halves - 1, LANE - TOP, 0), (1, 0, 0, TOP + rows)):
        block = pos + (1 if side else -1)
        inside = (block >= 0) & (block < n_pos)
        weight = jnp.where(inside, lines[n_steps + side, h : h + 1, :], 0.0)
        row_w[place : place + TOP, :] = down(weight)[low : low + TOP, :]
    for g in list(range(TOP // 8)) + list(range((TOP + rows) // 8, (2 * TOP + rows) // 8)):
        row_group(g)

    for copy in part_copies:
        copy.wait_recv()
    total = part[0]
    for r in range(1, inner):
        total = total + part[r]
    group[0] = total
    group_copies = [
        remote(group.at[0], group.at[r], group_send.at[r], group_recv.at[r], group_peers[r - 1])
        for r in range(1, outer)
    ]
    for copy in group_copies:
        copy.start()
    for copy in cov_copies + part_copies:
        copy.wait_send()
    each_halo(halos, "wait_send")
    each_wts("wait_send")
    for copy in group_copies:
        copy.wait_recv()
    total = group[0]
    for r in range(1, outer):
        total = total + group[r]
    expected = total[: blocks + 1, :]
    pairs = total[blocks + 1 :, :]
    lane = lax.broadcasted_iota(jnp.int32, expected.shape, 1)
    place = lax.broadcasted_iota(jnp.int32, expected.shape, 0) * LANE + lane
    needed = (place < cols + 2 * W) | (place >= width - 2 * W)
    place = off * cols + jnp.where(place < cols + SIDE, place, place - width)
    factor = pairs / jnp.where(expected > 0, expected, 1.0)
    factor_ref[...] = jnp.where(needed & (place >= 0) & (place < band), factor, 0.0)
    for copy in group_copies:
        copy.wait_send()


def near(distance, lowest, highest):
    return (distance >= lowest) & (distance <= highest)


def both(mask_a, mask_b):
    return jnp.where(mask_a | mask_b, 1.0, 0.0).astype(jnp.bfloat16)


def halves(values):
    high = values.astype(jnp.bfloat16)
    return high, (values - high.astype(jnp.float32)).astype(jnp.bfloat16)


def window_kernel(normed_ref, factor_ref, donut_ref, lower_ref, down_table, side_table):
    step = pl.program_id(0)
    width = normed_ref.shape[1]
    cols = donut_ref.shape[1]
    blocks = width // LANE

    @pl.when(step == 0)
    def _():
        out_row = lax.broadcasted_iota(jnp.int32, (STEP, 2 * SPAN), 0)
        out_row = (out_row // 8) * 8 + 7 - lax.rem(out_row, 8)
        in_row = lax.broadcasted_iota(jnp.int32, (STEP, 2 * SPAN), 1)
        in_row = jnp.where(in_row < SPAN, in_row, in_row - SPAN)
        a = in_row - TOP - out_row
        down_table[0:STEP, :] = both(near(a, P_SIZE + 1, W), near(a, -W, -P_SIZE - 1))
        down_table[STEP : 2 * STEP, :] = both(near(a, 1, P_SIZE), near(a, -P_SIZE, -1))
        down_table[2 * STEP : 3 * STEP, :] = both(near(a, P_SIZE + 1, W), near(a, P_SIZE + 1, W))
        down_table[3 * STEP :, :] = both(near(a, 1, P_SIZE), near(a, 1, P_SIZE))
        shape = (2 * LANE, LANE)
        b = lax.broadcasted_iota(jnp.int32, shape, 0) - SIDE - lax.broadcasted_iota(jnp.int32, shape, 1)
        side_table[0] = both(near(b, 1, W), near(b, -W, -1))
        side_table[1] = both(near(b, P_SIZE + 1, W), near(b, -W, -P_SIZE - 1))
        side_table[2] = both(near(b, -W, -1), near(b, -W, -1))
        side_table[3] = both(near(b, -W, -P_SIZE - 1), near(b, -W, -P_SIZE - 1))

    start = pl.multiple_of(step * STEP, STEP)
    factor = jnp.concatenate([factor_ref[b : b + 1, :] for b in range(blocks)], axis=1)
    ratios = normed_ref[pl.ds(start, SPAN), :] * factor
    level = pltpu.roll(ratios, SIDE, 1, stride=1, stride_axis=0)
    stacked = jnp.concatenate(halves(level), axis=0)
    summed = jnp.dot(down_table[...], stacked, preferred_element_type=jnp.float32)

    def sideways(k):
        parts = []
        for half in halves(summed[k * STEP : (k + 1) * STEP, :]):
            around = jnp.concatenate([half, half[:, :LANE]], axis=1)
            parts.append(jnp.concatenate([around[:, b * LANE : (b + 2) * LANE] for b in range(blocks)], axis=0))
        table = side_table[k]
        result = jnp.dot(parts[0], table, preferred_element_type=jnp.float32)
        return result + jnp.dot(parts[1], table, preferred_element_type=jnp.float32)

    flip = 7 - lax.broadcasted_iota(jnp.int32, (8, cols), 0)
    here = ratios[TOP : TOP + STEP, :cols]
    cells_donut = (2 * W + 1) ** 2 - (2 * P_SIZE + 1) ** 2 - 4 * (W - P_SIZE)
    cells_lower = W * W - P_SIZE * P_SIZE
    for out_ref, k, cell_count in ((donut_ref, 0, cells_donut), (lower_ref, 2, cells_lower)):
        tall = sideways(k) + sideways(k + 1)
        flat = jnp.concatenate([tall[b * STEP : (b + 1) * STEP, :] for b in range(blocks)], axis=1)
        for g in range(STEP // 8):
            rows_g = slice(8 * g, 8 * g + 8)
            back = pltpu.roll(flat[rows_g, :], width - TOP - 8 * g - 7, 1, stride=1, stride_axis=0)[:, :cols]
            back = jnp.take_along_axis(back, flip, axis=0)
            out_ref[rows_g, :] = here[rows_g, :] / jnp.maximum(back / cell_count, 0.25)


def local(counts, bin_mask):
    rows, cols = counts.shape
    n_pos = lax.axis_size("pos")
    n_off = lax.axis_size("off")
    inner = 8
    outer = n_pos // inner
    near_offs = 4
    far_offs = n_off // near_offs
    width = cols + LANE
    vecs = 2 * (cols // LANE + 1)
    n_slots = cols // rows + 6
    reach = (cols // rows + 3) * rows
    halves_n = rows // LANE
    third = -(-rows // 24) * 8
    dma = pltpu.SemaphoreType.DMA
    f32 = jnp.float32
    normed, factor = pl.pallas_call(
        functools.partial(comm_kernel, (n_pos, n_off)),
        out_shape=(
            pltpu.VMEM((rows + 2 * TOP, width), f32),
            pltpu.VMEM((vecs // 2, LANE), f32),
        ),
        in_specs=[pl.BlockSpec(memory_space=pltpu.HBM), pl.BlockSpec(memory_space=pltpu.HBM)],
        out_specs=(pl.BlockSpec(memory_space=pltpu.VMEM), pl.BlockSpec(memory_space=pltpu.VMEM)),
        scratch_shapes=[
            pltpu.VMEM((rows + 2 * TOP, cols + 2 * LANE), f32),
            pltpu.VMEM((2, third, LANE), f32),
            pltpu.VMEM((2, third, LANE), f32),
            pltpu.VMEM((halves_n, LANE), jnp.int32),
            pltpu.VMEM((near_offs, halves_n, LANE), f32),
            pltpu.VMEM((2 * halves_n, LANE), f32),
            pltpu.VMEM((far_offs, n_slots, 2 * halves_n, LANE), f32),
            pltpu.VMEM((n_slots, halves_n, LANE), f32),
            pltpu.VMEM((rows + 2 * TOP, LANE), f32),
            pltpu.VMEM((LANE // 8, 8, reach), f32),
            pltpu.VMEM((inner, vecs, LANE), f32),
            pltpu.VMEM((outer, vecs, LANE), f32),
            dma,
            dma,
            dma((near_offs,)),
            dma((near_offs,)),
            dma((8,)),
            dma((8,)),
            dma((far_offs, n_slots)),
            dma((far_offs, n_slots)),
            dma((inner,)),
            dma((inner,)),
            dma((outer,)),
            dma((outer,)),
        ],
        compiler_params=pltpu.CompilerParams(
            collective_id=0, has_side_effects=True, vmem_limit_bytes=24 * 1024 * 1024
        ),
        name="comm",
    )(
        pltpu.with_memory_space_constraint(counts, pltpu.HBM),
        pltpu.with_memory_space_constraint(bin_mask.reshape(halves_n, LANE), pltpu.HBM),
    )
    out = jax.ShapeDtypeStruct((rows, cols), jnp.float32)
    return pl.pallas_call(
        window_kernel,
        grid=(rows // STEP,),
        out_shape=(out, out),
        in_specs=[pl.BlockSpec(memory_space=pltpu.VMEM), pl.BlockSpec(memory_space=pltpu.VMEM)],
        out_specs=(pl.BlockSpec((STEP, cols), lambda i: (i, 0)), pl.BlockSpec((STEP, cols), lambda i: (i, 0))),
        scratch_shapes=[
            pltpu.VMEM((4 * STEP, 2 * SPAN), jnp.bfloat16),
            pltpu.VMEM((4, 2 * LANE, LANE), jnp.bfloat16),
        ],
        compiler_params=pltpu.CompilerParams(vmem_limit_bytes=24 * 1024 * 1024),
        name="windows",
    )(normed, factor)


def solution(mesh):
    placed = (P("pos", "off"), P("pos"))
    return jax.shard_map(
        local,
        mesh=mesh,
        in_specs=placed,
        out_specs=(P("pos", "off"), P("pos", "off")),
        check_vma=False,
    )
```

```python
import functools

import jax
import jax.numpy as jnp
from jax import lax
from jax.experimental import pallas as pl
from jax.experimental.pallas import tpu as pltpu
from jax.sharding import PartitionSpec as P

W = 20
P_SIZE = 8
TOP = 24
LANE = 128
SIDE = 64
STEP = 64
SPAN = STEP + 2 * TOP
MESH = pl.DeviceIdType.MESH


def comm_kernel(
    sizes, counts_ref, mask_ref, normed_ref, factor_ref,
    cells, strips_out, strips_in, mask, cov, own, wts, lines, row_w, tables, part, group,
    load_sem, mask_sem, cov_send, cov_recv, halo_send, halo_recv, wts_send, wts_recv, part_send, part_recv, group_send, group_recv,
):
    n_pos, n_off = sizes
    rows, cols = counts_ref.shape
    width = cols + LANE
    blocks = cols // LANE
    ratio = cols // rows
    near_offs = cov.shape[0]
    far_offs = n_off // near_offs
    inner = part.shape[0]
    outer = group.shape[0]
    pos = lax.axis_index("pos")
    off = lax.axis_index("off")
    total_bins = rows * n_pos
    band = cols * n_off
    row_halves = rows // LANE
    third = strips_in.shape[1]

    def at_pos(k):
        return lax.rem(pos + (k + n_pos), n_pos)

    def at_off(k):
        return lax.rem(off + (k + n_off), n_off)

    first = ratio * off
    far = off // near_offs
    near = off - far * near_offs
    quot = pos // inner
    rank = pos - quot * inner
    cov_peers = [(pos, far * near_offs + lax.rem(near + r, near_offs)) for r in range(1, near_offs)]
    halo_moves = [(0, -1), (0, 1), (-1, 0), (1, 0), (-1, -1), (-1, 1), (1, -1), (1, 1)]
    steps = list(range(-1, ratio + 2))
    n_steps = len(steps)
    self_step = steps.index(0)
    n_slots = n_steps + 3
    part_peers = [(quot * inner + lax.rem(rank + r, inner), off) for r in range(1, inner)]
    group_peers = [(lax.rem(quot + r, outer) * inner + rank, off) for r in range(1, outer)]

    def wts_target(t, slot):
        there = lax.rem(far + t, far_offs) * near_offs + near
        if slot < n_steps:
            return (lax.rem(pos - ratio * there - steps[slot] + n_pos, n_pos), there)
        return (at_pos((1, -1, 0)[slot - n_steps]), there)

    def wts_source(t, slot):
        there = lax.rem(far - t + far_offs, far_offs) * near_offs + near
        if slot < n_steps:
            return (lax.rem(pos + first + steps[slot] + n_pos, n_pos), there)
        return (at_pos((-1, 1, 0)[slot - n_steps]), there)

    moves = []
    for t in list(range(1, far_offs)) + [0]:
        for slot in range(n_slots):
            if t or slot != n_slots - 1:
                moves.append((t, slot, t == 0 and slot == self_step))

    load = pltpu.make_async_copy(counts_ref, cells.at[pl.ds(TOP, rows), pl.ds(0, cols)], load_sem)
    load.start()
    load_mask = pltpu.make_async_copy(mask_ref, mask, mask_sem)
    load_mask.start()

    barrier = pltpu.get_barrier_semaphore()

    def greet(device):
        pl.semaphore_signal(barrier, inc=1, device_id=device, device_id_type=MESH)

    for device in cov_peers:
        greet(device)
    for t, slot, selfish in moves:
        if selfish:
            pl.when(off > 0)(functools.partial(greet, wts_source(t, slot)))
        else:
            greet(wts_source(t, slot))
    for a, b in halo_moves:
        greet((at_pos(-a), at_off(-b)))
    for device in part_peers + group_peers:
        greet(device)

    @pl.when(off == 0)
    def _():
        strips_in[1] = jnp.zeros(strips_in.shape[1:], jnp.float32)
        for place in (0, TOP + rows):
            cells[place : place + TOP, cols + LANE :] = jnp.zeros((TOP, LANE), jnp.float32)

    @pl.when(off == n_off - 1)
    def _():
        strips_in[0] = jnp.zeros(strips_in.shape[1:], jnp.float32)
        for place in (0, TOP + rows):
            cells[place : place + TOP, cols : cols + LANE] = jnp.zeros((TOP, LANE), jnp.float32)

    load.wait()

    base = pos * rows + off * cols
    acc = None
    for b in range(blocks):
        row_i = lax.broadcasted_iota(jnp.int32, (rows, LANE), 0)
        col_i = lax.broadcasted_iota(jnp.int32, (rows, LANE), 1)
        piece = cells[TOP : TOP + rows, b * LANE : (b + 1) * LANE]
        piece = jnp.where(row_i + col_i < total_bins - base - b * LANE, piece, 0.0)
        acc = piece if acc is None else acc + piece
    for h in range(row_halves):
        turned = acc[h * LANE : (h + 1) * LANE, :].T
        cov[0, h : h + 1, :] = jnp.sum(turned, axis=0, keepdims=True)
    load_mask.wait()

    n_greet = len(cov_peers) + len(moves) - 1 + len(halo_moves) + len(part_peers) + len(group_peers)
    pl.semaphore_wait(barrier, n_greet + jnp.where(off > 0, 1, 0))

    def remote(src, dst, send, recv, device):
        return pltpu.make_async_remote_copy(
            src_ref=src, dst_ref=dst, send_sem=send, recv_sem=recv, device_id=device, device_id_type=MESH
        )

    cov_copies = [
        remote(cov.at[0], cov.at[r], cov_send.at[r], cov_recv.at[r], cov_peers[r - 1]) for r in range(1, near_offs)
    ]
    for copy in cov_copies:
        copy.start()

    spare = LANE // 3
    lane_t = lax.broadcasted_iota(jnp.int32, (third, LANE), 1)
    for side in (0, 1):
        packed = None
        for k in range(3):
            low = TOP + k * third
            high = min(low + third, TOP + rows)
            piece = cells[low:high, 0:LANE] if side == 0 else cells[low:high, cols - LANE : cols]
            if high - low < third:
                piece = jnp.concatenate([piece, jnp.zeros((third - high + low, LANE), jnp.float32)], axis=0)
            if side == 0:
                piece = pltpu.roll(piece, k * spare, 1) if k else piece
                here = (lane_t >= k * spare) & (lane_t < (k + 1) * spare)
            else:
                piece = pltpu.roll(piece, LANE - k * spare, 1) if k else piece
                here = (lane_t < LANE - k * spare) & (lane_t >= LANE - (k + 1) * spare)
            packed = jnp.where(here, piece, 0.0 if packed is None else packed)
        strips_out[side] = packed

    spans = {-1: (pl.ds(0, TOP), pl.ds(TOP + rows, TOP)), 1: (pl.ds(rows - TOP, TOP), pl.ds(0, TOP))}
    strips = {
        -1: (pl.ds(0, LANE), pl.ds(cols, LANE)),
        1: (pl.ds(cols - LANE, LANE), pl.ds(cols + LANE, LANE)),
        0: (pl.ds(0, cols), pl.ds(0, cols)),
    }
    halo_copies = []
    for k, (a, b) in enumerate(halo_moves):
        if a == 0:
            side = 0 if b < 0 else 1
            ends = strips_out.at[side], strips_in.at[side]
        else:
            ends = counts_ref.at[spans[a][0], strips[b][0]], cells.at[spans[a][1], strips[b][1]]
        halo_copies.append(remote(*ends, halo_send.at[k], halo_recv.at[k], (at_pos(a), at_off(b))))

    def sends(b):
        return off > 0 if b < 0 else off < n_off - 1

    def each_halo(copies, act):
        for (a, b), copy in copies:
            if b == 0:
                getattr(copy, act)()
            elif act == "wait_recv":
                pl.when(sends(-b))(copy.wait_recv)
            else:
                pl.when(sends(b))(getattr(copy, act))

    halos = list(zip(halo_moves, halo_copies))
    each_halo(halos[:2], "start")

    for copy in cov_copies:
        copy.wait_recv()
    coverage = cov[0]
    for r in range(1, near_offs):
        coverage = coverage + cov[r]
    own[0:row_halves, :] = coverage
    own[row_halves:, :] = mask[...].astype(jnp.float32)

    wts_copies = [
        remote(own, wts.at[t, slot], wts_send.at[t, slot], wts_recv.at[t, slot], wts_target(t, slot))
        for t, slot, _ in moves
    ]

    def each_wts(act):
        for (_, _, selfish), copy in zip(moves, wts_copies):
            if selfish:
                pl.when(off > 0)(getattr(copy, act))
            else:
                getattr(copy, act)()

    each_wts("start")
    wts[0, n_slots - 1] = own[...]

    @pl.when(off == 0)
    def _():
        wts[0, self_step] = own[...]

    each_wts("wait_recv")
    each_halo(halos[2:], "start")

    gathered = wts[0, :, 0:row_halves, :]
    for t in range(1, far_offs):
        gathered = gathered + wts[t, :, 0:row_halves, :]
    lines[...] = wts[0, :, row_halves:, :] / jnp.sqrt(gathered)

    def down(vector):
        return jnp.broadcast_to(vector, (LANE, LANE)).T

    for h in range(row_halves):
        row_w[TOP + h * LANE : TOP + (h + 1) * LANE, :] = down(lines[n_slots - 1, h : h + 1, :])

    pieces = []
    for k, d in enumerate(steps):
        block = pos + first + d
        inside = (block >= 0) & (block < n_pos)
        for h in range(row_halves):
            pieces.append(jnp.where(inside, lines[k, h : h + 1, :], 0.0))
    line = jnp.concatenate(pieces, axis=1)
    reach = line.shape[1]
    line = jnp.broadcast_to(line, (8, reach))
    line = pltpu.roll(line, reach - 7, 1, stride=1, stride_axis=0)
    flip = 7 - lax.broadcasted_iota(jnp.int32, (8, reach), 0)
    line = jnp.take_along_axis(line, flip, axis=0)
    phases = LANE // 8
    for h in range(phases):
        tables[h] = line if h == 0 else pltpu.roll(line, reach - 8 * h, 1)

    lane_8 = lax.broadcasted_iota(jnp.int32, (8, LANE), 1)
    low_lanes = lane_8 < SIDE

    def row_group(g):
        rows_g = slice(8 * g, 8 * g + 8)
        place = 8 * g + rows - TOP
        h, shift = (place % LANE) // 8, place // LANE * LANE
        weight = row_w[rows_g, :]
        outs = []
        for b in range(blocks + 1):
            if b < blocks:
                count = cells[rows_g, b * LANE : (b + 1) * LANE]
                col = tables[h, :, shift + b * LANE : shift + (b + 1) * LANE]
            else:
                own_row = 8 * g - TOP
                if 0 <= own_row < rows:
                    k, at = own_row // third, own_row % third
                    after, before = strips_in[0, at : at + 8, :], strips_in[1, at : at + 8, :]
                    if k:
                        after = pltpu.roll(after, LANE - k * spare, 1)
                        before = pltpu.roll(before, k * spare, 1)
                else:
                    after, before = cells[rows_g, cols : cols + LANE], cells[rows_g, cols + LANE : cols + 2 * LANE]
                count = jnp.where(low_lanes, after, before)
                col = jnp.where(
                    low_lanes,
                    tables[h, :, shift + cols : shift + cols + LANE],
                    tables[h, :, shift - LANE : shift],
                )
            value = count * weight * col
            normed_ref[rows_g, b * LANE : (b + 1) * LANE] = value
            outs.append((value, jnp.where((weight > 0) & (col > 0), 1.0, 0.0)))
        return outs

    each_halo(halos[:2], "wait_recv")
    sums = [None] * (2 * (blocks + 1))
    for g in range(TOP // 8, (TOP + rows) // 8):
        for b, (value, live) in enumerate(row_group(g)):
            for k, term in ((b, value), (blocks + 1 + b, live)):
                sums[k] = term if sums[k] is None else sums[k] + term
    for k, total in enumerate(sums):
        part[0, k : k + 1, :] = jnp.sum(total, axis=0, keepdims=True)

    part_copies = [
        remote(part.at[0], part.at[r], part_send.at[r], part_recv.at[r], part_peers[r - 1]) for r in range(1, inner)
    ]
    for copy in part_copies:
        copy.start()

    for copy in part_copies:
        copy.wait_recv()
    total = part[0]
    for r in range(1, inner):
        total = total + part[r]
    group[0] = total
    group_copies = [
        remote(group.at[0], group.at[r], group_send.at[r], group_recv.at[r], group_peers[r - 1])
        for r in range(1, outer)
    ]
    for copy in group_copies:
        copy.start()
    each_halo(halos[2:], "wait_recv")
    for side, h, low, place in ((0, row_halves - 1, LANE - TOP, 0), (1, 0, 0, TOP + rows)):
        block = pos + (1 if side else -1)
        inside = (block >= 0) & (block < n_pos)
        weight = jnp.where(inside, lines[n_steps + side, h : h + 1, :], 0.0)
        row_w[place : place + TOP, :] = down(weight)[low : low + TOP, :]
    for g in list(range(TOP // 8)) + list(range((TOP + rows) // 8, (2 * TOP + rows) // 8)):
        row_group(g)

    for copy in cov_copies + part_copies:
        copy.wait_send()
    each_halo(halos, "wait_send")
    each_wts("wait_send")
    for copy in group_copies:
        copy.wait_recv()
    total = group[0]
    for r in range(1, outer):
        total = total + group[r]
    expected = total[: blocks + 1, :]
    pairs = total[blocks + 1 :, :]
    lane = lax.broadcasted_iota(jnp.int32, expected.shape, 1)
    place = lax.broadcasted_iota(jnp.int32, expected.shape, 0) * LANE + lane
    needed = (place < cols + 2 * W) | (place >= width - 2 * W)
    place = off * cols + jnp.where(place < cols + SIDE, place, place - width)
    factor = pairs / jnp.where(expected > 0, expected, 1.0)
    factor_ref[...] = jnp.where(needed & (place >= 0) & (place < band), factor, 0.0)
    for copy in group_copies:
        copy.wait_send()


def near(distance, lowest, highest):
    return (distance >= lowest) & (distance <= highest)


def both(mask_a, mask_b):
    return jnp.where(mask_a | mask_b, 1.0, 0.0).astype(jnp.bfloat16)


def halves(values):
    high = values.astype(jnp.bfloat16)
    return high, (values - high.astype(jnp.float32)).astype(jnp.bfloat16)


def window_kernel(normed_ref, factor_ref, donut_ref, lower_ref, down_table, side_table):
    step = pl.program_id(0)
    width = normed_ref.shape[1]
    cols = donut_ref.shape[1]
    blocks = width // LANE

    @pl.when(step == 0)
    def _():
        out_row = lax.broadcasted_iota(jnp.int32, (STEP, 2 * SPAN), 0)
        out_row = (out_row // 8) * 8 + 7 - lax.rem(out_row, 8)
        in_row = lax.broadcasted_iota(jnp.int32, (STEP, 2 * SPAN), 1)
        in_row = jnp.where(in_row < SPAN, in_row, in_row - SPAN)
        a = in_row - TOP - out_row
        down_table[0:STEP, :] = both(near(a, P_SIZE + 1, W), near(a, -W, -P_SIZE - 1))
        down_table[STEP : 2 * STEP, :] = both(near(a, 1, P_SIZE), near(a, -P_SIZE, -1))
        down_table[2 * STEP : 3 * STEP, :] = both(near(a, P_SIZE + 1, W), near(a, P_SIZE + 1, W))
        down_table[3 * STEP :, :] = both(near(a, 1, P_SIZE), near(a, 1, P_SIZE))
        shape = (2 * LANE, LANE)
        b = lax.broadcasted_iota(jnp.int32, shape, 0) - SIDE - lax.broadcasted_iota(jnp.int32, shape, 1)
        side_table[0] = both(near(b, 1, W), near(b, -W, -1))
        side_table[1] = both(near(b, P_SIZE + 1, W), near(b, -W, -P_SIZE - 1))
        side_table[2] = both(near(b, -W, -1), near(b, -W, -1))
        side_table[3] = both(near(b, -W, -P_SIZE - 1), near(b, -W, -P_SIZE - 1))

    start = pl.multiple_of(step * STEP, STEP)
    factor = jnp.concatenate([factor_ref[b : b + 1, :] for b in range(blocks)], axis=1)
    ratios = normed_ref[pl.ds(start, SPAN), :] * factor
    level = pltpu.roll(ratios, SIDE, 1, stride=1, stride_axis=0)
    stacked = jnp.concatenate(halves(level), axis=0)
    summed = jnp.dot(down_table[...], stacked, preferred_element_type=jnp.float32)

    def sideways(k):
        parts = []
        for half in halves(summed[k * STEP : (k + 1) * STEP, :]):
            around = jnp.concatenate([half, half[:, :LANE]], axis=1)
            parts.append(jnp.concatenate([around[:, b * LANE : (b + 2) * LANE] for b in range(blocks)], axis=0))
        table = side_table[k]
        result = jnp.dot(parts[0], table, preferred_element_type=jnp.float32)
        return result + jnp.dot(parts[1], table, preferred_element_type=jnp.float32)

    flip = 7 - lax.broadcasted_iota(jnp.int32, (8, cols), 0)
    here = ratios[TOP : TOP + STEP, :cols]
    cells_donut = (2 * W + 1) ** 2 - (2 * P_SIZE + 1) ** 2 - 4 * (W - P_SIZE)
    cells_lower = W * W - P_SIZE * P_SIZE
    for out_ref, k, cell_count in ((donut_ref, 0, cells_donut), (lower_ref, 2, cells_lower)):
        tall = sideways(k) + sideways(k + 1)
        flat = jnp.concatenate([tall[b * STEP : (b + 1) * STEP, :] for b in range(blocks)], axis=1)
        for g in range(STEP // 8):
            rows_g = slice(8 * g, 8 * g + 8)
            back = pltpu.roll(flat[rows_g, :], width - TOP - 8 * g - 7, 1, stride=1, stride_axis=0)[:, :cols]
            back = jnp.take_along_axis(back, flip, axis=0)
            out_ref[rows_g, :] = here[rows_g, :] / jnp.maximum(back / cell_count, 0.25)


def local(counts, bin_mask):
    rows, cols = counts.shape
    n_pos = lax.axis_size("pos")
    n_off = lax.axis_size("off")
    inner = 8
    outer = n_pos // inner
    near_offs = 4
    far_offs = n_off // near_offs
    width = cols + LANE
    vecs = 2 * (cols // LANE + 1)
    n_slots = cols // rows + 6
    reach = (cols // rows + 3) * rows
    halves_n = rows // LANE
    third = -(-rows // 24) * 8
    dma = pltpu.SemaphoreType.DMA
    f32 = jnp.float32
    normed, factor = pl.pallas_call(
        functools.partial(comm_kernel, (n_pos, n_off)),
        out_shape=(
            pltpu.VMEM((rows + 2 * TOP, width), f32),
            pltpu.VMEM((vecs // 2, LANE), f32),
        ),
        in_specs=[pl.BlockSpec(memory_space=pltpu.HBM), pl.BlockSpec(memory_space=pltpu.HBM)],
        out_specs=(pl.BlockSpec(memory_space=pltpu.VMEM), pl.BlockSpec(memory_space=pltpu.VMEM)),
        scratch_shapes=[
            pltpu.VMEM((rows + 2 * TOP, cols + 2 * LANE), f32),
            pltpu.VMEM((2, third, LANE), f32),
            pltpu.VMEM((2, third, LANE), f32),
            pltpu.VMEM((halves_n, LANE), jnp.int32),
            pltpu.VMEM((near_offs, halves_n, LANE), f32),
            pltpu.VMEM((2 * halves_n, LANE), f32),
            pltpu.VMEM((far_offs, n_slots, 2 * halves_n, LANE), f32),
            pltpu.VMEM((n_slots, halves_n, LANE), f32),
            pltpu.VMEM((rows + 2 * TOP, LANE), f32),
            pltpu.VMEM((LANE // 8, 8, reach), f32),
            pltpu.VMEM((inner, vecs, LANE), f32),
            pltpu.VMEM((outer, vecs, LANE), f32),
            dma,
            dma,
            dma((near_offs,)),
            dma((near_offs,)),
            dma((8,)),
            dma((8,)),
            dma((far_offs, n_slots)),
            dma((far_offs, n_slots)),
            dma((inner,)),
            dma((inner,)),
            dma((outer,)),
            dma((outer,)),
        ],
        compiler_params=pltpu.CompilerParams(
            collective_id=0, has_side_effects=True, vmem_limit_bytes=24 * 1024 * 1024
        ),
        name="comm",
    )(
        pltpu.with_memory_space_constraint(counts, pltpu.HBM),
        pltpu.with_memory_space_constraint(bin_mask.reshape(halves_n, LANE), pltpu.HBM),
    )
    out = jax.ShapeDtypeStruct((rows, cols), jnp.float32)
    return pl.pallas_call(
        window_kernel,
        grid=(rows // STEP,),
        out_shape=(out, out),
        in_specs=[pl.BlockSpec(memory_space=pltpu.VMEM), pl.BlockSpec(memory_space=pltpu.VMEM)],
        out_specs=(pl.BlockSpec((STEP, cols), lambda i: (i, 0)), pl.BlockSpec((STEP, cols), lambda i: (i, 0))),
        scratch_shapes=[
            pltpu.VMEM((4 * STEP, 2 * SPAN), jnp.bfloat16),
            pltpu.VMEM((4, 2 * LANE, LANE), jnp.bfloat16),
        ],
        compiler_params=pltpu.CompilerParams(vmem_limit_bytes=24 * 1024 * 1024),
        name="windows",
    )(normed, factor)


def solution(mesh):
    placed = (P("pos", "off"), P("pos"))
    return jax.shard_map(
        local,
        mesh=mesh,
        in_specs=placed,
        out_specs=(P("pos", "off"), P("pos", "off")),
        check_vma=False,
    )
```

```python
import functools

import jax
import jax.numpy as jnp
from jax import lax
from jax.experimental import pallas as pl
from jax.experimental.pallas import tpu as pltpu
from jax.sharding import PartitionSpec as P

W = 20
P_SIZE = 8
TOP = 24
LANE = 128
SIDE = 64
STEP = 64
SPAN = STEP + 2 * TOP
MESH = pl.DeviceIdType.MESH


def comm_kernel(
    sizes, counts_ref, mask_ref, normed_ref, factor_ref,
    cells, strips_out, strips_in, mask, cov, own, wts, lines, row_w, tables, part, group,
    load_sem, mask_sem, cov_send, cov_recv, halo_send, halo_recv, wts_send, wts_recv, part_send, part_recv, group_send, group_recv,
):
    n_pos, n_off = sizes
    rows, cols = counts_ref.shape
    width = cols + LANE
    blocks = cols // LANE
    ratio = cols // rows
    near_offs = cov.shape[0]
    far_offs = n_off // near_offs
    inner = part.shape[0]
    outer = group.shape[0]
    pos = lax.axis_index("pos")
    off = lax.axis_index("off")
    total_bins = rows * n_pos
    band = cols * n_off
    row_halves = rows // LANE
    third = strips_in.shape[1]

    def at_pos(k):
        return lax.rem(pos + (k + n_pos), n_pos)

    def at_off(k):
        return lax.rem(off + (k + n_off), n_off)

    first = ratio * off
    far = off // near_offs
    near = off - far * near_offs
    quot = pos // inner
    rank = pos - quot * inner
    cov_peers = [(pos, far * near_offs + lax.rem(near + r, near_offs)) for r in range(1, near_offs)]
    halo_moves = [(0, -1), (0, 1), (-1, 0), (1, 0), (-1, -1), (-1, 1), (1, -1), (1, 1)]
    steps = list(range(-1, ratio + 2))
    n_steps = len(steps)
    self_step = steps.index(0)
    n_slots = n_steps + 3
    part_peers = [(quot * inner + lax.rem(rank + r, inner), off) for r in range(1, inner)]
    group_peers = [(lax.rem(quot + r, outer) * inner + rank, off) for r in range(1, outer)]

    def wts_target(t, slot):
        there = lax.rem(far + t, far_offs) * near_offs + near
        if slot < n_steps:
            return (lax.rem(pos - ratio * there - steps[slot] + n_pos, n_pos), there)
        return (at_pos((1, -1, 0)[slot - n_steps]), there)

    def wts_source(t, slot):
        there = lax.rem(far - t + far_offs, far_offs) * near_offs + near
        if slot < n_steps:
            return (lax.rem(pos + first + steps[slot] + n_pos, n_pos), there)
        return (at_pos((-1, 1, 0)[slot - n_steps]), there)

    moves = []
    for t in list(range(1, far_offs)) + [0]:
        for slot in range(n_slots):
            if t or slot != n_slots - 1:
                moves.append((t, slot, t == 0 and slot == self_step))

    load = pltpu.make_async_copy(counts_ref, cells.at[pl.ds(TOP, rows), pl.ds(0, cols)], load_sem)
    load.start()
    load_mask = pltpu.make_async_copy(mask_ref, mask, mask_sem)
    load_mask.start()

    barrier = pltpu.get_barrier_semaphore()

    def greet(device):
        pl.semaphore_signal(barrier, inc=1, device_id=device, device_id_type=MESH)

    for device in cov_peers:
        greet(device)
    for t, slot, selfish in moves:
        if selfish:
            pl.when(off > 0)(functools.partial(greet, wts_source(t, slot)))
        else:
            greet(wts_source(t, slot))
    for a, b in halo_moves:
        greet((at_pos(-a), at_off(-b)))
    for device in part_peers + group_peers:
        greet(device)

    @pl.when(off == 0)
    def _():
        strips_in[1] = jnp.zeros(strips_in.shape[1:], jnp.float32)
        for place in (0, TOP + rows):
            cells[place : place + TOP, cols + LANE :] = jnp.zeros((TOP, LANE), jnp.float32)

    @pl.when(off == n_off - 1)
    def _():
        strips_in[0] = jnp.zeros(strips_in.shape[1:], jnp.float32)
        for place in (0, TOP + rows):
            cells[place : place + TOP, cols : cols + LANE] = jnp.zeros((TOP, LANE), jnp.float32)

    load.wait()

    base = pos * rows + off * cols
    acc = None
    for b in range(blocks):
        row_i = lax.broadcasted_iota(jnp.int32, (rows, LANE), 0)
        col_i = lax.broadcasted_iota(jnp.int32, (rows, LANE), 1)
        piece = cells[TOP : TOP + rows, b * LANE : (b + 1) * LANE]
        piece = jnp.where(row_i + col_i < total_bins - base - b * LANE, piece, 0.0)
        acc = piece if acc is None else acc + piece
    for h in range(row_halves):
        turned = acc[h * LANE : (h + 1) * LANE, :].T
        cov[0, h : h + 1, :] = jnp.sum(turned, axis=0, keepdims=True)
    load_mask.wait()

    n_greet = len(cov_peers) + len(moves) - 1 + len(halo_moves) + len(part_peers) + len(group_peers)
    pl.semaphore_wait(barrier, n_greet + jnp.where(off > 0, 1, 0))

    def remote(src, dst, send, recv, device):
        return pltpu.make_async_remote_copy(
            src_ref=src, dst_ref=dst, send_sem=send, recv_sem=recv, device_id=device, device_id_type=MESH
        )

    cov_copies = [
        remote(cov.at[0], cov.at[r], cov_send.at[r], cov_recv.at[r], cov_peers[r - 1]) for r in range(1, near_offs)
    ]
    for copy in cov_copies:
        copy.start()

    spans = {-1: (pl.ds(0, TOP), pl.ds(TOP + rows, TOP)), 1: (pl.ds(rows - TOP, TOP), pl.ds(0, TOP))}
    strips = {
        -1: (pl.ds(0, LANE), pl.ds(cols, LANE)),
        1: (pl.ds(cols - LANE, LANE), pl.ds(cols + LANE, LANE)),
        0: (pl.ds(0, cols), pl.ds(0, cols)),
    }
    halo_copies = []
    for k, (a, b) in enumerate(halo_moves):
        if a == 0:
            side = 0 if b < 0 else 1
            ends = strips_out.at[side], strips_in.at[side]
        else:
            ends = counts_ref.at[spans[a][0], strips[b][0]], cells.at[spans[a][1], strips[b][1]]
        halo_copies.append(remote(*ends, halo_send.at[k], halo_recv.at[k], (at_pos(a), at_off(b))))

    def sends(b):
        return off > 0 if b < 0 else off < n_off - 1

    def each_halo(copies, act):
        for (a, b), copy in copies:
            if b == 0:
                getattr(copy, act)()
            elif act == "wait_recv":
                pl.when(sends(-b))(copy.wait_recv)
            else:
                pl.when(sends(b))(getattr(copy, act))

    halos = list(zip(halo_moves, halo_copies))
    each_halo(halos[2:], "start")

    spare = LANE // 3
    lane_t = lax.broadcasted_iota(jnp.int32, (third, LANE), 1)
    for side in (0, 1):
        packed = None
        for k in range(3):
            low = TOP + k * third
            high = min(low + third, TOP + rows)
            piece = cells[low:high, 0:LANE] if side == 0 else cells[low:high, cols - LANE : cols]
            if high - low < third:
                piece = jnp.concatenate([piece, jnp.zeros((third - high + low, LANE), jnp.float32)], axis=0)
            if side == 0:
                piece = pltpu.roll(piece, k * spare, 1) if k else piece
                here = (lane_t >= k * spare) & (lane_t < (k + 1) * spare)
            else:
                piece = pltpu.roll(piece, LANE - k * spare, 1) if k else piece
                here = (lane_t < LANE - k * spare) & (lane_t >= LANE - (k + 1) * spare)
            packed = jnp.where(here, piece, 0.0 if packed is None else packed)
        strips_out[side] = packed

    each_halo(halos[:2], "start")

    for copy in cov_copies:
        copy.wait_recv()
    coverage = cov[0]
    for r in range(1, near_offs):
        coverage = coverage + cov[r]
    own[0:row_halves, :] = coverage
    own[row_halves:, :] = mask[...].astype(jnp.float32)

    wts_copies = [
        remote(own, wts.at[t, slot], wts_send.at[t, slot], wts_recv.at[t, slot], wts_target(t, slot))
        for t, slot, _ in moves
    ]

    def each_wts(act):
        for (_, _, selfish), copy in zip(moves, wts_copies):
            if selfish:
                pl.when(off > 0)(getattr(copy, act))
            else:
                getattr(copy, act)()

    each_wts("start")
    wts[0, n_slots - 1] = own[...]

    @pl.when(off == 0)
    def _():
        wts[0, self_step] = own[...]

    each_wts("wait_recv")

    gathered = wts[0, :, 0:row_halves, :]
    for t in range(1, far_offs):
        gathered = gathered + wts[t, :, 0:row_halves, :]
    lines[...] = wts[0, :, row_halves:, :] / jnp.sqrt(gathered)

    def down(vector):
        return jnp.broadcast_to(vector, (LANE, LANE)).T

    for h in range(row_halves):
        row_w[TOP + h * LANE : TOP + (h + 1) * LANE, :] = down(lines[n_slots - 1, h : h + 1, :])

    pieces = []
    for k, d in enumerate(steps):
        block = pos + first + d
        inside = (block >= 0) & (block < n_pos)
        for h in range(row_halves):
            pieces.append(jnp.where(inside, lines[k, h : h + 1, :], 0.0))
    line = jnp.concatenate(pieces, axis=1)
    reach = line.shape[1]
    line = jnp.broadcast_to(line, (8, reach))
    line = pltpu.roll(line, reach - 7, 1, stride=1, stride_axis=0)
    flip = 7 - lax.broadcasted_iota(jnp.int32, (8, reach), 0)
    line = jnp.take_along_axis(line, flip, axis=0)
    phases = LANE // 8
    for h in range(phases):
        tables[h] = line if h == 0 else pltpu.roll(line, reach - 8 * h, 1)

    lane_8 = lax.broadcasted_iota(jnp.int32, (8, LANE), 1)
    low_lanes = lane_8 < SIDE

    def row_group(g):
        rows_g = slice(8 * g, 8 * g + 8)
        place = 8 * g + rows - TOP
        h, shift = (place % LANE) // 8, place // LANE * LANE
        weight = row_w[rows_g, :]
        outs = []
        for b in range(blocks + 1):
            if b < blocks:
                count = cells[rows_g, b * LANE : (b + 1) * LANE]
                col = tables[h, :, shift + b * LANE : shift + (b + 1) * LANE]
            else:
                own_row = 8 * g - TOP
                if 0 <= own_row < rows:
                    k, at = own_row // third, own_row % third
                    after, before = strips_in[0, at : at + 8, :], strips_in[1, at : at + 8, :]
                    if k:
                        after = pltpu.roll(after, LANE - k * spare, 1)
                        before = pltpu.roll(before, k * spare, 1)
                else:
                    after, before = cells[rows_g, cols : cols + LANE], cells[rows_g, cols + LANE : cols + 2 * LANE]
                count = jnp.where(low_lanes, after, before)
                col = jnp.where(
                    low_lanes,
                    tables[h, :, shift + cols : shift + cols + LANE],
                    tables[h, :, shift - LANE : shift],
                )
            value = count * weight * col
            normed_ref[rows_g, b * LANE : (b + 1) * LANE] = value
            outs.append((value, jnp.where((weight > 0) & (col > 0), 1.0, 0.0)))
        return outs

    each_halo(halos[:2], "wait_recv")
    sums = [None] * (2 * (blocks + 1))
    for g in range(TOP // 8, (TOP + rows) // 8):
        for b, (value, live) in enumerate(row_group(g)):
            for k, term in ((b, value), (blocks + 1 + b, live)):
                sums[k] = term if sums[k] is None else sums[k] + term
    for k, total in enumerate(sums):
        part[0, k : k + 1, :] = jnp.sum(total, axis=0, keepdims=True)

    part_copies = [
        remote(part.at[0], part.at[r], part_send.at[r], part_recv.at[r], part_peers[r - 1]) for r in range(1, inner)
    ]
    for copy in part_copies:
        copy.start()

    each_halo(halos[2:], "wait_recv")
    for side, h, low, place in ((0, row_halves - 1, LANE - TOP, 0), (1, 0, 0, TOP + rows)):
        block = pos + (1 if side else -1)
        inside = (block >= 0) & (block < n_pos)
        weight = jnp.where(inside, lines[n_steps + side, h : h + 1, :], 0.0)
        row_w[place : place + TOP, :] = down(weight)[low : low + TOP, :]
    for g in list(range(TOP // 8)) + list(range((TOP + rows) // 8, (2 * TOP + rows) // 8)):
        row_group(g)

    for copy in part_copies:
        copy.wait_recv()
    total = part[0]
    for r in range(1, inner):
        total = total + part[r]
    group[0] = total
    group_copies = [
        remote(group.at[0], group.at[r], group_send.at[r], group_recv.at[r], group_peers[r - 1])
        for r in range(1, outer)
    ]
    for copy in group_copies:
        copy.start()
    for copy in cov_copies + part_copies:
        copy.wait_send()
    each_halo(halos, "wait_send")
    each_wts("wait_send")
    for copy in group_copies:
        copy.wait_recv()
    total = group[0]
    for r in range(1, outer):
        total = total + group[r]
    expected = total[: blocks + 1, :]
    pairs = total[blocks + 1 :, :]
    lane = lax.broadcasted_iota(jnp.int32, expected.shape, 1)
    place = lax.broadcasted_iota(jnp.int32, expected.shape, 0) * LANE + lane
    needed = (place < cols + 2 * W) | (place >= width - 2 * W)
    place = off * cols + jnp.where(place < cols + SIDE, place, place - width)
    factor = pairs / jnp.where(expected > 0, expected, 1.0)
    factor_ref[...] = jnp.where(needed & (place >= 0) & (place < band), factor, 0.0)
    for copy in group_copies:
        copy.wait_send()


def near(distance, lowest, highest):
    return (distance >= lowest) & (distance <= highest)


def both(mask_a, mask_b):
    return jnp.where(mask_a | mask_b, 1.0, 0.0).astype(jnp.bfloat16)


def halves(values):
    high = values.astype(jnp.bfloat16)
    return high, (values - high.astype(jnp.float32)).astype(jnp.bfloat16)


def window_kernel(normed_ref, factor_ref, donut_ref, lower_ref, donut, lower, sems):
    width = normed_ref.shape[1]
    rows, cols = donut_ref.shape
    blocks = width // LANE

    out_row = lax.broadcasted_iota(jnp.int32, (STEP, 2 * SPAN), 0)
    out_row = (out_row // 8) * 8 + 7 - lax.rem(out_row, 8)
    in_row = lax.broadcasted_iota(jnp.int32, (STEP, 2 * SPAN), 1)
    in_row = jnp.where(in_row < SPAN, in_row, in_row - SPAN)
    a = in_row - TOP - out_row
    down_table = jnp.concatenate(
        [
            both(near(a, P_SIZE + 1, W), near(a, -W, -P_SIZE - 1)),
            both(near(a, 1, P_SIZE), near(a, -P_SIZE, -1)),
            both(near(a, P_SIZE + 1, W), near(a, P_SIZE + 1, W)),
            both(near(a, 1, P_SIZE), near(a, 1, P_SIZE)),
        ],
        axis=0,
    )
    shape = (2 * LANE, LANE)
    b = lax.broadcasted_iota(jnp.int32, shape, 0) - SIDE - lax.broadcasted_iota(jnp.int32, shape, 1)
    side_table = [
        both(near(b, 1, W), near(b, -W, -1)),
        both(near(b, P_SIZE + 1, W), near(b, -W, -P_SIZE - 1)),
        both(near(b, -W, -1), near(b, -W, -1)),
        both(near(b, -W, -P_SIZE - 1), near(b, -W, -P_SIZE - 1)),
    ]
    flip = 7 - lax.broadcasted_iota(jnp.int32, (8, cols), 0)
    cells_donut = (2 * W + 1) ** 2 - (2 * P_SIZE + 1) ** 2 - 4 * (W - P_SIZE)
    cells_lower = W * W - P_SIZE * P_SIZE
    factor = jnp.concatenate([factor_ref[b : b + 1, :] for b in range(blocks)], axis=1)

    copies = []
    for start in range(0, rows, STEP):
        ratios = normed_ref[start : start + SPAN, :] * factor
        level = pltpu.roll(ratios, SIDE, 1, stride=1, stride_axis=0)
        stacked = jnp.concatenate(halves(level), axis=0)
        summed = jnp.dot(down_table, stacked, preferred_element_type=jnp.float32)

        def sideways(k):
            parts = []
            for half in halves(summed[k * STEP : (k + 1) * STEP, :]):
                around = jnp.concatenate([half, half[:, :LANE]], axis=1)
                parts.append(jnp.concatenate([around[:, b * LANE : (b + 2) * LANE] for b in range(blocks)], axis=0))
            return parts

        here = ratios[TOP : TOP + STEP, :cols]
        for to, out_ref, out, k, cell_count in (
            (0, donut_ref, donut, 0, cells_donut),
            (1, lower_ref, lower, 2, cells_lower),
        ):
            wide = jnp.concatenate(sideways(k) + sideways(k + 1), axis=1)
            table = jnp.concatenate([side_table[k]] * 2 + [side_table[k + 1]] * 2, axis=0)
            tall = jnp.dot(wide, table, preferred_element_type=jnp.float32)
            flat = jnp.concatenate([tall[b * STEP : (b + 1) * STEP, :] for b in range(blocks)], axis=1)
            for g in range(STEP // 8):
                rows_g = slice(8 * g, 8 * g + 8)
                back = pltpu.roll(flat[rows_g, :], width - TOP - 8 * g - 7, 1, stride=1, stride_axis=0)[:, :cols]
                back = jnp.take_along_axis(back, flip, axis=0)
                out[start + 8 * g : start + 8 * g + 8, :] = here[rows_g, :] / jnp.maximum(back / cell_count, 0.25)
            span = pl.ds(start, STEP)
            copies.append(pltpu.make_async_copy(out.at[span, :], out_ref.at[span, :], sems.at[to, start // STEP]))
            copies[-1].start()
    for copy in copies:
        copy.wait()


def windows(normed, factor):
    rows, cols = normed.shape[0] - 2 * TOP, normed.shape[1] - LANE
    out = jax.ShapeDtypeStruct((rows, cols), jnp.float32)
    return pl.pallas_call(
        window_kernel,
        out_shape=(out, out),
        in_specs=[pl.BlockSpec(memory_space=pltpu.VMEM), pl.BlockSpec(memory_space=pltpu.VMEM)],
        out_specs=(pl.BlockSpec(memory_space=pltpu.HBM), pl.BlockSpec(memory_space=pltpu.HBM)),
        scratch_shapes=[
            pltpu.VMEM((rows, cols), jnp.float32),
            pltpu.VMEM((rows, cols), jnp.float32),
            pltpu.SemaphoreType.DMA((2, rows // STEP)),
        ],
        compiler_params=pltpu.CompilerParams(vmem_limit_bytes=32 * 1024 * 1024),
        name="windows",
    )(normed, factor)


def local(counts, bin_mask):
    rows, cols = counts.shape
    n_pos = lax.axis_size("pos")
    n_off = lax.axis_size("off")
    inner = 8
    outer = n_pos // inner
    near_offs = 4
    far_offs = n_off // near_offs
    width = cols + LANE
    vecs = 2 * (cols // LANE + 1)
    n_slots = cols // rows + 6
    reach = (cols // rows + 3) * rows
    halves_n = rows // LANE
    third = -(-rows // 24) * 8
    dma = pltpu.SemaphoreType.DMA
    f32 = jnp.float32
    normed, factor = pl.pallas_call(
        functools.partial(comm_kernel, (n_pos, n_off)),
        out_shape=(
            pltpu.VMEM((rows + 2 * TOP, width), f32),
            pltpu.VMEM((vecs // 2, LANE), f32),
        ),
        in_specs=[pl.BlockSpec(memory_space=pltpu.HBM), pl.BlockSpec(memory_space=pltpu.HBM)],
        out_specs=(pl.BlockSpec(memory_space=pltpu.VMEM), pl.BlockSpec(memory_space=pltpu.VMEM)),
        scratch_shapes=[
            pltpu.VMEM((rows + 2 * TOP, cols + 2 * LANE), f32),
            pltpu.VMEM((2, third, LANE), f32),
            pltpu.VMEM((2, third, LANE), f32),
            pltpu.VMEM((halves_n, LANE), jnp.int32),
            pltpu.VMEM((near_offs, halves_n, LANE), f32),
            pltpu.VMEM((2 * halves_n, LANE), f32),
            pltpu.VMEM((far_offs, n_slots, 2 * halves_n, LANE), f32),
            pltpu.VMEM((n_slots, halves_n, LANE), f32),
            pltpu.VMEM((rows + 2 * TOP, LANE), f32),
            pltpu.VMEM((LANE // 8, 8, reach), f32),
            pltpu.VMEM((inner, vecs, LANE), f32),
            pltpu.VMEM((outer, vecs, LANE), f32),
            dma,
            dma,
            dma((near_offs,)),
            dma((near_offs,)),
            dma((8,)),
            dma((8,)),
            dma((far_offs, n_slots)),
            dma((far_offs, n_slots)),
            dma((inner,)),
            dma((inner,)),
            dma((outer,)),
            dma((outer,)),
        ],
        compiler_params=pltpu.CompilerParams(
            collective_id=0, has_side_effects=True, vmem_limit_bytes=24 * 1024 * 1024
        ),
        name="comm",
    )(
        pltpu.with_memory_space_constraint(counts, pltpu.HBM),
        pltpu.with_memory_space_constraint(bin_mask.reshape(halves_n, LANE), pltpu.HBM),
    )
    return windows(normed, factor)


def solution(mesh):
    placed = (P("pos", "off"), P("pos"))
    return jax.shard_map(
        local,
        mesh=mesh,
        in_specs=placed,
        out_specs=(P("pos", "off"), P("pos", "off")),
        check_vma=False,
    )
```

```python
import functools

import jax
import jax.numpy as jnp
from jax import lax
from jax.experimental import pallas as pl
from jax.experimental.pallas import tpu as pltpu
from jax.sharding import PartitionSpec as P

W = 20
P_SIZE = 8
TOP = 24
LANE = 128
SIDE = 64
STEP = 64
SPAN = STEP + 2 * TOP
MESH = pl.DeviceIdType.MESH


def comm_kernel(
    sizes, counts_ref, mask_ref, normed_ref, factor_ref,
    cells, strips_out, strips_in, mask, own_live, live, cov, own, wts, lines, row_w, tables, part, group, part_live, group_live,
    load_sem, mask_sem, cov_send, cov_recv, halo_send, halo_recv, live_send, live_recv, wts_send, wts_recv,
    part_send, part_recv, group_send, group_recv, part_live_send, part_live_recv, group_live_send, group_live_recv,
):
    n_pos, n_off = sizes
    rows, cols = counts_ref.shape
    width = cols + LANE
    blocks = cols // LANE
    ratio = cols // rows
    near_offs = cov.shape[0]
    far_offs = n_off // near_offs
    inner = part.shape[0]
    outer = group.shape[0]
    pos = lax.axis_index("pos")
    off = lax.axis_index("off")
    total_bins = rows * n_pos
    band = cols * n_off
    row_halves = rows // LANE
    third = strips_in.shape[1]

    def at_pos(k):
        return lax.rem(pos + (k + n_pos), n_pos)

    def at_off(k):
        return lax.rem(off + (k + n_off), n_off)

    first = ratio * off
    far = off // near_offs
    near = off - far * near_offs
    quot = pos // inner
    rank = pos - quot * inner
    cov_peers = [(pos, far * near_offs + lax.rem(near + r, near_offs)) for r in range(1, near_offs)]
    halo_moves = [(0, -1), (0, 1), (-1, 0), (1, 0), (-1, -1), (-1, 1), (1, -1), (1, 1)]
    steps = list(range(-1, ratio + 2))
    n_steps = len(steps)
    self_step = steps.index(0)
    n_slots = n_steps + 3
    part_peers = [(quot * inner + lax.rem(rank + r, inner), off) for r in range(1, inner)]
    group_peers = [(lax.rem(quot + r, outer) * inner + rank, off) for r in range(1, outer)]

    def wts_target(t, slot):
        there = lax.rem(far + t, far_offs) * near_offs + near
        if slot < n_steps:
            return (lax.rem(pos - ratio * there - steps[slot] + n_pos, n_pos), there)
        return (at_pos((1, -1, 0)[slot - n_steps]), there)

    def wts_source(t, slot):
        there = lax.rem(far - t + far_offs, far_offs) * near_offs + near
        if slot < n_steps:
            return (lax.rem(pos + first + steps[slot] + n_pos, n_pos), there)
        return (at_pos((-1, 1, 0)[slot - n_steps]), there)

    moves = []
    for t in list(range(1, far_offs)) + [0]:
        for slot in range(n_slots):
            if t or slot != n_slots - 1:
                moves.append((t, slot, t == 0 and slot == self_step))

    load = pltpu.make_async_copy(counts_ref, cells.at[pl.ds(TOP, rows), pl.ds(0, cols)], load_sem)
    load.start()
    load_mask = pltpu.make_async_copy(mask_ref, mask, mask_sem)
    load_mask.start()

    barrier = pltpu.get_barrier_semaphore()

    def greet(device):
        pl.semaphore_signal(barrier, inc=1, device_id=device, device_id_type=MESH)

    for device in cov_peers:
        greet(device)
    for t, slot, selfish in moves:
        if selfish:
            pl.when(off > 0)(functools.partial(greet, wts_source(t, slot)))
        else:
            greet(wts_source(t, slot))
    for a, b in halo_moves:
        greet((at_pos(-a), at_off(-b)))
    for device in part_peers + group_peers:
        greet(device)

    @pl.when(off == 0)
    def _():
        strips_in[1] = jnp.zeros(strips_in.shape[1:], jnp.float32)
        for place in (0, TOP + rows):
            cells[place : place + TOP, cols + LANE :] = jnp.zeros((TOP, LANE), jnp.float32)

    @pl.when(off == n_off - 1)
    def _():
        strips_in[0] = jnp.zeros(strips_in.shape[1:], jnp.float32)
        for place in (0, TOP + rows):
            cells[place : place + TOP, cols : cols + LANE] = jnp.zeros((TOP, LANE), jnp.float32)

    load.wait()

    base = pos * rows + off * cols
    acc = None
    for b in range(blocks):
        row_i = lax.broadcasted_iota(jnp.int32, (rows, LANE), 0)
        col_i = lax.broadcasted_iota(jnp.int32, (rows, LANE), 1)
        piece = cells[TOP : TOP + rows, b * LANE : (b + 1) * LANE]
        piece = jnp.where(row_i + col_i < total_bins - base - b * LANE, piece, 0.0)
        acc = piece if acc is None else acc + piece
    for h in range(row_halves):
        turned = acc[h * LANE : (h + 1) * LANE, :].T
        cov[0, h : h + 1, :] = jnp.sum(turned, axis=0, keepdims=True)
    load_mask.wait()
    own_live[...] = mask[...].astype(jnp.float32)

    n_greet = len(cov_peers) + len(moves) - 1 + len(halo_moves) + len(part_peers) + len(group_peers)
    pl.semaphore_wait(barrier, n_greet + jnp.where(off > 0, 1, 0))

    def remote(src, dst, send, recv, device):
        return pltpu.make_async_remote_copy(
            src_ref=src, dst_ref=dst, send_sem=send, recv_sem=recv, device_id=device, device_id_type=MESH
        )

    cov_copies = [
        remote(cov.at[0], cov.at[r], cov_send.at[r], cov_recv.at[r], cov_peers[r - 1]) for r in range(1, near_offs)
    ]
    for copy in cov_copies:
        copy.start()

    live_copies = [
        remote(own_live, live.at[k], live_send.at[k], live_recv.at[k], wts_target(0, k)) for k in range(n_steps)
    ]

    def each_live(act):
        for k, copy in enumerate(live_copies):
            if k == self_step:
                pl.when(off > 0)(getattr(copy, act))
            else:
                getattr(copy, act)()

    each_live("start")

    @pl.when(off == 0)
    def _():
        live[self_step] = own_live[...]

    spans = {-1: (pl.ds(0, TOP), pl.ds(TOP + rows, TOP)), 1: (pl.ds(rows - TOP, TOP), pl.ds(0, TOP))}
    strips = {
        -1: (pl.ds(0, LANE), pl.ds(cols, LANE)),
        1: (pl.ds(cols - LANE, LANE), pl.ds(cols + LANE, LANE)),
        0: (pl.ds(0, cols), pl.ds(0, cols)),
    }
    halo_copies = []
    for k, (a, b) in enumerate(halo_moves):
        if a == 0:
            side = 0 if b < 0 else 1
            ends = strips_out.at[side], strips_in.at[side]
        else:
            ends = counts_ref.at[spans[a][0], strips[b][0]], cells.at[spans[a][1], strips[b][1]]
        halo_copies.append(remote(*ends, halo_send.at[k], halo_recv.at[k], (at_pos(a), at_off(b))))

    def sends(b):
        return off > 0 if b < 0 else off < n_off - 1

    def each_halo(copies, act):
        for (a, b), copy in copies:
            if b == 0:
                getattr(copy, act)()
            elif act == "wait_recv":
                pl.when(sends(-b))(copy.wait_recv)
            else:
                pl.when(sends(b))(getattr(copy, act))

    halos = list(zip(halo_moves, halo_copies))
    each_halo(halos[2:], "start")

    spare = LANE // 3
    lane_t = lax.broadcasted_iota(jnp.int32, (third, LANE), 1)
    for side in (0, 1):
        packed = None
        for k in range(3):
            low = TOP + k * third
            high = min(low + third, TOP + rows)
            piece = cells[low:high, 0:LANE] if side == 0 else cells[low:high, cols - LANE : cols]
            if high - low < third:
                piece = jnp.concatenate([piece, jnp.zeros((third - high + low, LANE), jnp.float32)], axis=0)
            if side == 0:
                piece = pltpu.roll(piece, k * spare, 1) if k else piece
                here = (lane_t >= k * spare) & (lane_t < (k + 1) * spare)
            else:
                piece = pltpu.roll(piece, LANE - k * spare, 1) if k else piece
                here = (lane_t < LANE - k * spare) & (lane_t >= LANE - (k + 1) * spare)
            packed = jnp.where(here, piece, 0.0 if packed is None else packed)
        strips_out[side] = packed

    each_halo(halos[:2], "start")

    for copy in cov_copies:
        copy.wait_recv()
    coverage = cov[0]
    for r in range(1, near_offs):
        coverage = coverage + cov[r]
    own[0:row_halves, :] = coverage
    own[row_halves:, :] = own_live[...]

    wts_copies = [
        remote(own, wts.at[t, slot], wts_send.at[t, slot], wts_recv.at[t, slot], wts_target(t, slot))
        for t, slot, _ in moves
    ]

    def each_wts(act):
        for (_, _, selfish), copy in zip(moves, wts_copies):
            if selfish:
                pl.when(off > 0)(getattr(copy, act))
            else:
                getattr(copy, act)()

    each_wts("start")
    wts[0, n_slots - 1] = own[...]

    @pl.when(off == 0)
    def _():
        wts[0, self_step] = own[...]

    def down(vector):
        return jnp.broadcast_to(vector, (LANE, LANE)).T

    phases = LANE // 8

    def spread(source):
        pieces = []
        for k, d in enumerate(steps):
            block = pos + first + d
            inside = (block >= 0) & (block < n_pos)
            for h in range(row_halves):
                pieces.append(jnp.where(inside, source[k, h : h + 1, :], 0.0))
        line = jnp.concatenate(pieces, axis=1)
        reach = line.shape[1]
        line = jnp.broadcast_to(line, (8, reach))
        line = pltpu.roll(line, reach - 7, 1, stride=1, stride_axis=0)
        flip = 7 - lax.broadcasted_iota(jnp.int32, (8, reach), 0)
        line = jnp.take_along_axis(line, flip, axis=0)
        for h in range(phases):
            tables[h] = line if h == 0 else pltpu.roll(line, reach - 8 * h, 1)

    lane_8 = lax.broadcasted_iota(jnp.int32, (8, LANE), 1)
    low_lanes = lane_8 < SIDE

    def column(g, b):
        place = 8 * g + rows - TOP
        h, shift = (place % LANE) // 8, place // LANE * LANE
        if b < blocks:
            return tables[h, :, shift + b * LANE : shift + (b + 1) * LANE]
        after = tables[h, :, shift + cols : shift + cols + LANE]
        return jnp.where(low_lanes, after, tables[h, :, shift - LANE : shift])

    own_groups = range(TOP // 8, (TOP + rows) // 8)

    def column_sums(to, terms_of):
        sums = [None] * (blocks + 1)
        for g in own_groups:
            for b, term in enumerate(terms_of(g)):
                sums[b] = term if sums[b] is None else sums[b] + term
        for b, total in enumerate(sums):
            to[0, b : b + 1, :] = jnp.sum(total, axis=0, keepdims=True)

    def share(buffer, send, recv, peers):
        copies = [
            remote(buffer.at[0], buffer.at[r], send.at[r], recv.at[r], peers[r - 1]) for r in range(1, buffer.shape[0])
        ]
        for copy in copies:
            copy.start()
        return copies

    def gather(copies, buffer):
        for copy in copies:
            copy.wait_recv()
        total = buffer[0]
        for r in range(1, buffer.shape[0]):
            total = total + buffer[r]
        return total

    each_live("wait_recv")
    for h in range(row_halves):
        row_w[TOP + h * LANE : TOP + (h + 1) * LANE, :] = down(own_live[h : h + 1, :])
    spread(live)

    def live_terms(g):
        row = row_w[8 * g : 8 * g + 8, :]
        return [row * column(g, b) for b in range(blocks + 1)]

    column_sums(part_live, live_terms)
    part_live_copies = share(part_live, part_live_send, part_live_recv, part_peers)

    each_wts("wait_recv")
    gathered = wts[0, :, 0:row_halves, :]
    for t in range(1, far_offs):
        gathered = gathered + wts[t, :, 0:row_halves, :]
    lines[...] = wts[0, :, row_halves:, :] / jnp.sqrt(gathered)
    for h in range(row_halves):
        row_w[TOP + h * LANE : TOP + (h + 1) * LANE, :] = down(lines[n_slots - 1, h : h + 1, :])
    spread(lines)

    def row_group(g):
        rows_g = slice(8 * g, 8 * g + 8)
        weight = row_w[rows_g, :]
        outs = []
        for b in range(blocks + 1):
            if b < blocks:
                count = cells[rows_g, b * LANE : (b + 1) * LANE]
            else:
                own_row = 8 * g - TOP
                if 0 <= own_row < rows:
                    k, at = own_row // third, own_row % third
                    after, before = strips_in[0, at : at + 8, :], strips_in[1, at : at + 8, :]
                    if k:
                        after = pltpu.roll(after, LANE - k * spare, 1)
                        before = pltpu.roll(before, k * spare, 1)
                else:
                    after, before = cells[rows_g, cols : cols + LANE], cells[rows_g, cols + LANE : cols + 2 * LANE]
                count = jnp.where(low_lanes, after, before)
            value = count * weight * column(g, b)
            normed_ref[rows_g, b * LANE : (b + 1) * LANE] = value
            outs.append(value)
        return outs

    each_halo(halos[:2], "wait_recv")
    column_sums(part, row_group)
    part_copies = share(part, part_send, part_recv, part_peers)

    each_halo(halos[2:], "wait_recv")
    for side, h, low, place in ((0, row_halves - 1, LANE - TOP, 0), (1, 0, 0, TOP + rows)):
        block = pos + (1 if side else -1)
        inside = (block >= 0) & (block < n_pos)
        weight = jnp.where(inside, lines[n_steps + side, h : h + 1, :], 0.0)
        row_w[place : place + TOP, :] = down(weight)[low : low + TOP, :]
    for g in list(range(TOP // 8)) + list(range((TOP + rows) // 8, (2 * TOP + rows) // 8)):
        row_group(g)

    group_live[0] = gather(part_live_copies, part_live)
    group_live_copies = share(group_live, group_live_send, group_live_recv, group_peers)
    group[0] = gather(part_copies, part)
    group_copies = share(group, group_send, group_recv, group_peers)
    for copy in cov_copies + part_copies + part_live_copies:
        copy.wait_send()
    each_halo(halos, "wait_send")
    each_wts("wait_send")
    each_live("wait_send")
    pairs = gather(group_live_copies, group_live)
    expected = gather(group_copies, group)
    lane = lax.broadcasted_iota(jnp.int32, expected.shape, 1)
    place = lax.broadcasted_iota(jnp.int32, expected.shape, 0) * LANE + lane
    needed = (place < cols + 2 * W) | (place >= width - 2 * W)
    place = off * cols + jnp.where(place < cols + SIDE, place, place - width)
    factor = pairs / jnp.where(expected > 0, expected, 1.0)
    factor_ref[...] = jnp.where(needed & (place >= 0) & (place < band), factor, 0.0)
    for copy in group_copies + group_live_copies:
        copy.wait_send()


def near(distance, lowest, highest):
    return (distance >= lowest) & (distance <= highest)


def both(mask_a, mask_b):
    return jnp.where(mask_a | mask_b, 1.0, 0.0).astype(jnp.bfloat16)


def halves(values):
    high = values.astype(jnp.bfloat16)
    return high, (values - high.astype(jnp.float32)).astype(jnp.bfloat16)


def window_kernel(normed_ref, factor_ref, donut_ref, lower_ref, donut, lower, sems):
    width = normed_ref.shape[1]
    rows, cols = donut_ref.shape
    blocks = width // LANE

    out_row = lax.broadcasted_iota(jnp.int32, (STEP, 2 * SPAN), 0)
    out_row = (out_row // 8) * 8 + 7 - lax.rem(out_row, 8)
    in_row = lax.broadcasted_iota(jnp.int32, (STEP, 2 * SPAN), 1)
    in_row = jnp.where(in_row < SPAN, in_row, in_row - SPAN)
    a = in_row - TOP - out_row
    down_table = jnp.concatenate(
        [
            both(near(a, P_SIZE + 1, W), near(a, -W, -P_SIZE - 1)),
            both(near(a, 1, P_SIZE), near(a, -P_SIZE, -1)),
            both(near(a, P_SIZE + 1, W), near(a, P_SIZE + 1, W)),
            both(near(a, 1, P_SIZE), near(a, 1, P_SIZE)),
        ],
        axis=0,
    )
    def side_tables(depth, wide, split):
        shape = (depth, wide)
        at = lax.broadcasted_iota(jnp.int32, shape, 0)
        if split:
            at = jnp.where(at < SIDE, at + wide, at - LANE)
        b = at - lax.broadcasted_iota(jnp.int32, shape, 1)
        return [
            both(near(b, 1, W), near(b, -W, -1)),
            both(near(b, P_SIZE + 1, W), near(b, -W, -P_SIZE - 1)),
            both(near(b, -W, -1), near(b, -W, -1)),
            both(near(b, -W, -P_SIZE - 1), near(b, -W, -P_SIZE - 1)),
        ]

    main_t, rim_t = side_tables(2 * LANE, 2 * LANE, False), side_tables(LANE, 2 * LANE, True)
    mid_t, edge_t = side_tables(LANE, LANE, False), side_tables(LANE, LANE, True)
    pair_table, last_table = [], []
    for k in (0, 2):
        pair_table.append(jnp.concatenate([main_t[k]] * 2 + [main_t[k + 1]] * 2 + [rim_t[k]] * 2 + [rim_t[k + 1]] * 2, axis=0))
        last_table.append(jnp.concatenate([mid_t[k], edge_t[k]] * 2 + [mid_t[k + 1], edge_t[k + 1]] * 2, axis=0))
    flip = 7 - lax.broadcasted_iota(jnp.int32, (8, cols), 0)
    cells_donut = (2 * W + 1) ** 2 - (2 * P_SIZE + 1) ** 2 - 4 * (W - P_SIZE)
    cells_lower = W * W - P_SIZE * P_SIZE
    factor = jnp.concatenate([factor_ref[b : b + 1, :] for b in range(blocks)], axis=1)

    copies = []

    def upright(start):
        ratios = normed_ref[start : start + SPAN, :] * factor
        level = pltpu.roll(ratios, 0, 1, stride=1, stride_axis=0)
        stacked = jnp.concatenate(halves(level), axis=0)
        summed = jnp.dot(down_table, stacked, preferred_element_type=jnp.float32)
        return ratios[TOP : TOP + STEP, :cols], summed

    lanes = lax.broadcasted_iota(jnp.int32, (STEP, LANE), 1)

    def sideways(summed, k):
        mains, rims = [], []
        x = summed[k * STEP : (k + 1) * STEP, :]
        pieces = [x[:, b * LANE : (b + 1) * LANE] for b in range(blocks)]
        rim = jnp.concatenate(
            [jnp.where(lanes < SIDE, pieces[(2 * c + 2) % blocks], pieces[(2 * c - 1) % blocks]) for c in range(blocks // 2)],
            axis=0,
        )
        last = jnp.concatenate([pieces[-1], jnp.where(lanes < SIDE, pieces[0], pieces[-2])], axis=1)
        main = jnp.concatenate([x[:, 2 * c * LANE : (2 * c + 2) * LANE] for c in range(blocks // 2)], axis=0)
        return halves(main), halves(rim), halves(last)

    def level_out(start, here, summed):
        for to, out_ref, out, k, cell_count in (
            (0, donut_ref, donut, 0, cells_donut),
            (1, lower_ref, lower, 2, cells_lower),
        ):
            (m0, r0, l0), (m1, r1, l1) = sideways(summed, k), sideways(summed, k + 1)
            tall = jnp.dot(jnp.concatenate(m0 + m1 + r0 + r1, axis=1), pair_table[k // 2], preferred_element_type=jnp.float32)
            end = jnp.dot(jnp.concatenate(l0 + l1, axis=1), last_table[k // 2], preferred_element_type=jnp.float32)
            flat = jnp.concatenate([tall[c * STEP : (c + 1) * STEP, :] for c in range(blocks // 2)] + [end], axis=1)
            for g in range(STEP // 8):
                rows_g = slice(8 * g, 8 * g + 8)
                back = pltpu.roll(flat[rows_g, :], width - TOP - 8 * g - 7, 1, stride=1, stride_axis=0)[:, :cols]
                back = jnp.take_along_axis(back, flip, axis=0)
                out[start + 8 * g : start + 8 * g + 8, :] = here[rows_g, :] / jnp.maximum(back / cell_count, 0.25)
            span = pl.ds(start, STEP)
            copies.append(pltpu.make_async_copy(out.at[span, :], out_ref.at[span, :], sems.at[to, start // STEP]))
            copies[-1].start()

    for start in range(0, rows, STEP):
        level_out(start, *upright(start))
    for copy in copies:
        copy.wait()


def windows(normed, factor):
    rows, cols = normed.shape[0] - 2 * TOP, normed.shape[1] - LANE
    out = jax.ShapeDtypeStruct((rows, cols), jnp.float32)
    return pl.pallas_call(
        window_kernel,
        out_shape=(out, out),
        in_specs=[pl.BlockSpec(memory_space=pltpu.VMEM), pl.BlockSpec(memory_space=pltpu.VMEM)],
        out_specs=(pl.BlockSpec(memory_space=pltpu.HBM), pl.BlockSpec(memory_space=pltpu.HBM)),
        scratch_shapes=[
            pltpu.VMEM((rows, cols), jnp.float32),
            pltpu.VMEM((rows, cols), jnp.float32),
            pltpu.SemaphoreType.DMA((2, rows // STEP)),
        ],
        compiler_params=pltpu.CompilerParams(vmem_limit_bytes=32 * 1024 * 1024),
        name="windows",
    )(normed, factor)


def local(counts, bin_mask):
    rows, cols = counts.shape
    n_pos = lax.axis_size("pos")
    n_off = lax.axis_size("off")
    inner = 8
    outer = n_pos // inner
    near_offs = 4
    far_offs = n_off // near_offs
    width = cols + LANE
    vecs = cols // LANE + 1
    n_slots = cols // rows + 6
    reach = (cols // rows + 3) * rows
    halves_n = rows // LANE
    third = -(-rows // 24) * 8
    dma = pltpu.SemaphoreType.DMA
    f32 = jnp.float32
    normed, factor = pl.pallas_call(
        functools.partial(comm_kernel, (n_pos, n_off)),
        out_shape=(
            pltpu.VMEM((rows + 2 * TOP, width), f32),
            pltpu.VMEM((vecs, LANE), f32),
        ),
        in_specs=[pl.BlockSpec(memory_space=pltpu.HBM), pl.BlockSpec(memory_space=pltpu.HBM)],
        out_specs=(pl.BlockSpec(memory_space=pltpu.VMEM), pl.BlockSpec(memory_space=pltpu.VMEM)),
        scratch_shapes=[
            pltpu.VMEM((rows + 2 * TOP, cols + 2 * LANE), f32),
            pltpu.VMEM((2, third, LANE), f32),
            pltpu.VMEM((2, third, LANE), f32),
            pltpu.VMEM((halves_n, LANE), jnp.int32),
            pltpu.VMEM((halves_n, LANE), f32),
            pltpu.VMEM((n_slots - 3, halves_n, LANE), f32),
            pltpu.VMEM((near_offs, halves_n, LANE), f32),
            pltpu.VMEM((2 * halves_n, LANE), f32),
            pltpu.VMEM((far_offs, n_slots, 2 * halves_n, LANE), f32),
            pltpu.VMEM((n_slots, halves_n, LANE), f32),
            pltpu.VMEM((rows + 2 * TOP, LANE), f32),
            pltpu.VMEM((LANE // 8, 8, reach), f32),
            pltpu.VMEM((inner, vecs, LANE), f32),
            pltpu.VMEM((outer, vecs, LANE), f32),
            pltpu.VMEM((inner, vecs, LANE), f32),
            pltpu.VMEM((outer, vecs, LANE), f32),
            dma,
            dma,
            dma((near_offs,)),
            dma((near_offs,)),
            dma((8,)),
            dma((8,)),
            dma((n_slots - 3,)),
            dma((n_slots - 3,)),
            dma((far_offs, n_slots)),
            dma((far_offs, n_slots)),
            dma((inner,)),
            dma((inner,)),
            dma((outer,)),
            dma((outer,)),
            dma((inner,)),
            dma((inner,)),
            dma((outer,)),
            dma((outer,)),
        ],
        compiler_params=pltpu.CompilerParams(
            collective_id=0, has_side_effects=True, vmem_limit_bytes=24 * 1024 * 1024
        ),
        name="comm",
    )(
        pltpu.with_memory_space_constraint(counts, pltpu.HBM),
        pltpu.with_memory_space_constraint(bin_mask.reshape(halves_n, LANE), pltpu.HBM),
    )
    return windows(normed, factor)


def solution(mesh):
    placed = (P("pos", "off"), P("pos"))
    return jax.shard_map(
        local,
        mesh=mesh,
        in_specs=placed,
        out_specs=(P("pos", "off"), P("pos", "off")),
        check_vma=False,
    )
```

```python
import functools

import jax
import jax.numpy as jnp
from jax import lax
from jax.experimental import pallas as pl
from jax.experimental.pallas import tpu as pltpu
from jax.sharding import PartitionSpec as P

W = 20
P_SIZE = 8
TOP = 24
LANE = 128
SIDE = 64
STEP = 64
SPAN = STEP + 2 * TOP
MESH = pl.DeviceIdType.MESH


def comm_kernel(
    sizes, counts_ref, mask_ref, normed_ref, factor_ref,
    cells, strips_out, strips_in, mask, own_live, live, cov, own, wts, lines, row_w, tables, part, group, part_live, group_live,
    load_sem, mask_sem, cov_send, cov_recv, halo_send, halo_recv, live_send, live_recv, wts_send, wts_recv,
    part_send, part_recv, group_send, group_recv, part_live_send, part_live_recv, group_live_send, group_live_recv,
):
    n_pos, n_off = sizes
    rows, cols = counts_ref.shape
    width = cols + LANE
    blocks = cols // LANE
    ratio = cols // rows
    near_offs = cov.shape[0]
    far_offs = n_off // near_offs
    inner = part.shape[0]
    outer = group.shape[0]
    pos = lax.axis_index("pos")
    off = lax.axis_index("off")
    total_bins = rows * n_pos
    band = cols * n_off
    row_halves = rows // LANE
    third = strips_in.shape[1]

    def at_pos(k):
        return lax.rem(pos + (k + n_pos), n_pos)

    def at_off(k):
        return lax.rem(off + (k + n_off), n_off)

    first = ratio * off
    far = off // near_offs
    near = off - far * near_offs
    quot = pos // inner
    rank = pos - quot * inner
    cov_peers = [(pos, far * near_offs + lax.rem(near + r, near_offs)) for r in range(1, near_offs)]
    halo_moves = [(0, -1), (0, 1), (-1, 0), (1, 0), (-1, -1), (-1, 1), (1, -1), (1, 1)]
    steps = list(range(-1, ratio + 2))
    n_steps = len(steps)
    self_step = steps.index(0)
    own_slot = n_steps
    n_slots = n_steps + 3
    part_peers = [(quot * inner + lax.rem(rank + r, inner), off) for r in range(1, inner)]
    group_peers = [(lax.rem(quot + r, outer) * inner + rank, off) for r in range(1, outer)]

    def wts_target(t, slot):
        there = lax.rem(far + t, far_offs) * near_offs + near
        if slot < n_steps:
            return (lax.rem(pos - ratio * there - steps[slot] + n_pos, n_pos), there)
        return (at_pos((0, 1, -1)[slot - n_steps]), there)

    def wts_source(t, slot):
        there = lax.rem(far - t + far_offs, far_offs) * near_offs + near
        if slot < n_steps:
            return (lax.rem(pos + first + steps[slot] + n_pos, n_pos), there)
        return (at_pos((0, -1, 1)[slot - n_steps]), there)

    moves = []
    for t in list(range(1, far_offs)) + [0]:
        for slot in range(n_slots):
            if t or slot != own_slot:
                moves.append((t, slot, t == 0 and slot == self_step))
    live_slots = [slot for slot in range(n_slots) if slot != own_slot]

    load = pltpu.make_async_copy(counts_ref, cells.at[pl.ds(TOP, rows), pl.ds(0, cols)], load_sem)
    load.start()
    load_mask = pltpu.make_async_copy(mask_ref, mask, mask_sem)
    load_mask.start()

    barrier = pltpu.get_barrier_semaphore()

    def greet(device):
        pl.semaphore_signal(barrier, inc=1, device_id=device, device_id_type=MESH)

    for t, slot, selfish in moves:
        if selfish:
            pl.when(off > 0)(functools.partial(greet, wts_source(t, slot)))
        else:
            greet(wts_source(t, slot))
    for device in cov_peers:
        greet(device)
    for a, b in halo_moves:
        greet((at_pos(-a), at_off(-b)))
    for device in part_peers + group_peers:
        greet(device)

    @pl.when(off == 0)
    def _():
        strips_in[1] = jnp.zeros(strips_in.shape[1:], jnp.float32)
        for place in (0, TOP + rows):
            cells[place : place + TOP, cols + LANE :] = jnp.zeros((TOP, LANE), jnp.float32)

    @pl.when(off == n_off - 1)
    def _():
        strips_in[0] = jnp.zeros(strips_in.shape[1:], jnp.float32)
        for place in (0, TOP + rows):
            cells[place : place + TOP, cols : cols + LANE] = jnp.zeros((TOP, LANE), jnp.float32)

    load.wait()

    base = pos * rows + off * cols
    acc = None
    for b in range(blocks):
        row_i = lax.broadcasted_iota(jnp.int32, (rows, LANE), 0)
        col_i = lax.broadcasted_iota(jnp.int32, (rows, LANE), 1)
        piece = cells[TOP : TOP + rows, b * LANE : (b + 1) * LANE]
        piece = jnp.where(row_i + col_i < total_bins - base - b * LANE, piece, 0.0)
        acc = piece if acc is None else acc + piece
    for h in range(row_halves):
        turned = acc[h * LANE : (h + 1) * LANE, :].T
        cov[0, h : h + 1, :] = jnp.sum(turned, axis=0, keepdims=True)
    load_mask.wait()
    own_live[...] = mask[...].astype(jnp.float32)

    n_greet = len(cov_peers) + len(moves) - 1 + len(halo_moves) + len(part_peers) + len(group_peers)
    pl.semaphore_wait(barrier, n_greet + jnp.where(off > 0, 1, 0))

    def remote(src, dst, send, recv, device):
        return pltpu.make_async_remote_copy(
            src_ref=src, dst_ref=dst, send_sem=send, recv_sem=recv, device_id=device, device_id_type=MESH
        )

    cov_copies = [
        remote(cov.at[0], cov.at[r], cov_send.at[r], cov_recv.at[r], cov_peers[r - 1]) for r in range(1, near_offs)
    ]
    for copy in cov_copies:
        copy.start()

    live_copies = [
        remote(own_live, live.at[k], live_send.at[k], live_recv.at[k], wts_target(0, k)) for k in live_slots
    ]

    def each_live(act):
        for k, copy in zip(live_slots, live_copies):
            if k == self_step:
                pl.when(off > 0)(getattr(copy, act))
            else:
                getattr(copy, act)()

    each_live("start")
    live[own_slot] = own_live[...]

    @pl.when(off == 0)
    def _():
        live[self_step] = own_live[...]

    spans = {-1: (pl.ds(0, TOP), pl.ds(TOP + rows, TOP)), 1: (pl.ds(rows - TOP, TOP), pl.ds(0, TOP))}
    strips = {
        -1: (pl.ds(0, LANE), pl.ds(cols, LANE)),
        1: (pl.ds(cols - LANE, LANE), pl.ds(cols + LANE, LANE)),
        0: (pl.ds(0, cols), pl.ds(0, cols)),
    }
    halo_copies = []
    for k, (a, b) in enumerate(halo_moves):
        if a == 0:
            side = 0 if b < 0 else 1
            ends = strips_out.at[side], strips_in.at[side]
        else:
            ends = counts_ref.at[spans[a][0], strips[b][0]], cells.at[spans[a][1], strips[b][1]]
        halo_copies.append(remote(*ends, halo_send.at[k], halo_recv.at[k], (at_pos(a), at_off(b))))

    def sends(b):
        return off > 0 if b < 0 else off < n_off - 1

    def each_halo(copies, act):
        for (a, b), copy in copies:
            if b == 0:
                getattr(copy, act)()
            elif act == "wait_recv":
                pl.when(sends(-b))(copy.wait_recv)
            else:
                pl.when(sends(b))(getattr(copy, act))

    halos = list(zip(halo_moves, halo_copies))
    each_halo(halos[2:], "start")

    spare = LANE // 3
    lane_t = lax.broadcasted_iota(jnp.int32, (third, LANE), 1)
    for side in (0, 1):
        packed = None
        for k in range(3):
            low = TOP + k * third
            high = min(low + third, TOP + rows)
            piece = cells[low:high, 0:LANE] if side == 0 else cells[low:high, cols - LANE : cols]
            if high - low < third:
                piece = jnp.concatenate([piece, jnp.zeros((third - high + low, LANE), jnp.float32)], axis=0)
            if side == 0:
                piece = pltpu.roll(piece, k * spare, 1) if k else piece
                here = (lane_t >= k * spare) & (lane_t < (k + 1) * spare)
            else:
                piece = pltpu.roll(piece, LANE - k * spare, 1) if k else piece
                here = (lane_t < LANE - k * spare) & (lane_t >= LANE - (k + 1) * spare)
            packed = jnp.where(here, piece, 0.0 if packed is None else packed)
        strips_out[side] = packed

    each_halo(halos[:2], "start")

    for copy in cov_copies:
        copy.wait_recv()
    coverage = cov[0]
    for r in range(1, near_offs):
        coverage = coverage + cov[r]
    own[...] = coverage

    wts_copies = [
        remote(own, wts.at[t, slot], wts_send.at[t, slot], wts_recv.at[t, slot], wts_target(t, slot))
        for t, slot, _ in moves
    ]

    def each_wts(act, side):
        for (_, slot, selfish), copy in zip(moves, wts_copies):
            if side != (slot > own_slot):
                continue
            if selfish:
                pl.when(off > 0)(getattr(copy, act))
            else:
                getattr(copy, act)()

    each_wts("start", False)
    wts[0, own_slot] = own[...]

    @pl.when(off == 0)
    def _():
        wts[0, self_step] = own[...]

    def down(vector):
        return jnp.broadcast_to(vector, (LANE, LANE)).T

    phases = LANE // 8

    def spread(source):
        pieces = []
        for k, d in enumerate(steps):
            block = pos + first + d
            inside = (block >= 0) & (block < n_pos)
            for h in range(row_halves):
                pieces.append(jnp.where(inside, source[k, h : h + 1, :], 0.0))
        line = jnp.concatenate(pieces, axis=1)
        reach = line.shape[1]
        line = jnp.broadcast_to(line, (8, reach))
        line = pltpu.roll(line, reach - 7, 1, stride=1, stride_axis=0)
        flip = 7 - lax.broadcasted_iota(jnp.int32, (8, reach), 0)
        line = jnp.take_along_axis(line, flip, axis=0)
        for h in range(phases):
            tables[h] = line if h == 0 else pltpu.roll(line, reach - 8 * h, 1)

    lane_8 = lax.broadcasted_iota(jnp.int32, (8, LANE), 1)
    low_lanes = lane_8 < SIDE

    def column(g, b):
        place = 8 * g + rows - TOP
        h, shift = (place % LANE) // 8, place // LANE * LANE
        if b < blocks:
            return tables[h, :, shift + b * LANE : shift + (b + 1) * LANE]
        after = tables[h, :, shift + cols : shift + cols + LANE]
        return jnp.where(low_lanes, after, tables[h, :, shift - LANE : shift])

    own_groups = range(TOP // 8, (TOP + rows) // 8)

    def column_sums(to, terms_of):
        sums = [None] * (blocks + 1)
        for g in own_groups:
            for b, term in enumerate(terms_of(g)):
                sums[b] = term if sums[b] is None else sums[b] + term
        for b, total in enumerate(sums):
            to[0, b : b + 1, :] = jnp.sum(total, axis=0, keepdims=True)

    def share(buffer, send, recv, peers):
        copies = [
            remote(buffer.at[0], buffer.at[r], send.at[r], recv.at[r], peers[r - 1]) for r in range(1, buffer.shape[0])
        ]
        for copy in copies:
            copy.start()
        return copies

    def gather(copies, buffer):
        for copy in copies:
            copy.wait_recv()
        total = buffer[0]
        for r in range(1, buffer.shape[0]):
            total = total + buffer[r]
        return total

    each_live("wait_recv")
    for h in range(row_halves):
        row_w[TOP + h * LANE : TOP + (h + 1) * LANE, :] = down(own_live[h : h + 1, :])
    spread(live)

    def live_terms(g):
        row = row_w[8 * g : 8 * g + 8, :]
        return [row * column(g, b) for b in range(blocks + 1)]

    column_sums(part_live, live_terms)
    part_live_copies = share(part_live, part_live_send, part_live_recv, part_peers)

    def weigh(low, high):
        gathered = wts[0, low:high]
        for t in range(1, far_offs):
            gathered = gathered + wts[t, low:high]
        lines[low:high] = live[low:high] / jnp.sqrt(gathered)

    each_wts("wait_recv", False)
    weigh(0, own_slot + 1)
    for h in range(row_halves):
        row_w[TOP + h * LANE : TOP + (h + 1) * LANE, :] = down(lines[own_slot, h : h + 1, :])
    spread(lines)

    def row_group(g):
        rows_g = slice(8 * g, 8 * g + 8)
        weight = row_w[rows_g, :]
        outs = []
        for b in range(blocks + 1):
            if b < blocks:
                count = cells[rows_g, b * LANE : (b + 1) * LANE]
            else:
                own_row = 8 * g - TOP
                if 0 <= own_row < rows:
                    k, at = own_row // third, own_row % third
                    after, before = strips_in[0, at : at + 8, :], strips_in[1, at : at + 8, :]
                    if k:
                        after = pltpu.roll(after, LANE - k * spare, 1)
                        before = pltpu.roll(before, k * spare, 1)
                else:
                    after, before = cells[rows_g, cols : cols + LANE], cells[rows_g, cols + LANE : cols + 2 * LANE]
                count = jnp.where(low_lanes, after, before)
            value = count * weight * column(g, b)
            normed_ref[rows_g, b * LANE : (b + 1) * LANE] = value
            outs.append(value)
        return outs

    each_halo(halos[:2], "wait_recv")
    column_sums(part, row_group)
    part_copies = share(part, part_send, part_recv, part_peers)

    each_wts("start", True)

    group_live[0] = gather(part_live_copies, part_live)
    group_live_copies = share(group_live, group_live_send, group_live_recv, group_peers)
    group[0] = gather(part_copies, part)
    group_copies = share(group, group_send, group_recv, group_peers)

    each_halo(halos[2:], "wait_recv")
    each_wts("wait_recv", True)
    weigh(own_slot + 1, n_slots)
    for side, h, low, place in ((0, row_halves - 1, LANE - TOP, 0), (1, 0, 0, TOP + rows)):
        block = pos + (1 if side else -1)
        inside = (block >= 0) & (block < n_pos)
        weight = jnp.where(inside, lines[own_slot + 1 + side, h : h + 1, :], 0.0)
        row_w[place : place + TOP, :] = down(weight)[low : low + TOP, :]
    for g in list(range(TOP // 8)) + list(range((TOP + rows) // 8, (2 * TOP + rows) // 8)):
        row_group(g)

    for copy in cov_copies + part_copies + part_live_copies:
        copy.wait_send()
    each_halo(halos, "wait_send")
    each_wts("wait_send", False)
    each_wts("wait_send", True)
    each_live("wait_send")
    pairs = gather(group_live_copies, group_live)
    expected = gather(group_copies, group)
    lane = lax.broadcasted_iota(jnp.int32, expected.shape, 1)
    place = lax.broadcasted_iota(jnp.int32, expected.shape, 0) * LANE + lane
    needed = (place < cols + 2 * W) | (place >= width - 2 * W)
    place = off * cols + jnp.where(place < cols + SIDE, place, place - width)
    factor = pairs / jnp.where(expected > 0, expected, 1.0)
    factor_ref[...] = jnp.where(needed & (place >= 0) & (place < band), factor, 0.0)
    for copy in group_copies + group_live_copies:
        copy.wait_send()


def near(distance, lowest, highest):
    return (distance >= lowest) & (distance <= highest)


def both(mask_a, mask_b):
    return jnp.where(mask_a | mask_b, 1.0, 0.0).astype(jnp.bfloat16)


def halves(values):
    high = values.astype(jnp.bfloat16)
    return high, (values - high.astype(jnp.float32)).astype(jnp.bfloat16)


def window_kernel(normed_ref, factor_ref, donut_ref, lower_ref, donut, lower, sems):
    width = normed_ref.shape[1]
    rows, cols = donut_ref.shape
    blocks = width // LANE

    out_row = lax.broadcasted_iota(jnp.int32, (STEP, 2 * SPAN), 0)
    out_row = (out_row // 8) * 8 + 7 - lax.rem(out_row, 8)
    in_row = lax.broadcasted_iota(jnp.int32, (STEP, 2 * SPAN), 1)
    in_row = jnp.where(in_row < SPAN, in_row, in_row - SPAN)
    a = in_row - TOP - out_row
    down_table = jnp.concatenate(
        [
            both(near(a, P_SIZE + 1, W), near(a, -W, -P_SIZE - 1)),
            both(near(a, 1, P_SIZE), near(a, -P_SIZE, -1)),
            both(near(a, P_SIZE + 1, W), near(a, P_SIZE + 1, W)),
            both(near(a, 1, P_SIZE), near(a, 1, P_SIZE)),
        ],
        axis=0,
    )
    def side_tables(depth, wide, split):
        shape = (depth, wide)
        at = lax.broadcasted_iota(jnp.int32, shape, 0)
        if split:
            at = jnp.where(at < SIDE, at + wide, at - LANE)
        b = at - lax.broadcasted_iota(jnp.int32, shape, 1)
        return [
            both(near(b, 1, W), near(b, -W, -1)),
            both(near(b, P_SIZE + 1, W), near(b, -W, -P_SIZE - 1)),
            both(near(b, -W, -1), near(b, -W, -1)),
            both(near(b, -W, -P_SIZE - 1), near(b, -W, -P_SIZE - 1)),
        ]

    main_t, rim_t = side_tables(2 * LANE, 2 * LANE, False), side_tables(LANE, 2 * LANE, True)
    mid_t, edge_t = side_tables(LANE, LANE, False), side_tables(LANE, LANE, True)
    pair_table, last_table = [], []
    for k in (0, 2):
        pair_table.append(jnp.concatenate([main_t[k]] * 2 + [main_t[k + 1]] * 2 + [rim_t[k]] * 2 + [rim_t[k + 1]] * 2, axis=0))
        last_table.append(jnp.concatenate([mid_t[k], edge_t[k]] * 2 + [mid_t[k + 1], edge_t[k + 1]] * 2, axis=0))
    flip = 7 - lax.broadcasted_iota(jnp.int32, (8, cols), 0)
    cells_donut = (2 * W + 1) ** 2 - (2 * P_SIZE + 1) ** 2 - 4 * (W - P_SIZE)
    cells_lower = W * W - P_SIZE * P_SIZE
    factor = jnp.concatenate([factor_ref[b : b + 1, :] for b in range(blocks)], axis=1)

    copies = []

    def upright(start):
        ratios = normed_ref[start : start + SPAN, :] * factor
        level = pltpu.roll(ratios, 0, 1, stride=1, stride_axis=0)
        stacked = jnp.concatenate(halves(level), axis=0)
        summed = jnp.dot(down_table, stacked, preferred_element_type=jnp.float32)
        return ratios[TOP : TOP + STEP, :cols], summed

    lanes = lax.broadcasted_iota(jnp.int32, (STEP, LANE), 1)

    def sideways(summed, k):
        mains, rims = [], []
        x = summed[k * STEP : (k + 1) * STEP, :]
        pieces = [x[:, b * LANE : (b + 1) * LANE] for b in range(blocks)]
        rim = jnp.concatenate(
            [jnp.where(lanes < SIDE, pieces[(2 * c + 2) % blocks], pieces[(2 * c - 1) % blocks]) for c in range(blocks // 2)],
            axis=0,
        )
        last = jnp.concatenate([pieces[-1], jnp.where(lanes < SIDE, pieces[0], pieces[-2])], axis=1)
        main = jnp.concatenate([x[:, 2 * c * LANE : (2 * c + 2) * LANE] for c in range(blocks // 2)], axis=0)
        return halves(main), halves(rim), halves(last)

    def level_out(start, here, summed):
        for to, out_ref, out, k, cell_count in (
            (0, donut_ref, donut, 0, cells_donut),
            (1, lower_ref, lower, 2, cells_lower),
        ):
            (m0, r0, l0), (m1, r1, l1) = sideways(summed, k), sideways(summed, k + 1)
            tall = jnp.dot(jnp.concatenate(m0 + m1 + r0 + r1, axis=1), pair_table[k // 2], preferred_element_type=jnp.float32)
            end = jnp.dot(jnp.concatenate(l0 + l1, axis=1), last_table[k // 2], preferred_element_type=jnp.float32)
            flat = jnp.concatenate([tall[c * STEP : (c + 1) * STEP, :] for c in range(blocks // 2)] + [end], axis=1)
            for g in range(STEP // 8):
                rows_g = slice(8 * g, 8 * g + 8)
                back = pltpu.roll(flat[rows_g, :], width - TOP - 8 * g - 7, 1, stride=1, stride_axis=0)[:, :cols]
                back = jnp.take_along_axis(back, flip, axis=0)
                out[start + 8 * g : start + 8 * g + 8, :] = here[rows_g, :] / jnp.maximum(back / cell_count, 0.25)
            span = pl.ds(start, STEP)
            copies.append(pltpu.make_async_copy(out.at[span, :], out_ref.at[span, :], sems.at[to, start // STEP]))
            copies[-1].start()

    for start in range(0, rows, STEP):
        level_out(start, *upright(start))
    for copy in copies:
        copy.wait()


def windows(normed, factor):
    rows, cols = normed.shape[0] - 2 * TOP, normed.shape[1] - LANE
    out = jax.ShapeDtypeStruct((rows, cols), jnp.float32)
    return pl.pallas_call(
        window_kernel,
        out_shape=(out, out),
        in_specs=[pl.BlockSpec(memory_space=pltpu.VMEM), pl.BlockSpec(memory_space=pltpu.VMEM)],
        out_specs=(pl.BlockSpec(memory_space=pltpu.HBM), pl.BlockSpec(memory_space=pltpu.HBM)),
        scratch_shapes=[
            pltpu.VMEM((rows, cols), jnp.float32),
            pltpu.VMEM((rows, cols), jnp.float32),
            pltpu.SemaphoreType.DMA((2, rows // STEP)),
        ],
        compiler_params=pltpu.CompilerParams(vmem_limit_bytes=32 * 1024 * 1024),
        name="windows",
    )(normed, factor)


def local(counts, bin_mask):
    rows, cols = counts.shape
    n_pos = lax.axis_size("pos")
    n_off = lax.axis_size("off")
    inner = 8
    outer = n_pos // inner
    near_offs = 4
    far_offs = n_off // near_offs
    width = cols + LANE
    vecs = cols // LANE + 1
    n_slots = cols // rows + 6
    reach = (cols // rows + 3) * rows
    halves_n = rows // LANE
    third = -(-rows // 24) * 8
    dma = pltpu.SemaphoreType.DMA
    f32 = jnp.float32
    normed, factor = pl.pallas_call(
        functools.partial(comm_kernel, (n_pos, n_off)),
        out_shape=(
            pltpu.VMEM((rows + 2 * TOP, width), f32),
            pltpu.VMEM((vecs, LANE), f32),
        ),
        in_specs=[pl.BlockSpec(memory_space=pltpu.HBM), pl.BlockSpec(memory_space=pltpu.HBM)],
        out_specs=(pl.BlockSpec(memory_space=pltpu.VMEM), pl.BlockSpec(memory_space=pltpu.VMEM)),
        scratch_shapes=[
            pltpu.VMEM((rows + 2 * TOP, cols + 2 * LANE), f32),
            pltpu.VMEM((2, third, LANE), f32),
            pltpu.VMEM((2, third, LANE), f32),
            pltpu.VMEM((halves_n, LANE), jnp.int32),
            pltpu.VMEM((halves_n, LANE), f32),
            pltpu.VMEM((n_slots, halves_n, LANE), f32),
            pltpu.VMEM((near_offs, halves_n, LANE), f32),
            pltpu.VMEM((halves_n, LANE), f32),
            pltpu.VMEM((far_offs, n_slots, halves_n, LANE), f32),
            pltpu.VMEM((n_slots, halves_n, LANE), f32),
            pltpu.VMEM((rows + 2 * TOP, LANE), f32),
            pltpu.VMEM((LANE // 8, 8, reach), f32),
            pltpu.VMEM((inner, vecs, LANE), f32),
            pltpu.VMEM((outer, vecs, LANE), f32),
            pltpu.VMEM((inner, vecs, LANE), f32),
            pltpu.VMEM((outer, vecs, LANE), f32),
            dma,
            dma,
            dma((near_offs,)),
            dma((near_offs,)),
            dma((8,)),
            dma((8,)),
            dma((n_slots,)),
            dma((n_slots,)),
            dma((far_offs, n_slots)),
            dma((far_offs, n_slots)),
            dma((inner,)),
            dma((inner,)),
            dma((outer,)),
            dma((outer,)),
            dma((inner,)),
            dma((inner,)),
            dma((outer,)),
            dma((outer,)),
        ],
        compiler_params=pltpu.CompilerParams(
            collective_id=0, has_side_effects=True, vmem_limit_bytes=24 * 1024 * 1024
        ),
        name="comm",
    )(
        pltpu.with_memory_space_constraint(counts, pltpu.HBM),
        pltpu.with_memory_space_constraint(bin_mask.reshape(halves_n, LANE), pltpu.HBM),
    )
    return windows(normed, factor)


def solution(mesh):
    placed = (P("pos", "off"), P("pos"))
    return jax.shard_map(
        local,
        mesh=mesh,
        in_specs=placed,
        out_specs=(P("pos", "off"), P("pos", "off")),
        check_vma=False,
    )
```

```python
import functools

import jax
import jax.numpy as jnp
from jax import lax
from jax.experimental import pallas as pl
from jax.experimental.pallas import tpu as pltpu
from jax.sharding import PartitionSpec as P

W = 20
P_SIZE = 8
TOP = 24
LANE = 128
SIDE = 64
STEP = 64
SPAN = STEP + 2 * TOP
MESH = pl.DeviceIdType.MESH


def comm_kernel(
    sizes, counts_ref, mask_ref, normed_ref, factor_ref,
    cells, strips_out, strips_in, mask, own_live, live, cov, own, wts, lines, row_w, tables, part, group, part_live, group_live,
    load_sem, mask_sem, cov_send, cov_recv, halo_send, halo_recv, live_send, live_recv, wts_send, wts_recv,
    part_send, part_recv, group_send, group_recv, part_live_send, part_live_recv, group_live_send, group_live_recv,
):
    n_pos, n_off = sizes
    rows, cols = counts_ref.shape
    width = cols + LANE
    blocks = cols // LANE
    ratio = cols // rows
    near_offs = cov.shape[0]
    far_offs = n_off // near_offs
    inner = part.shape[0]
    outer = group.shape[0]
    pos = lax.axis_index("pos")
    off = lax.axis_index("off")
    total_bins = rows * n_pos
    band = cols * n_off
    row_halves = rows // LANE
    third = strips_in.shape[1]

    def at_pos(k):
        return lax.rem(pos + (k + n_pos), n_pos)

    def at_off(k):
        return lax.rem(off + (k + n_off), n_off)

    first = ratio * off
    far = off // near_offs
    near = off - far * near_offs
    quot = pos // inner
    rank = pos - quot * inner
    cov_peers = [(pos, far * near_offs + lax.rem(near + r, near_offs)) for r in range(1, near_offs)]
    halo_moves = [(0, -1), (0, 1), (-1, 0), (1, 0), (-1, -1), (-1, 1), (1, -1), (1, 1)]
    steps = list(range(-1, ratio + 2))
    n_steps = len(steps)
    self_step = steps.index(0)
    own_slot = n_steps
    n_slots = n_steps + 3
    part_peers = [(quot * inner + lax.rem(rank + r, inner), off) for r in range(1, inner)]
    group_peers = [(lax.rem(quot + r, outer) * inner + rank, off) for r in range(1, outer)]

    def wts_target(t, slot):
        there = lax.rem(far + t, far_offs) * near_offs + near
        if slot < n_steps:
            return (lax.rem(pos - ratio * there - steps[slot] + n_pos, n_pos), there)
        return (at_pos((0, 1, -1)[slot - n_steps]), there)

    def wts_source(t, slot):
        there = lax.rem(far - t + far_offs, far_offs) * near_offs + near
        if slot < n_steps:
            return (lax.rem(pos + first + steps[slot] + n_pos, n_pos), there)
        return (at_pos((0, -1, 1)[slot - n_steps]), there)

    def within(place):
        return (place >= 0) & (place < n_pos)

    def wts_sends(t, slot):
        there = lax.rem(far + t, far_offs) * near_offs + near
        if slot < n_steps:
            valid = within(pos - ratio * there - steps[slot])
            return valid & (off > 0) if t == 0 and slot == self_step else valid
        return within(pos + (0, 1, -1)[slot - n_steps])

    def wts_receives(t, slot):
        if slot < n_steps:
            valid = within(pos + first + steps[slot])
            return valid & (off > 0) if t == 0 and slot == self_step else valid
        return within(pos + (0, -1, 1)[slot - n_steps])

    moves = []
    for t in list(range(1, far_offs)) + [0]:
        for slot in range(n_slots):
            if t or slot != own_slot:
                moves.append((t, slot))
    live_slots = [slot for slot in range(n_slots) if slot != own_slot]

    load = pltpu.make_async_copy(counts_ref, cells.at[pl.ds(TOP, rows), pl.ds(0, cols)], load_sem)
    load.start()
    load_mask = pltpu.make_async_copy(mask_ref, mask, mask_sem)
    load_mask.start()

    barrier = pltpu.get_barrier_semaphore()

    def greet(device):
        pl.semaphore_signal(barrier, inc=1, device_id=device, device_id_type=MESH)

    for t, slot in moves:
        if slot == own_slot:
            greet(wts_source(t, slot))
        else:
            pl.when(wts_receives(t, slot))(functools.partial(greet, wts_source(t, slot)))
    for device in cov_peers:
        greet(device)
    for a, b in halo_moves:
        greet((at_pos(-a), at_off(-b)))
    for device in part_peers + group_peers:
        greet(device)

    @pl.when(off == 0)
    def _():
        strips_in[1] = jnp.zeros(strips_in.shape[1:], jnp.float32)
        for place in (0, TOP + rows):
            cells[place : place + TOP, cols + LANE :] = jnp.zeros((TOP, LANE), jnp.float32)

    @pl.when(off == n_off - 1)
    def _():
        strips_in[0] = jnp.zeros(strips_in.shape[1:], jnp.float32)
        for place in (0, TOP + rows):
            cells[place : place + TOP, cols : cols + LANE] = jnp.zeros((TOP, LANE), jnp.float32)

    load.wait()

    base = pos * rows + off * cols
    acc = None
    for b in range(blocks):
        row_i = lax.broadcasted_iota(jnp.int32, (rows, LANE), 0)
        col_i = lax.broadcasted_iota(jnp.int32, (rows, LANE), 1)
        piece = cells[TOP : TOP + rows, b * LANE : (b + 1) * LANE]
        piece = jnp.where(row_i + col_i < total_bins - base - b * LANE, piece, 0.0)
        acc = piece if acc is None else acc + piece
    for h in range(row_halves):
        turned = acc[h * LANE : (h + 1) * LANE, :].T
        cov[0, h : h + 1, :] = jnp.sum(turned, axis=0, keepdims=True)
    load_mask.wait()
    own_live[...] = mask[...].astype(jnp.float32)

    n_greet = len(cov_peers) + len(halo_moves) + len(part_peers) + len(group_peers)
    for t, slot in moves:
        n_greet = n_greet + jnp.where(wts_sends(t, slot), 1, 0)
    pl.semaphore_wait(barrier, n_greet)

    def remote(src, dst, send, recv, device):
        return pltpu.make_async_remote_copy(
            src_ref=src, dst_ref=dst, send_sem=send, recv_sem=recv, device_id=device, device_id_type=MESH
        )

    cov_copies = [
        remote(cov.at[0], cov.at[r], cov_send.at[r], cov_recv.at[r], cov_peers[r - 1]) for r in range(1, near_offs)
    ]
    for copy in cov_copies:
        copy.start()

    live_copies = [
        remote(own_live, live.at[k], live_send.at[k], live_recv.at[k], wts_target(0, k)) for k in live_slots
    ]

    def each_live(act):
        valid = wts_receives if act == "wait_recv" else wts_sends
        for k, copy in zip(live_slots, live_copies):
            pl.when(valid(0, k))(getattr(copy, act))

    each_live("start")
    live[own_slot] = own_live[...]

    @pl.when(off == 0)
    def _():
        live[self_step] = own_live[...]

    spans = {-1: (pl.ds(0, TOP), pl.ds(TOP + rows, TOP)), 1: (pl.ds(rows - TOP, TOP), pl.ds(0, TOP))}
    strips = {
        -1: (pl.ds(0, LANE), pl.ds(cols, LANE)),
        1: (pl.ds(cols - LANE, LANE), pl.ds(cols + LANE, LANE)),
        0: (pl.ds(0, cols), pl.ds(0, cols)),
    }
    halo_copies = []
    for k, (a, b) in enumerate(halo_moves):
        if a == 0:
            side = 0 if b < 0 else 1
            ends = strips_out.at[side], strips_in.at[side]
        else:
            ends = counts_ref.at[spans[a][0], strips[b][0]], cells.at[spans[a][1], strips[b][1]]
        halo_copies.append(remote(*ends, halo_send.at[k], halo_recv.at[k], (at_pos(a), at_off(b))))

    def sends(b):
        return off > 0 if b < 0 else off < n_off - 1

    def each_halo(copies, act):
        for (a, b), copy in copies:
            if b == 0:
                getattr(copy, act)()
            elif act == "wait_recv":
                pl.when(sends(-b))(copy.wait_recv)
            else:
                pl.when(sends(b))(getattr(copy, act))

    halos = list(zip(halo_moves, halo_copies))
    each_halo(halos[2:], "start")

    spare = LANE // 3
    lane_t = lax.broadcasted_iota(jnp.int32, (third, LANE), 1)
    for side in (0, 1):
        packed = None
        for k in range(3):
            low = TOP + k * third
            high = min(low + third, TOP + rows)
            piece = cells[low:high, 0:LANE] if side == 0 else cells[low:high, cols - LANE : cols]
            if high - low < third:
                piece = jnp.concatenate([piece, jnp.zeros((third - high + low, LANE), jnp.float32)], axis=0)
            if side == 0:
                piece = pltpu.roll(piece, k * spare, 1) if k else piece
                here = (lane_t >= k * spare) & (lane_t < (k + 1) * spare)
            else:
                piece = pltpu.roll(piece, LANE - k * spare, 1) if k else piece
                here = (lane_t < LANE - k * spare) & (lane_t >= LANE - (k + 1) * spare)
            packed = jnp.where(here, piece, 0.0 if packed is None else packed)
        strips_out[side] = packed

    each_halo(halos[:2], "start")

    for copy in cov_copies:
        copy.wait_recv()
    coverage = cov[0]
    for r in range(1, near_offs):
        coverage = coverage + cov[r]
    own[...] = coverage

    wts_copies = [
        remote(own, wts.at[t, slot], wts_send.at[t, slot], wts_recv.at[t, slot], wts_target(t, slot))
        for t, slot in moves
    ]

    def each_wts(act, side):
        valid = wts_receives if act == "wait_recv" else wts_sends
        for (t, slot), copy in zip(moves, wts_copies):
            if side != (slot > own_slot):
                continue
            if slot == own_slot:
                getattr(copy, act)()
            else:
                pl.when(valid(t, slot))(getattr(copy, act))

    each_wts("start", False)
    wts[0, own_slot] = own[...]

    @pl.when(off == 0)
    def _():
        wts[0, self_step] = own[...]

    def down(vector):
        return jnp.broadcast_to(vector, (LANE, LANE)).T

    phases = LANE // 8

    def spread(source):
        pieces = []
        for k, d in enumerate(steps):
            block = pos + first + d
            inside = (block >= 0) & (block < n_pos)
            for h in range(row_halves):
                pieces.append(jnp.where(inside, source[k, h : h + 1, :], 0.0))
        line = jnp.concatenate(pieces, axis=1)
        reach = line.shape[1]
        line = jnp.broadcast_to(line, (8, reach))
        line = pltpu.roll(line, reach - 7, 1, stride=1, stride_axis=0)
        flip = 7 - lax.broadcasted_iota(jnp.int32, (8, reach), 0)
        line = jnp.take_along_axis(line, flip, axis=0)
        for h in range(phases):
            tables[h] = line if h == 0 else pltpu.roll(line, reach - 8 * h, 1)

    lane_8 = lax.broadcasted_iota(jnp.int32, (8, LANE), 1)
    low_lanes = lane_8 < SIDE

    def column(g, b):
        place = 8 * g + rows - TOP
        h, shift = (place % LANE) // 8, place // LANE * LANE
        if b < blocks:
            return tables[h, :, shift + b * LANE : shift + (b + 1) * LANE]
        after = tables[h, :, shift + cols : shift + cols + LANE]
        return jnp.where(low_lanes, after, tables[h, :, shift - LANE : shift])

    own_groups = range(TOP // 8, (TOP + rows) // 8)

    def column_sums(to, terms_of):
        sums = [None] * (blocks + 1)
        for g in own_groups:
            for b, term in enumerate(terms_of(g)):
                sums[b] = term if sums[b] is None else sums[b] + term
        for b, total in enumerate(sums):
            to[0, b : b + 1, :] = jnp.sum(total, axis=0, keepdims=True)

    def share(buffer, send, recv, peers):
        copies = [
            remote(buffer.at[0], buffer.at[r], send.at[r], recv.at[r], peers[r - 1]) for r in range(1, buffer.shape[0])
        ]
        for copy in copies:
            copy.start()
        return copies

    def gather(copies, buffer):
        for copy in copies:
            copy.wait_recv()
        total = buffer[0]
        for r in range(1, buffer.shape[0]):
            total = total + buffer[r]
        return total

    each_live("wait_recv")
    for h in range(row_halves):
        row_w[TOP + h * LANE : TOP + (h + 1) * LANE, :] = down(own_live[h : h + 1, :])
    spread(live)

    def live_terms(g):
        row = row_w[8 * g : 8 * g + 8, :]
        return [row * column(g, b) for b in range(blocks + 1)]

    column_sums(part_live, live_terms)
    part_live_copies = share(part_live, part_live_send, part_live_recv, part_peers)

    def weigh(low, high):
        gathered = wts[0, low:high]
        for t in range(1, far_offs):
            gathered = gathered + wts[t, low:high]
        lines[low:high] = live[low:high] / jnp.sqrt(gathered)

    each_wts("wait_recv", False)
    weigh(0, own_slot + 1)
    for h in range(row_halves):
        row_w[TOP + h * LANE : TOP + (h + 1) * LANE, :] = down(lines[own_slot, h : h + 1, :])
    spread(lines)

    def row_group(g):
        rows_g = slice(8 * g, 8 * g + 8)
        weight = row_w[rows_g, :]
        outs = []
        for b in range(blocks + 1):
            if b < blocks:
                count = cells[rows_g, b * LANE : (b + 1) * LANE]
            else:
                own_row = 8 * g - TOP
                if 0 <= own_row < rows:
                    k, at = own_row // third, own_row % third
                    after, before = strips_in[0, at : at + 8, :], strips_in[1, at : at + 8, :]
                    if k:
                        after = pltpu.roll(after, LANE - k * spare, 1)
                        before = pltpu.roll(before, k * spare, 1)
                else:
                    after, before = cells[rows_g, cols : cols + LANE], cells[rows_g, cols + LANE : cols + 2 * LANE]
                count = jnp.where(low_lanes, after, before)
            value = count * weight * column(g, b)
            normed_ref[rows_g, b * LANE : (b + 1) * LANE] = value
            outs.append(value)
        return outs

    each_halo(halos[:2], "wait_recv")
    column_sums(part, row_group)
    part_copies = share(part, part_send, part_recv, part_peers)

    each_wts("start", True)

    group_live[0] = gather(part_live_copies, part_live)
    group_live_copies = share(group_live, group_live_send, group_live_recv, group_peers)
    group[0] = gather(part_copies, part)
    group_copies = share(group, group_send, group_recv, group_peers)

    each_halo(halos[2:], "wait_recv")
    each_wts("wait_recv", True)
    weigh(own_slot + 1, n_slots)
    for side, h, low, place in ((0, row_halves - 1, LANE - TOP, 0), (1, 0, 0, TOP + rows)):
        block = pos + (1 if side else -1)
        inside = (block >= 0) & (block < n_pos)
        weight = jnp.where(inside, lines[own_slot + 1 + side, h : h + 1, :], 0.0)
        row_w[place : place + TOP, :] = down(weight)[low : low + TOP, :]
    for g in list(range(TOP // 8)) + list(range((TOP + rows) // 8, (2 * TOP + rows) // 8)):
        row_group(g)

    for copy in cov_copies + part_copies + part_live_copies:
        copy.wait_send()
    each_halo(halos, "wait_send")
    each_wts("wait_send", False)
    each_wts("wait_send", True)
    each_live("wait_send")
    pairs = gather(group_live_copies, group_live)
    expected = gather(group_copies, group)
    lane = lax.broadcasted_iota(jnp.int32, expected.shape, 1)
    place = lax.broadcasted_iota(jnp.int32, expected.shape, 0) * LANE + lane
    needed = (place < cols + 2 * W) | (place >= width - 2 * W)
    place = off * cols + jnp.where(place < cols + SIDE, place, place - width)
    factor = pairs / jnp.where(expected > 0, expected, 1.0)
    factor_ref[...] = jnp.where(needed & (place >= 0) & (place < band), factor, 0.0)
    for copy in group_copies + group_live_copies:
        copy.wait_send()


def near(distance, lowest, highest):
    return (distance >= lowest) & (distance <= highest)


def both(mask_a, mask_b):
    return jnp.where(mask_a | mask_b, 1.0, 0.0).astype(jnp.bfloat16)


def halves(values):
    high = values.astype(jnp.bfloat16)
    return high, (values - high.astype(jnp.float32)).astype(jnp.bfloat16)


def window_kernel(normed_ref, factor_ref, donut_ref, lower_ref, donut, lower, sems):
    width = normed_ref.shape[1]
    rows, cols = donut_ref.shape
    blocks = width // LANE

    out_row = lax.broadcasted_iota(jnp.int32, (STEP, 2 * SPAN), 0)
    out_row = (out_row // 8) * 8 + 7 - lax.rem(out_row, 8)
    in_row = lax.broadcasted_iota(jnp.int32, (STEP, 2 * SPAN), 1)
    in_row = jnp.where(in_row < SPAN, in_row, in_row - SPAN)
    a = in_row - TOP - out_row
    down_table = jnp.concatenate(
        [
            both(near(a, P_SIZE + 1, W), near(a, -W, -P_SIZE - 1)),
            both(near(a, 1, P_SIZE), near(a, -P_SIZE, -1)),
            both(near(a, P_SIZE + 1, W), near(a, P_SIZE + 1, W)),
            both(near(a, 1, P_SIZE), near(a, 1, P_SIZE)),
        ],
        axis=0,
    )
    def side_tables(depth, wide, split):
        shape = (depth, wide)
        at = lax.broadcasted_iota(jnp.int32, shape, 0)
        if split:
            at = jnp.where(at < SIDE, at + wide, at - LANE)
        b = at - lax.broadcasted_iota(jnp.int32, shape, 1)
        return [
            both(near(b, 1, W), near(b, -W, -1)),
            both(near(b, P_SIZE + 1, W), near(b, -W, -P_SIZE - 1)),
            both(near(b, -W, -1), near(b, -W, -1)),
            both(near(b, -W, -P_SIZE - 1), near(b, -W, -P_SIZE - 1)),
        ]

    main_t, rim_t = side_tables(2 * LANE, 2 * LANE, False), side_tables(LANE, 2 * LANE, True)
    mid_t, edge_t = side_tables(LANE, LANE, False), side_tables(LANE, LANE, True)
    pair_table, last_table = [], []
    for k in (0, 2):
        pair_table.append(jnp.concatenate([main_t[k]] * 2 + [main_t[k + 1]] * 2 + [rim_t[k]] * 2 + [rim_t[k + 1]] * 2, axis=0))
        last_table.append(jnp.concatenate([mid_t[k], edge_t[k]] * 2 + [mid_t[k + 1], edge_t[k + 1]] * 2, axis=0))
    flip = 7 - lax.broadcasted_iota(jnp.int32, (8, cols), 0)
    cells_donut = (2 * W + 1) ** 2 - (2 * P_SIZE + 1) ** 2 - 4 * (W - P_SIZE)
    cells_lower = W * W - P_SIZE * P_SIZE
    factor = jnp.concatenate([factor_ref[b : b + 1, :] for b in range(blocks)], axis=1)

    copies = []

    def upright(start):
        ratios = normed_ref[start : start + SPAN, :] * factor
        level = pltpu.roll(ratios, 0, 1, stride=1, stride_axis=0)
        stacked = jnp.concatenate(halves(level), axis=0)
        summed = jnp.dot(down_table, stacked, preferred_element_type=jnp.float32)
        return ratios[TOP : TOP + STEP, :cols], summed

    lanes = lax.broadcasted_iota(jnp.int32, (STEP, LANE), 1)

    def sideways(summed, k):
        mains, rims = [], []
        x = summed[k * STEP : (k + 1) * STEP, :]
        pieces = [x[:, b * LANE : (b + 1) * LANE] for b in range(blocks)]
        rim = jnp.concatenate(
            [jnp.where(lanes < SIDE, pieces[(2 * c + 2) % blocks], pieces[(2 * c - 1) % blocks]) for c in range(blocks // 2)],
            axis=0,
        )
        last = jnp.concatenate([pieces[-1], jnp.where(lanes < SIDE, pieces[0], pieces[-2])], axis=1)
        main = jnp.concatenate([x[:, 2 * c * LANE : (2 * c + 2) * LANE] for c in range(blocks // 2)], axis=0)
        return halves(main), halves(rim), halves(last)

    def level_out(start, here, summed):
        for to, out_ref, out, k, cell_count in (
            (0, donut_ref, donut, 0, cells_donut),
            (1, lower_ref, lower, 2, cells_lower),
        ):
            (m0, r0, l0), (m1, r1, l1) = sideways(summed, k), sideways(summed, k + 1)
            tall = jnp.dot(jnp.concatenate(m0 + m1 + r0 + r1, axis=1), pair_table[k // 2], preferred_element_type=jnp.float32)
            end = jnp.dot(jnp.concatenate(l0 + l1, axis=1), last_table[k // 2], preferred_element_type=jnp.float32)
            flat = jnp.concatenate([tall[c * STEP : (c + 1) * STEP, :] for c in range(blocks // 2)] + [end], axis=1)
            for g in range(STEP // 8):
                rows_g = slice(8 * g, 8 * g + 8)
                back = pltpu.roll(flat[rows_g, :], width - TOP - 8 * g - 7, 1, stride=1, stride_axis=0)[:, :cols]
                back = jnp.take_along_axis(back, flip, axis=0)
                out[start + 8 * g : start + 8 * g + 8, :] = here[rows_g, :] / jnp.maximum(back / cell_count, 0.25)
            span = pl.ds(start, STEP)
            copies.append(pltpu.make_async_copy(out.at[span, :], out_ref.at[span, :], sems.at[to, start // STEP]))
            copies[-1].start()

    for start in range(0, rows, STEP):
        level_out(start, *upright(start))
    for copy in copies:
        copy.wait()


def windows(normed, factor):
    rows, cols = normed.shape[0] - 2 * TOP, normed.shape[1] - LANE
    out = jax.ShapeDtypeStruct((rows, cols), jnp.float32)
    return pl.pallas_call(
        window_kernel,
        out_shape=(out, out),
        in_specs=[pl.BlockSpec(memory_space=pltpu.VMEM), pl.BlockSpec(memory_space=pltpu.VMEM)],
        out_specs=(pl.BlockSpec(memory_space=pltpu.HBM), pl.BlockSpec(memory_space=pltpu.HBM)),
        scratch_shapes=[
            pltpu.VMEM((rows, cols), jnp.float32),
            pltpu.VMEM((rows, cols), jnp.float32),
            pltpu.SemaphoreType.DMA((2, rows // STEP)),
        ],
        compiler_params=pltpu.CompilerParams(vmem_limit_bytes=32 * 1024 * 1024),
        name="windows",
    )(normed, factor)


def local(counts, bin_mask):
    rows, cols = counts.shape
    n_pos = lax.axis_size("pos")
    n_off = lax.axis_size("off")
    inner = 8
    outer = n_pos // inner
    near_offs = 4
    far_offs = n_off // near_offs
    width = cols + LANE
    vecs = cols // LANE + 1
    n_slots = cols // rows + 6
    reach = (cols // rows + 3) * rows
    halves_n = rows // LANE
    third = -(-rows // 24) * 8
    dma = pltpu.SemaphoreType.DMA
    f32 = jnp.float32
    normed, factor = pl.pallas_call(
        functools.partial(comm_kernel, (n_pos, n_off)),
        out_shape=(
            pltpu.VMEM((rows + 2 * TOP, width), f32),
            pltpu.VMEM((vecs, LANE), f32),
        ),
        in_specs=[pl.BlockSpec(memory_space=pltpu.HBM), pl.BlockSpec(memory_space=pltpu.HBM)],
        out_specs=(pl.BlockSpec(memory_space=pltpu.VMEM), pl.BlockSpec(memory_space=pltpu.VMEM)),
        scratch_shapes=[
            pltpu.VMEM((rows + 2 * TOP, cols + 2 * LANE), f32),
            pltpu.VMEM((2, third, LANE), f32),
            pltpu.VMEM((2, third, LANE), f32),
            pltpu.VMEM((halves_n, LANE), jnp.int32),
            pltpu.VMEM((halves_n, LANE), f32),
            pltpu.VMEM((n_slots, halves_n, LANE), f32),
            pltpu.VMEM((near_offs, halves_n, LANE), f32),
            pltpu.VMEM((halves_n, LANE), f32),
            pltpu.VMEM((far_offs, n_slots, halves_n, LANE), f32),
            pltpu.VMEM((n_slots, halves_n, LANE), f32),
            pltpu.VMEM((rows + 2 * TOP, LANE), f32),
            pltpu.VMEM((LANE // 8, 8, reach), f32),
            pltpu.VMEM((inner, vecs, LANE), f32),
            pltpu.VMEM((outer, vecs, LANE), f32),
            pltpu.VMEM((inner, vecs, LANE), f32),
            pltpu.VMEM((outer, vecs, LANE), f32),
            dma,
            dma,
            dma((near_offs,)),
            dma((near_offs,)),
            dma((8,)),
            dma((8,)),
            dma((n_slots,)),
            dma((n_slots,)),
            dma((far_offs, n_slots)),
            dma((far_offs, n_slots)),
            dma((inner,)),
            dma((inner,)),
            dma((outer,)),
            dma((outer,)),
            dma((inner,)),
            dma((inner,)),
            dma((outer,)),
            dma((outer,)),
        ],
        compiler_params=pltpu.CompilerParams(
            collective_id=0, has_side_effects=True, vmem_limit_bytes=24 * 1024 * 1024
        ),
        name="comm",
    )(
        pltpu.with_memory_space_constraint(counts, pltpu.HBM),
        pltpu.with_memory_space_constraint(bin_mask.reshape(halves_n, LANE), pltpu.HBM),
    )
    return windows(normed, factor)


def solution(mesh):
    placed = (P("pos", "off"), P("pos"))
    return jax.shard_map(
        local,
        mesh=mesh,
        in_specs=placed,
        out_specs=(P("pos", "off"), P("pos", "off")),
        check_vma=False,
    )
```

```python
import functools

import jax
import jax.numpy as jnp
from jax import lax
from jax.experimental import pallas as pl
from jax.experimental.pallas import tpu as pltpu
from jax.sharding import PartitionSpec as P

W = 20
P_SIZE = 8
TOP = 24
LANE = 128
SIDE = 64
STEP = 64
SPAN = STEP + 2 * TOP
MESH = pl.DeviceIdType.MESH


def comm_kernel(
    sizes, counts_ref, mask_ref, normed_ref, factor_ref,
    cells, strips_out, strips_in, mask, own_live, live, cov, own, wts, lines, row_w, tables, part, group, part_live, group_live,
    load_sem, mask_sem, cov_send, cov_recv, halo_send, halo_recv, live_send, live_recv, wts_send, wts_recv,
    part_send, part_recv, group_send, group_recv, part_live_send, part_live_recv, group_live_send, group_live_recv,
):
    n_pos, n_off = sizes
    rows, cols = counts_ref.shape
    width = cols + LANE
    blocks = cols // LANE
    ratio = cols // rows
    near_offs = cov.shape[0]
    far_offs = n_off // near_offs
    inner = part.shape[0]
    outer = group.shape[0]
    pos = lax.axis_index("pos")
    off = lax.axis_index("off")
    total_bins = rows * n_pos
    band = cols * n_off
    row_halves = rows // LANE
    third = strips_in.shape[1]

    def at_pos(k):
        return lax.rem(pos + (k + n_pos), n_pos)

    def at_off(k):
        return lax.rem(off + (k + n_off), n_off)

    first = ratio * off
    far = off // near_offs
    near = off - far * near_offs
    quot = pos // inner
    rank = pos - quot * inner
    cov_peers = [(pos, far * near_offs + lax.rem(near + r, near_offs)) for r in range(1, near_offs)]
    halo_moves = [(0, -1), (0, 1), (-1, 0), (1, 0), (-1, -1), (-1, 1), (1, -1), (1, 1)]
    steps = list(range(-1, ratio + 2))
    n_steps = len(steps)
    self_step = steps.index(0)
    own_slot = n_steps
    n_slots = n_steps + 3
    part_peers = [(quot * inner + lax.rem(rank + r, inner), off) for r in range(1, inner)]
    group_peers = [(lax.rem(quot + r, outer) * inner + rank, off) for r in range(1, outer)]

    def wts_target(t, slot):
        there = lax.rem(far + t, far_offs) * near_offs + near
        if slot < n_steps:
            return (lax.rem(pos - ratio * there - steps[slot] + n_pos, n_pos), there)
        return (at_pos((0, 1, -1)[slot - n_steps]), there)

    def wts_source(t, slot):
        there = lax.rem(far - t + far_offs, far_offs) * near_offs + near
        if slot < n_steps:
            return (lax.rem(pos + first + steps[slot] + n_pos, n_pos), there)
        return (at_pos((0, -1, 1)[slot - n_steps]), there)

    def within(place):
        return (place >= 0) & (place < n_pos)

    def wts_sends(t, slot):
        there = lax.rem(far + t, far_offs) * near_offs + near
        if slot < n_steps:
            valid = within(pos - ratio * there - steps[slot])
            return valid & (off > 0) if t == 0 and slot == self_step else valid
        return within(pos + (0, 1, -1)[slot - n_steps])

    def wts_receives(t, slot):
        if slot < n_steps:
            valid = within(pos + first + steps[slot])
            return valid & (off > 0) if t == 0 and slot == self_step else valid
        return within(pos + (0, -1, 1)[slot - n_steps])

    moves = []
    for t in list(range(1, far_offs)) + [0]:
        for slot in range(n_slots):
            if t or slot != own_slot:
                moves.append((t, slot))
    live_slots = [slot for slot in range(n_slots) if slot != own_slot]

    load = pltpu.make_async_copy(counts_ref, cells.at[pl.ds(TOP, rows), pl.ds(0, cols)], load_sem)
    load.start()
    load_mask = pltpu.make_async_copy(mask_ref, mask, mask_sem)
    load_mask.start()

    def sends(b):
        return off > 0 if b < 0 else off < n_off - 1

    barrier = pltpu.get_barrier_semaphore()

    def greet(device):
        pl.semaphore_signal(barrier, inc=1, device_id=device, device_id_type=MESH)

    for t, slot in moves:
        if slot == own_slot:
            greet(wts_source(t, slot))
        else:
            pl.when(wts_receives(t, slot))(functools.partial(greet, wts_source(t, slot)))
    for device in cov_peers:
        greet(device)
    for a, b in halo_moves:
        source = (at_pos(-a), at_off(-b))
        if b == 0:
            greet(source)
        else:
            pl.when(sends(-b))(functools.partial(greet, source))
    for device in part_peers + group_peers:
        greet(device)

    @pl.when(off == 0)
    def _():
        strips_in[1] = jnp.zeros(strips_in.shape[1:], jnp.float32)
        for place in (0, TOP + rows):
            cells[place : place + TOP, cols + LANE :] = jnp.zeros((TOP, LANE), jnp.float32)

    @pl.when(off == n_off - 1)
    def _():
        strips_in[0] = jnp.zeros(strips_in.shape[1:], jnp.float32)
        for place in (0, TOP + rows):
            cells[place : place + TOP, cols : cols + LANE] = jnp.zeros((TOP, LANE), jnp.float32)

    load.wait()

    base = pos * rows + off * cols
    acc = None
    for b in range(blocks):
        row_i = lax.broadcasted_iota(jnp.int32, (rows, LANE), 0)
        col_i = lax.broadcasted_iota(jnp.int32, (rows, LANE), 1)
        piece = cells[TOP : TOP + rows, b * LANE : (b + 1) * LANE]
        piece = jnp.where(row_i + col_i < total_bins - base - b * LANE, piece, 0.0)
        acc = piece if acc is None else acc + piece
    for h in range(row_halves):
        turned = acc[h * LANE : (h + 1) * LANE, :].T
        cov[0, h : h + 1, :] = jnp.sum(turned, axis=0, keepdims=True)
    load_mask.wait()
    own_live[...] = mask[...].astype(jnp.float32)

    n_greet = len(cov_peers) + len(part_peers) + len(group_peers)
    for _, b in halo_moves:
        n_greet = n_greet + (jnp.where(sends(b), 1, 0) if b else 1)
    for t, slot in moves:
        n_greet = n_greet + jnp.where(wts_sends(t, slot), 1, 0)
    pl.semaphore_wait(barrier, n_greet)

    def remote(src, dst, send, recv, device):
        return pltpu.make_async_remote_copy(
            src_ref=src, dst_ref=dst, send_sem=send, recv_sem=recv, device_id=device, device_id_type=MESH
        )

    cov_copies = [
        remote(cov.at[0], cov.at[r], cov_send.at[r], cov_recv.at[r], cov_peers[r - 1]) for r in range(1, near_offs)
    ]
    for copy in cov_copies:
        copy.start()

    live_copies = [
        remote(own_live, live.at[k], live_send.at[k], live_recv.at[k], wts_target(0, k)) for k in live_slots
    ]

    def each_live(act):
        valid = wts_receives if act == "wait_recv" else wts_sends
        for k, copy in zip(live_slots, live_copies):
            pl.when(valid(0, k))(getattr(copy, act))

    each_live("start")
    live[own_slot] = own_live[...]

    @pl.when(off == 0)
    def _():
        live[self_step] = own_live[...]

    spans = {-1: (pl.ds(0, TOP), pl.ds(TOP + rows, TOP)), 1: (pl.ds(rows - TOP, TOP), pl.ds(0, TOP))}
    strips = {
        -1: (pl.ds(0, LANE), pl.ds(cols, LANE)),
        1: (pl.ds(cols - LANE, LANE), pl.ds(cols + LANE, LANE)),
        0: (pl.ds(0, cols), pl.ds(0, cols)),
    }
    halo_copies = []
    for k, (a, b) in enumerate(halo_moves):
        if a == 0:
            side = 0 if b < 0 else 1
            ends = strips_out.at[side], strips_in.at[side]
        else:
            ends = counts_ref.at[spans[a][0], strips[b][0]], cells.at[spans[a][1], strips[b][1]]
        halo_copies.append(remote(*ends, halo_send.at[k], halo_recv.at[k], (at_pos(a), at_off(b))))

    def each_halo(copies, act):
        for (a, b), copy in copies:
            if b == 0:
                getattr(copy, act)()
            elif act == "wait_recv":
                pl.when(sends(-b))(copy.wait_recv)
            else:
                pl.when(sends(b))(getattr(copy, act))

    halos = list(zip(halo_moves, halo_copies))
    each_halo(halos[2:], "start")

    spare = LANE // 3
    lane_t = lax.broadcasted_iota(jnp.int32, (third, LANE), 1)
    for side in (0, 1):
        packed = None
        for k in range(3):
            low = TOP + k * third
            high = min(low + third, TOP + rows)
            piece = cells[low:high, 0:LANE] if side == 0 else cells[low:high, cols - LANE : cols]
            if high - low < third:
                piece = jnp.concatenate([piece, jnp.zeros((third - high + low, LANE), jnp.float32)], axis=0)
            if side == 0:
                piece = pltpu.roll(piece, k * spare, 1) if k else piece
                here = (lane_t >= k * spare) & (lane_t < (k + 1) * spare)
            else:
                piece = pltpu.roll(piece, LANE - k * spare, 1) if k else piece
                here = (lane_t < LANE - k * spare) & (lane_t >= LANE - (k + 1) * spare)
            packed = jnp.where(here, piece, 0.0 if packed is None else packed)
        strips_out[side] = packed

    each_halo(halos[:2], "start")

    for copy in cov_copies:
        copy.wait_recv()
    coverage = cov[0]
    for r in range(1, near_offs):
        coverage = coverage + cov[r]
    own[...] = coverage

    wts_copies = [
        remote(own, wts.at[t, slot], wts_send.at[t, slot], wts_recv.at[t, slot], wts_target(t, slot))
        for t, slot in moves
    ]

    def each_wts(act, side):
        valid = wts_receives if act == "wait_recv" else wts_sends
        for (t, slot), copy in zip(moves, wts_copies):
            if side != (slot > own_slot):
                continue
            if slot == own_slot:
                getattr(copy, act)()
            else:
                pl.when(valid(t, slot))(getattr(copy, act))

    each_wts("start", False)
    wts[0, own_slot] = own[...]

    @pl.when(off == 0)
    def _():
        wts[0, self_step] = own[...]

    def down(vector):
        return jnp.broadcast_to(vector, (LANE, LANE)).T

    phases = LANE // 8

    def spread(source):
        pieces = []
        for k, d in enumerate(steps):
            block = pos + first + d
            inside = (block >= 0) & (block < n_pos)
            for h in range(row_halves):
                pieces.append(jnp.where(inside, source[k, h : h + 1, :], 0.0))
        line = jnp.concatenate(pieces, axis=1)
        reach = line.shape[1]
        line = jnp.broadcast_to(line, (8, reach))
        line = pltpu.roll(line, reach - 7, 1, stride=1, stride_axis=0)
        flip = 7 - lax.broadcasted_iota(jnp.int32, (8, reach), 0)
        line = jnp.take_along_axis(line, flip, axis=0)
        for h in range(phases):
            tables[h] = line if h == 0 else pltpu.roll(line, reach - 8 * h, 1)

    lane_8 = lax.broadcasted_iota(jnp.int32, (8, LANE), 1)
    low_lanes = lane_8 < SIDE

    def column(g, b):
        place = 8 * g + rows - TOP
        h, shift = (place % LANE) // 8, place // LANE * LANE
        if b < blocks:
            return tables[h, :, shift + b * LANE : shift + (b + 1) * LANE]
        after = tables[h, :, shift + cols : shift + cols + LANE]
        return jnp.where(low_lanes, after, tables[h, :, shift - LANE : shift])

    own_groups = range(TOP // 8, (TOP + rows) // 8)

    def column_sums(to, terms_of):
        sums = [None] * (blocks + 1)
        for g in own_groups:
            for b, term in enumerate(terms_of(g)):
                sums[b] = term if sums[b] is None else sums[b] + term
        for b, total in enumerate(sums):
            to[0, b : b + 1, :] = jnp.sum(total, axis=0, keepdims=True)

    def share(buffer, send, recv, peers):
        copies = [
            remote(buffer.at[0], buffer.at[r], send.at[r], recv.at[r], peers[r - 1]) for r in range(1, buffer.shape[0])
        ]
        for copy in copies:
            copy.start()
        return copies

    def gather(copies, buffer):
        for copy in copies:
            copy.wait_recv()
        total = buffer[0]
        for r in range(1, buffer.shape[0]):
            total = total + buffer[r]
        return total

    each_live("wait_recv")
    for h in range(row_halves):
        row_w[TOP + h * LANE : TOP + (h + 1) * LANE, :] = down(own_live[h : h + 1, :])
    spread(live)

    def live_terms(g):
        row = row_w[8 * g : 8 * g + 8, :]
        return [row * column(g, b) for b in range(blocks + 1)]

    column_sums(part_live, live_terms)
    part_live_copies = share(part_live, part_live_send, part_live_recv, part_peers)

    def weigh(low, high):
        gathered = wts[0, low:high]
        for t in range(1, far_offs):
            gathered = gathered + wts[t, low:high]
        lines[low:high] = live[low:high] / jnp.sqrt(gathered)

    each_wts("wait_recv", False)
    weigh(0, own_slot + 1)
    for h in range(row_halves):
        row_w[TOP + h * LANE : TOP + (h + 1) * LANE, :] = down(lines[own_slot, h : h + 1, :])
    spread(lines)

    def row_group(g):
        rows_g = slice(8 * g, 8 * g + 8)
        weight = row_w[rows_g, :]
        outs = []
        for b in range(blocks + 1):
            if b < blocks:
                count = cells[rows_g, b * LANE : (b + 1) * LANE]
            else:
                own_row = 8 * g - TOP
                if 0 <= own_row < rows:
                    k, at = own_row // third, own_row % third
                    after, before = strips_in[0, at : at + 8, :], strips_in[1, at : at + 8, :]
                    if k:
                        after = pltpu.roll(after, LANE - k * spare, 1)
                        before = pltpu.roll(before, k * spare, 1)
                else:
                    after, before = cells[rows_g, cols : cols + LANE], cells[rows_g, cols + LANE : cols + 2 * LANE]
                count = jnp.where(low_lanes, after, before)
            value = count * weight * column(g, b)
            normed_ref[rows_g, b * LANE : (b + 1) * LANE] = value
            outs.append(value)
        return outs

    each_halo(halos[:2], "wait_recv")
    column_sums(part, row_group)
    part_copies = share(part, part_send, part_recv, part_peers)

    each_wts("start", True)

    group_live[0] = gather(part_live_copies, part_live)
    group_live_copies = share(group_live, group_live_send, group_live_recv, group_peers)
    group[0] = gather(part_copies, part)
    group_copies = share(group, group_send, group_recv, group_peers)

    each_halo(halos[2:], "wait_recv")
    each_wts("wait_recv", True)
    weigh(own_slot + 1, n_slots)
    for side, h, low, place in ((0, row_halves - 1, LANE - TOP, 0), (1, 0, 0, TOP + rows)):
        block = pos + (1 if side else -1)
        inside = (block >= 0) & (block < n_pos)
        weight = jnp.where(inside, lines[own_slot + 1 + side, h : h + 1, :], 0.0)
        row_w[place : place + TOP, :] = down(weight)[low : low + TOP, :]
    for g in list(range(TOP // 8)) + list(range((TOP + rows) // 8, (2 * TOP + rows) // 8)):
        row_group(g)

    for copy in cov_copies + part_copies + part_live_copies:
        copy.wait_send()
    each_halo(halos, "wait_send")
    each_wts("wait_send", False)
    each_wts("wait_send", True)
    each_live("wait_send")
    pairs = gather(group_live_copies, group_live)
    expected = gather(group_copies, group)
    lane = lax.broadcasted_iota(jnp.int32, expected.shape, 1)
    place = lax.broadcasted_iota(jnp.int32, expected.shape, 0) * LANE + lane
    needed = (place < cols + 2 * W) | (place >= width - 2 * W)
    place = off * cols + jnp.where(place < cols + SIDE, place, place - width)
    factor = pairs / jnp.where(expected > 0, expected, 1.0)
    factor_ref[...] = jnp.where(needed & (place >= 0) & (place < band), factor, 0.0)
    for copy in group_copies + group_live_copies:
        copy.wait_send()


def near(distance, lowest, highest):
    return (distance >= lowest) & (distance <= highest)


def both(mask_a, mask_b):
    return jnp.where(mask_a | mask_b, 1.0, 0.0).astype(jnp.bfloat16)


def halves(values):
    high = values.astype(jnp.bfloat16)
    return high, (values - high.astype(jnp.float32)).astype(jnp.bfloat16)


def window_kernel(normed_ref, factor_ref, donut_ref, lower_ref, donut, lower, sems):
    width = normed_ref.shape[1]
    rows, cols = donut_ref.shape
    blocks = width // LANE

    out_row = lax.broadcasted_iota(jnp.int32, (STEP, 2 * SPAN), 0)
    out_row = (out_row // 8) * 8 + 7 - lax.rem(out_row, 8)
    in_row = lax.broadcasted_iota(jnp.int32, (STEP, 2 * SPAN), 1)
    in_row = jnp.where(in_row < SPAN, in_row, in_row - SPAN)
    a = in_row - TOP - out_row
    down_table = jnp.concatenate(
        [
            both(near(a, P_SIZE + 1, W), near(a, -W, -P_SIZE - 1)),
            both(near(a, 1, P_SIZE), near(a, -P_SIZE, -1)),
            both(near(a, P_SIZE + 1, W), near(a, P_SIZE + 1, W)),
            both(near(a, 1, P_SIZE), near(a, 1, P_SIZE)),
        ],
        axis=0,
    )
    def side_tables(depth, wide, split):
        shape = (depth, wide)
        at = lax.broadcasted_iota(jnp.int32, shape, 0)
        if split:
            at = jnp.where(at < SIDE, at + wide, at - LANE)
        b = at - lax.broadcasted_iota(jnp.int32, shape, 1)
        return [
            both(near(b, 1, W), near(b, -W, -1)),
            both(near(b, P_SIZE + 1, W), near(b, -W, -P_SIZE - 1)),
            both(near(b, -W, -1), near(b, -W, -1)),
            both(near(b, -W, -P_SIZE - 1), near(b, -W, -P_SIZE - 1)),
        ]

    main_t, rim_t = side_tables(2 * LANE, 2 * LANE, False), side_tables(LANE, 2 * LANE, True)
    mid_t, edge_t = side_tables(LANE, LANE, False), side_tables(LANE, LANE, True)
    pair_table, last_table = [], []
    for k in (0, 2):
        pair_table.append(jnp.concatenate([main_t[k]] * 2 + [main_t[k + 1]] * 2 + [rim_t[k]] * 2 + [rim_t[k + 1]] * 2, axis=0))
        last_table.append(jnp.concatenate([mid_t[k], edge_t[k]] * 2 + [mid_t[k + 1], edge_t[k + 1]] * 2, axis=0))
    flip = 7 - lax.broadcasted_iota(jnp.int32, (8, cols), 0)
    cells_donut = (2 * W + 1) ** 2 - (2 * P_SIZE + 1) ** 2 - 4 * (W - P_SIZE)
    cells_lower = W * W - P_SIZE * P_SIZE
    factor = jnp.concatenate([factor_ref[b : b + 1, :] for b in range(blocks)], axis=1)

    copies = []

    def upright(start):
        ratios = normed_ref[start : start + SPAN, :] * factor
        level = pltpu.roll(ratios, 0, 1, stride=1, stride_axis=0)
        stacked = jnp.concatenate(halves(level), axis=0)
        summed = jnp.dot(down_table, stacked, preferred_element_type=jnp.float32)
        return ratios[TOP : TOP + STEP, :cols], summed

    lanes = lax.broadcasted_iota(jnp.int32, (STEP, LANE), 1)

    def sideways(summed, k):
        mains, rims = [], []
        x = summed[k * STEP : (k + 1) * STEP, :]
        pieces = [x[:, b * LANE : (b + 1) * LANE] for b in range(blocks)]
        rim = jnp.concatenate(
            [jnp.where(lanes < SIDE, pieces[(2 * c + 2) % blocks], pieces[(2 * c - 1) % blocks]) for c in range(blocks // 2)],
            axis=0,
        )
        last = jnp.concatenate([pieces[-1], jnp.where(lanes < SIDE, pieces[0], pieces[-2])], axis=1)
        main = jnp.concatenate([x[:, 2 * c * LANE : (2 * c + 2) * LANE] for c in range(blocks // 2)], axis=0)
        return halves(main), halves(rim), halves(last)

    def level_out(start, here, summed):
        for to, out_ref, out, k, cell_count in (
            (0, donut_ref, donut, 0, cells_donut),
            (1, lower_ref, lower, 2, cells_lower),
        ):
            (m0, r0, l0), (m1, r1, l1) = sideways(summed, k), sideways(summed, k + 1)
            tall = jnp.dot(jnp.concatenate(m0 + m1 + r0 + r1, axis=1), pair_table[k // 2], preferred_element_type=jnp.float32)
            end = jnp.dot(jnp.concatenate(l0 + l1, axis=1), last_table[k // 2], preferred_element_type=jnp.float32)
            flat = jnp.concatenate([tall[c * STEP : (c + 1) * STEP, :] for c in range(blocks // 2)] + [end], axis=1)
            for g in range(STEP // 8):
                rows_g = slice(8 * g, 8 * g + 8)
                back = pltpu.roll(flat[rows_g, :], width - TOP - 8 * g - 7, 1, stride=1, stride_axis=0)[:, :cols]
                back = jnp.take_along_axis(back, flip, axis=0)
                out[start + 8 * g : start + 8 * g + 8, :] = here[rows_g, :] / jnp.maximum(back / cell_count, 0.25)
            span = pl.ds(start, STEP)
            copies.append(pltpu.make_async_copy(out.at[span, :], out_ref.at[span, :], sems.at[to, start // STEP]))
            copies[-1].start()

    for start in range(0, rows, STEP):
        level_out(start, *upright(start))
    for copy in copies:
        copy.wait()


def windows(normed, factor):
    rows, cols = normed.shape[0] - 2 * TOP, normed.shape[1] - LANE
    out = jax.ShapeDtypeStruct((rows, cols), jnp.float32)
    return pl.pallas_call(
        window_kernel,
        out_shape=(out, out),
        in_specs=[pl.BlockSpec(memory_space=pltpu.VMEM), pl.BlockSpec(memory_space=pltpu.VMEM)],
        out_specs=(pl.BlockSpec(memory_space=pltpu.HBM), pl.BlockSpec(memory_space=pltpu.HBM)),
        scratch_shapes=[
            pltpu.VMEM((rows, cols), jnp.float32),
            pltpu.VMEM((rows, cols), jnp.float32),
            pltpu.SemaphoreType.DMA((2, rows // STEP)),
        ],
        compiler_params=pltpu.CompilerParams(vmem_limit_bytes=32 * 1024 * 1024),
        name="windows",
    )(normed, factor)


def local(counts, bin_mask):
    rows, cols = counts.shape
    n_pos = lax.axis_size("pos")
    n_off = lax.axis_size("off")
    inner = 8
    outer = n_pos // inner
    near_offs = 4
    far_offs = n_off // near_offs
    width = cols + LANE
    vecs = cols // LANE + 1
    n_slots = cols // rows + 6
    reach = (cols // rows + 3) * rows
    halves_n = rows // LANE
    third = -(-rows // 24) * 8
    dma = pltpu.SemaphoreType.DMA
    f32 = jnp.float32
    normed, factor = pl.pallas_call(
        functools.partial(comm_kernel, (n_pos, n_off)),
        out_shape=(
            pltpu.VMEM((rows + 2 * TOP, width), f32),
            pltpu.VMEM((vecs, LANE), f32),
        ),
        in_specs=[pl.BlockSpec(memory_space=pltpu.HBM), pl.BlockSpec(memory_space=pltpu.HBM)],
        out_specs=(pl.BlockSpec(memory_space=pltpu.VMEM), pl.BlockSpec(memory_space=pltpu.VMEM)),
        scratch_shapes=[
            pltpu.VMEM((rows + 2 * TOP, cols + 2 * LANE), f32),
            pltpu.VMEM((2, third, LANE), f32),
            pltpu.VMEM((2, third, LANE), f32),
            pltpu.VMEM((halves_n, LANE), jnp.int32),
            pltpu.VMEM((halves_n, LANE), f32),
            pltpu.VMEM((n_slots, halves_n, LANE), f32),
            pltpu.VMEM((near_offs, halves_n, LANE), f32),
            pltpu.VMEM((halves_n, LANE), f32),
            pltpu.VMEM((far_offs, n_slots, halves_n, LANE), f32),
            pltpu.VMEM((n_slots, halves_n, LANE), f32),
            pltpu.VMEM((rows + 2 * TOP, LANE), f32),
            pltpu.VMEM((LANE // 8, 8, reach), f32),
            pltpu.VMEM((inner, vecs, LANE), f32),
            pltpu.VMEM((outer, vecs, LANE), f32),
            pltpu.VMEM((inner, vecs, LANE), f32),
            pltpu.VMEM((outer, vecs, LANE), f32),
            dma,
            dma,
            dma((near_offs,)),
            dma((near_offs,)),
            dma((8,)),
            dma((8,)),
            dma((n_slots,)),
            dma((n_slots,)),
            dma((far_offs, n_slots)),
            dma((far_offs, n_slots)),
            dma((inner,)),
            dma((inner,)),
            dma((outer,)),
            dma((outer,)),
            dma((inner,)),
            dma((inner,)),
            dma((outer,)),
            dma((outer,)),
        ],
        compiler_params=pltpu.CompilerParams(
            collective_id=0, has_side_effects=True, vmem_limit_bytes=24 * 1024 * 1024
        ),
        name="comm",
    )(
        pltpu.with_memory_space_constraint(counts, pltpu.HBM),
        pltpu.with_memory_space_constraint(bin_mask.reshape(halves_n, LANE), pltpu.HBM),
    )
    return windows(normed, factor)


def solution(mesh):
    placed = (P("pos", "off"), P("pos"))
    return jax.shard_map(
        local,
        mesh=mesh,
        in_specs=placed,
        out_specs=(P("pos", "off"), P("pos", "off")),
        check_vma=False,
    )
```

```python
import functools

import jax
import jax.numpy as jnp
from jax import lax
from jax.experimental import pallas as pl
from jax.experimental.pallas import tpu as pltpu
from jax.sharding import PartitionSpec as P

W = 20
P_SIZE = 8
TOP = 24
LANE = 128
SIDE = 64
STEP = 64
SPAN = STEP + 2 * TOP
MESH = pl.DeviceIdType.MESH


def comm_kernel(
    sizes, counts_ref, mask_ref, normed_ref, factor_ref,
    cells, strips_out, strips_in, mask, own_live, live, cov, own, wts, lines, row_w, tables, part, group, part_live, group_live,
    load_sem, mask_sem, cov_send, cov_recv, halo_send, halo_recv, live_send, live_recv, wts_send, wts_recv,
    part_send, part_recv, group_send, group_recv, part_live_send, part_live_recv, group_live_send, group_live_recv,
):
    n_pos, n_off = sizes
    rows, cols = counts_ref.shape
    width = cols + LANE
    blocks = cols // LANE
    ratio = cols // rows
    near_offs = cov.shape[0]
    far_offs = n_off // near_offs
    inner = part.shape[0]
    outer = group.shape[0]
    pos = lax.axis_index("pos")
    off = lax.axis_index("off")
    total_bins = rows * n_pos
    band = cols * n_off
    row_halves = rows // LANE
    third = strips_in.shape[1]

    def at_pos(k):
        return lax.rem(pos + (k + n_pos), n_pos)

    def at_off(k):
        return lax.rem(off + (k + n_off), n_off)

    first = ratio * off
    far = off // near_offs
    near = off - far * near_offs
    quot = pos // inner
    rank = pos - quot * inner
    cov_peers = [(pos, far * near_offs + lax.rem(near + r, near_offs)) for r in range(1, near_offs)]
    halo_moves = [(0, -1), (0, 1), (-1, 0), (1, 0), (-1, -1), (-1, 1), (1, -1), (1, 1)]
    steps = list(range(-1, ratio + 2))
    n_steps = len(steps)
    self_step = steps.index(0)
    own_slot = n_steps
    n_slots = n_steps + 3
    part_peers = [(quot * inner + lax.rem(rank + r, inner), off) for r in range(1, inner)]
    group_peers = [(lax.rem(quot + r, outer) * inner + rank, off) for r in range(1, outer)]

    def wts_target(t, slot):
        there = lax.rem(far + t, far_offs) * near_offs + near
        if slot < n_steps:
            return (lax.rem(pos - ratio * there - steps[slot] + n_pos, n_pos), there)
        return (at_pos((0, 1, -1)[slot - n_steps]), there)

    def wts_source(t, slot):
        there = lax.rem(far - t + far_offs, far_offs) * near_offs + near
        if slot < n_steps:
            return (lax.rem(pos + first + steps[slot] + n_pos, n_pos), there)
        return (at_pos((0, -1, 1)[slot - n_steps]), there)

    meets = pos + first + steps[0] < n_pos

    def within(place):
        return (place >= 0) & (place < n_pos)

    def wts_sends(t, slot):
        there = lax.rem(far + t, far_offs) * near_offs + near
        if slot < n_steps:
            valid = within(pos - ratio * there - steps[slot])
            return valid & (off > 0) if t == 0 and slot == self_step else valid
        to = pos + (0, 1, -1)[slot - n_steps]
        return within(to) & (to + ratio * there + steps[0] < n_pos)

    def wts_receives(t, slot):
        if slot < n_steps:
            valid = within(pos + first + steps[slot])
            return valid & (off > 0) if t == 0 and slot == self_step else valid
        return within(pos + (0, -1, 1)[slot - n_steps]) & meets

    moves = []
    for t in list(range(1, far_offs)) + [0]:
        for slot in range(n_slots):
            if t or slot != own_slot:
                moves.append((t, slot))
    live_slots = [slot for slot in range(n_slots) if slot != own_slot]

    load = pltpu.make_async_copy(counts_ref, cells.at[pl.ds(TOP, rows), pl.ds(0, cols)], load_sem)
    load.start()
    load_mask = pltpu.make_async_copy(mask_ref, mask, mask_sem)
    load_mask.start()

    def sends(b):
        return off > 0 if b < 0 else off < n_off - 1

    barrier = pltpu.get_barrier_semaphore()

    def greet(device):
        pl.semaphore_signal(barrier, inc=1, device_id=device, device_id_type=MESH)

    for t, slot in moves:
        pl.when(wts_receives(t, slot))(functools.partial(greet, wts_source(t, slot)))
    for device in cov_peers:
        greet(device)
    for a, b in halo_moves:
        source = (at_pos(-a), at_off(-b))
        if b == 0:
            greet(source)
        else:
            pl.when(sends(-b))(functools.partial(greet, source))
    for device in part_peers + group_peers:
        greet(device)

    @pl.when(off == 0)
    def _():
        strips_in[1] = jnp.zeros(strips_in.shape[1:], jnp.float32)
        for place in (0, TOP + rows):
            cells[place : place + TOP, cols + LANE :] = jnp.zeros((TOP, LANE), jnp.float32)

    @pl.when(off == n_off - 1)
    def _():
        strips_in[0] = jnp.zeros(strips_in.shape[1:], jnp.float32)
        for place in (0, TOP + rows):
            cells[place : place + TOP, cols : cols + LANE] = jnp.zeros((TOP, LANE), jnp.float32)

    load.wait()

    base = pos * rows + off * cols
    acc = None
    for b in range(blocks):
        row_i = lax.broadcasted_iota(jnp.int32, (rows, LANE), 0)
        col_i = lax.broadcasted_iota(jnp.int32, (rows, LANE), 1)
        piece = cells[TOP : TOP + rows, b * LANE : (b + 1) * LANE]
        piece = jnp.where(row_i + col_i < total_bins - base - b * LANE, piece, 0.0)
        acc = piece if acc is None else acc + piece
    for h in range(row_halves):
        turned = acc[h * LANE : (h + 1) * LANE, :].T
        cov[0, h : h + 1, :] = jnp.sum(turned, axis=0, keepdims=True)
    load_mask.wait()
    own_live[...] = mask[...].astype(jnp.float32)

    n_greet = len(cov_peers) + len(part_peers) + len(group_peers)
    for _, b in halo_moves:
        n_greet = n_greet + (jnp.where(sends(b), 1, 0) if b else 1)
    for t, slot in moves:
        n_greet = n_greet + jnp.where(wts_sends(t, slot), 1, 0)
    pl.semaphore_wait(barrier, n_greet)

    def remote(src, dst, send, recv, device):
        return pltpu.make_async_remote_copy(
            src_ref=src, dst_ref=dst, send_sem=send, recv_sem=recv, device_id=device, device_id_type=MESH
        )

    cov_copies = [
        remote(cov.at[0], cov.at[r], cov_send.at[r], cov_recv.at[r], cov_peers[r - 1]) for r in range(1, near_offs)
    ]
    for copy in cov_copies:
        copy.start()

    live_copies = [
        remote(own_live, live.at[k], live_send.at[k], live_recv.at[k], wts_target(0, k)) for k in live_slots
    ]

    def each_live(act):
        valid = wts_receives if act == "wait_recv" else wts_sends
        for k, copy in zip(live_slots, live_copies):
            pl.when(valid(0, k))(getattr(copy, act))

    each_live("start")
    live[own_slot] = own_live[...]

    @pl.when(off == 0)
    def _():
        live[self_step] = own_live[...]

    spans = {-1: (pl.ds(0, TOP), pl.ds(TOP + rows, TOP)), 1: (pl.ds(rows - TOP, TOP), pl.ds(0, TOP))}
    strips = {
        -1: (pl.ds(0, LANE), pl.ds(cols, LANE)),
        1: (pl.ds(cols - LANE, LANE), pl.ds(cols + LANE, LANE)),
        0: (pl.ds(0, cols), pl.ds(0, cols)),
    }
    halo_copies = []
    for k, (a, b) in enumerate(halo_moves):
        if a == 0:
            side = 0 if b < 0 else 1
            ends = strips_out.at[side], strips_in.at[side]
        else:
            ends = counts_ref.at[spans[a][0], strips[b][0]], cells.at[spans[a][1], strips[b][1]]
        halo_copies.append(remote(*ends, halo_send.at[k], halo_recv.at[k], (at_pos(a), at_off(b))))

    def each_halo(copies, act):
        for (a, b), copy in copies:
            if b == 0:
                getattr(copy, act)()
            elif act == "wait_recv":
                pl.when(sends(-b))(copy.wait_recv)
            else:
                pl.when(sends(b))(getattr(copy, act))

    halos = list(zip(halo_moves, halo_copies))
    each_halo(halos[2:], "start")

    spare = LANE // 3
    lane_t = lax.broadcasted_iota(jnp.int32, (third, LANE), 1)
    for side in (0, 1):
        packed = None
        for k in range(3):
            low = TOP + k * third
            high = min(low + third, TOP + rows)
            piece = cells[low:high, 0:LANE] if side == 0 else cells[low:high, cols - LANE : cols]
            if high - low < third:
                piece = jnp.concatenate([piece, jnp.zeros((third - high + low, LANE), jnp.float32)], axis=0)
            if side == 0:
                piece = pltpu.roll(piece, k * spare, 1) if k else piece
                here = (lane_t >= k * spare) & (lane_t < (k + 1) * spare)
            else:
                piece = pltpu.roll(piece, LANE - k * spare, 1) if k else piece
                here = (lane_t < LANE - k * spare) & (lane_t >= LANE - (k + 1) * spare)
            packed = jnp.where(here, piece, 0.0 if packed is None else packed)
        strips_out[side] = packed

    each_halo(halos[:2], "start")

    for copy in cov_copies:
        copy.wait_recv()
    coverage = cov[0]
    for r in range(1, near_offs):
        coverage = coverage + cov[r]
    own[...] = coverage

    wts_copies = [
        remote(own, wts.at[t, slot], wts_send.at[t, slot], wts_recv.at[t, slot], wts_target(t, slot))
        for t, slot in moves
    ]

    def each_wts(act, side):
        valid = wts_receives if act == "wait_recv" else wts_sends
        for (t, slot), copy in zip(moves, wts_copies):
            if side != (slot > own_slot):
                continue
            pl.when(valid(t, slot))(getattr(copy, act))

    each_wts("start", False)
    wts[0, own_slot] = own[...]

    @pl.when(off == 0)
    def _():
        wts[0, self_step] = own[...]

    def down(vector):
        return jnp.broadcast_to(vector, (LANE, LANE)).T

    phases = LANE // 8

    def spread(source):
        pieces = []
        for k, d in enumerate(steps):
            block = pos + first + d
            inside = (block >= 0) & (block < n_pos)
            for h in range(row_halves):
                pieces.append(jnp.where(inside, source[k, h : h + 1, :], 0.0))
        line = jnp.concatenate(pieces, axis=1)
        reach = line.shape[1]
        line = jnp.broadcast_to(line, (8, reach))
        line = pltpu.roll(line, reach - 7, 1, stride=1, stride_axis=0)
        flip = 7 - lax.broadcasted_iota(jnp.int32, (8, reach), 0)
        line = jnp.take_along_axis(line, flip, axis=0)
        for h in range(phases):
            tables[h] = line if h == 0 else pltpu.roll(line, reach - 8 * h, 1)

    lane_8 = lax.broadcasted_iota(jnp.int32, (8, LANE), 1)
    low_lanes = lane_8 < SIDE

    def column(g, b):
        place = 8 * g + rows - TOP
        h, shift = (place % LANE) // 8, place // LANE * LANE
        if b < blocks:
            return tables[h, :, shift + b * LANE : shift + (b + 1) * LANE]
        after = tables[h, :, shift + cols : shift + cols + LANE]
        return jnp.where(low_lanes, after, tables[h, :, shift - LANE : shift])

    own_groups = range(TOP // 8, (TOP + rows) // 8)

    def column_sums(to, terms_of):
        sums = [None] * (blocks + 1)
        for g in own_groups:
            for b, term in enumerate(terms_of(g)):
                sums[b] = term if sums[b] is None else sums[b] + term
        for b, total in enumerate(sums):
            to[0, b : b + 1, :] = jnp.sum(total, axis=0, keepdims=True)

    def share(buffer, send, recv, peers):
        copies = [
            remote(buffer.at[0], buffer.at[r], send.at[r], recv.at[r], peers[r - 1]) for r in range(1, buffer.shape[0])
        ]
        for copy in copies:
            copy.start()
        return copies

    def gather(copies, buffer):
        for copy in copies:
            copy.wait_recv()
        total = buffer[0]
        for r in range(1, buffer.shape[0]):
            total = total + buffer[r]
        return total

    each_live("wait_recv")
    for h in range(row_halves):
        row_w[TOP + h * LANE : TOP + (h + 1) * LANE, :] = down(own_live[h : h + 1, :])
    spread(live)

    def live_terms(g):
        row = row_w[8 * g : 8 * g + 8, :]
        return [row * column(g, b) for b in range(blocks + 1)]

    column_sums(part_live, live_terms)
    part_live_copies = share(part_live, part_live_send, part_live_recv, part_peers)

    def weigh(low, high):
        gathered = wts[0, low:high]
        for t in range(1, far_offs):
            gathered = gathered + wts[t, low:high]
        lines[low:high] = live[low:high] / jnp.sqrt(gathered)

    each_wts("wait_recv", False)
    weigh(0, own_slot + 1)
    for h in range(row_halves):
        row_w[TOP + h * LANE : TOP + (h + 1) * LANE, :] = down(jnp.where(meets, lines[own_slot, h : h + 1, :], 0.0))
    spread(lines)

    def row_group(g):
        rows_g = slice(8 * g, 8 * g + 8)
        weight = row_w[rows_g, :]
        outs = []
        for b in range(blocks + 1):
            if b < blocks:
                count = cells[rows_g, b * LANE : (b + 1) * LANE]
            else:
                own_row = 8 * g - TOP
                if 0 <= own_row < rows:
                    k, at = own_row // third, own_row % third
                    after, before = strips_in[0, at : at + 8, :], strips_in[1, at : at + 8, :]
                    if k:
                        after = pltpu.roll(after, LANE - k * spare, 1)
                        before = pltpu.roll(before, k * spare, 1)
                else:
                    after, before = cells[rows_g, cols : cols + LANE], cells[rows_g, cols + LANE : cols + 2 * LANE]
                count = jnp.where(low_lanes, after, before)
            value = count * weight * column(g, b)
            normed_ref[rows_g, b * LANE : (b + 1) * LANE] = value
            outs.append(value)
        return outs

    each_halo(halos[:2], "wait_recv")
    column_sums(part, row_group)
    part_copies = share(part, part_send, part_recv, part_peers)

    each_wts("start", True)

    group_live[0] = gather(part_live_copies, part_live)
    group_live_copies = share(group_live, group_live_send, group_live_recv, group_peers)
    group[0] = gather(part_copies, part)
    group_copies = share(group, group_send, group_recv, group_peers)

    each_halo(halos[2:], "wait_recv")
    each_wts("wait_recv", True)
    weigh(own_slot + 1, n_slots)
    for side, h, low, place in ((0, row_halves - 1, LANE - TOP, 0), (1, 0, 0, TOP + rows)):
        block = pos + (1 if side else -1)
        inside = (block >= 0) & (block < n_pos)
        weight = jnp.where(inside & meets, lines[own_slot + 1 + side, h : h + 1, :], 0.0)
        row_w[place : place + TOP, :] = down(weight)[low : low + TOP, :]
    for g in list(range(TOP // 8)) + list(range((TOP + rows) // 8, (2 * TOP + rows) // 8)):
        row_group(g)

    for copy in cov_copies + part_copies + part_live_copies:
        copy.wait_send()
    each_halo(halos, "wait_send")
    each_wts("wait_send", False)
    each_wts("wait_send", True)
    each_live("wait_send")
    pairs = gather(group_live_copies, group_live)
    expected = gather(group_copies, group)
    lane = lax.broadcasted_iota(jnp.int32, expected.shape, 1)
    place = lax.broadcasted_iota(jnp.int32, expected.shape, 0) * LANE + lane
    needed = (place < cols + 2 * W) | (place >= width - 2 * W)
    place = off * cols + jnp.where(place < cols + SIDE, place, place - width)
    factor = pairs / jnp.where(expected > 0, expected, 1.0)
    factor_ref[...] = jnp.where(needed & (place >= 0) & (place < band), factor, 0.0)
    for copy in group_copies + group_live_copies:
        copy.wait_send()


def near(distance, lowest, highest):
    return (distance >= lowest) & (distance <= highest)


def both(mask_a, mask_b):
    return jnp.where(mask_a | mask_b, 1.0, 0.0).astype(jnp.bfloat16)


def halves(values):
    high = values.astype(jnp.bfloat16)
    return high, (values - high.astype(jnp.float32)).astype(jnp.bfloat16)


def window_kernel(normed_ref, factor_ref, donut_ref, lower_ref, donut, lower, sems):
    width = normed_ref.shape[1]
    rows, cols = donut_ref.shape
    blocks = width // LANE

    out_row = lax.broadcasted_iota(jnp.int32, (STEP, 2 * SPAN), 0)
    out_row = (out_row // 8) * 8 + 7 - lax.rem(out_row, 8)
    in_row = lax.broadcasted_iota(jnp.int32, (STEP, 2 * SPAN), 1)
    in_row = jnp.where(in_row < SPAN, in_row, in_row - SPAN)
    a = in_row - TOP - out_row
    down_table = jnp.concatenate(
        [
            both(near(a, P_SIZE + 1, W), near(a, -W, -P_SIZE - 1)),
            both(near(a, 1, P_SIZE), near(a, -P_SIZE, -1)),
            both(near(a, P_SIZE + 1, W), near(a, P_SIZE + 1, W)),
            both(near(a, 1, P_SIZE), near(a, 1, P_SIZE)),
        ],
        axis=0,
    )
    def side_tables(depth, wide, split):
        shape = (depth, wide)
        at = lax.broadcasted_iota(jnp.int32, shape, 0)
        if split:
            at = jnp.where(at < SIDE, at + wide, at - LANE)
        b = at - lax.broadcasted_iota(jnp.int32, shape, 1)
        return [
            both(near(b, 1, W), near(b, -W, -1)),
            both(near(b, P_SIZE + 1, W), near(b, -W, -P_SIZE - 1)),
            both(near(b, -W, -1), near(b, -W, -1)),
            both(near(b, -W, -P_SIZE - 1), near(b, -W, -P_SIZE - 1)),
        ]

    main_t, rim_t = side_tables(2 * LANE, 2 * LANE, False), side_tables(LANE, 2 * LANE, True)
    mid_t, edge_t = side_tables(LANE, LANE, False), side_tables(LANE, LANE, True)
    pair_table, last_table = [], []
    for k in (0, 2):
        pair_table.append(jnp.concatenate([main_t[k]] * 2 + [main_t[k + 1]] * 2 + [rim_t[k]] * 2 + [rim_t[k + 1]] * 2, axis=0))
        last_table.append(jnp.concatenate([mid_t[k], edge_t[k]] * 2 + [mid_t[k + 1], edge_t[k + 1]] * 2, axis=0))
    flip = 7 - lax.broadcasted_iota(jnp.int32, (8, cols), 0)
    cells_donut = (2 * W + 1) ** 2 - (2 * P_SIZE + 1) ** 2 - 4 * (W - P_SIZE)
    cells_lower = W * W - P_SIZE * P_SIZE
    factor = jnp.concatenate([factor_ref[b : b + 1, :] for b in range(blocks)], axis=1)

    copies = []

    def upright(start):
        ratios = normed_ref[start : start + SPAN, :] * factor
        level = pltpu.roll(ratios, 0, 1, stride=1, stride_axis=0)
        stacked = jnp.concatenate(halves(level), axis=0)
        summed = jnp.dot(down_table, stacked, preferred_element_type=jnp.float32)
        return ratios[TOP : TOP + STEP, :cols], summed

    lanes = lax.broadcasted_iota(jnp.int32, (STEP, LANE), 1)

    def sideways(summed, k):
        mains, rims = [], []
        x = summed[k * STEP : (k + 1) * STEP, :]
        pieces = [x[:, b * LANE : (b + 1) * LANE] for b in range(blocks)]
        rim = jnp.concatenate(
            [jnp.where(lanes < SIDE, pieces[(2 * c + 2) % blocks], pieces[(2 * c - 1) % blocks]) for c in range(blocks // 2)],
            axis=0,
        )
        last = jnp.concatenate([pieces[-1], jnp.where(lanes < SIDE, pieces[0], pieces[-2])], axis=1)
        main = jnp.concatenate([x[:, 2 * c * LANE : (2 * c + 2) * LANE] for c in range(blocks // 2)], axis=0)
        return halves(main), halves(rim), halves(last)

    def level_out(start, here, summed):
        for to, out_ref, out, k, cell_count in (
            (0, donut_ref, donut, 0, cells_donut),
            (1, lower_ref, lower, 2, cells_lower),
        ):
            (m0, r0, l0), (m1, r1, l1) = sideways(summed, k), sideways(summed, k + 1)
            tall = jnp.dot(jnp.concatenate(m0 + m1 + r0 + r1, axis=1), pair_table[k // 2], preferred_element_type=jnp.float32)
            end = jnp.dot(jnp.concatenate(l0 + l1, axis=1), last_table[k // 2], preferred_element_type=jnp.float32)
            flat = jnp.concatenate([tall[c * STEP : (c + 1) * STEP, :] for c in range(blocks // 2)] + [end], axis=1)
            for g in range(STEP // 8):
                rows_g = slice(8 * g, 8 * g + 8)
                back = pltpu.roll(flat[rows_g, :], width - TOP - 8 * g - 7, 1, stride=1, stride_axis=0)[:, :cols]
                back = jnp.take_along_axis(back, flip, axis=0)
                out[start + 8 * g : start + 8 * g + 8, :] = here[rows_g, :] / jnp.maximum(back / cell_count, 0.25)
            span = pl.ds(start, STEP)
            copies.append(pltpu.make_async_copy(out.at[span, :], out_ref.at[span, :], sems.at[to, start // STEP]))
            copies[-1].start()

    for start in range(0, rows, STEP):
        level_out(start, *upright(start))
    for copy in copies:
        copy.wait()


def windows(normed, factor):
    rows, cols = normed.shape[0] - 2 * TOP, normed.shape[1] - LANE
    out = jax.ShapeDtypeStruct((rows, cols), jnp.float32)
    return pl.pallas_call(
        window_kernel,
        out_shape=(out, out),
        in_specs=[pl.BlockSpec(memory_space=pltpu.VMEM), pl.BlockSpec(memory_space=pltpu.VMEM)],
        out_specs=(pl.BlockSpec(memory_space=pltpu.HBM), pl.BlockSpec(memory_space=pltpu.HBM)),
        scratch_shapes=[
            pltpu.VMEM((rows, cols), jnp.float32),
            pltpu.VMEM((rows, cols), jnp.float32),
            pltpu.SemaphoreType.DMA((2, rows // STEP)),
        ],
        compiler_params=pltpu.CompilerParams(vmem_limit_bytes=32 * 1024 * 1024),
        name="windows",
    )(normed, factor)


def local(counts, bin_mask):
    rows, cols = counts.shape
    n_pos = lax.axis_size("pos")
    n_off = lax.axis_size("off")
    inner = 8
    outer = n_pos // inner
    near_offs = 4
    far_offs = n_off // near_offs
    width = cols + LANE
    vecs = cols // LANE + 1
    n_slots = cols // rows + 6
    reach = (cols // rows + 3) * rows
    halves_n = rows // LANE
    third = -(-rows // 24) * 8
    dma = pltpu.SemaphoreType.DMA
    f32 = jnp.float32
    normed, factor = pl.pallas_call(
        functools.partial(comm_kernel, (n_pos, n_off)),
        out_shape=(
            pltpu.VMEM((rows + 2 * TOP, width), f32),
            pltpu.VMEM((vecs, LANE), f32),
        ),
        in_specs=[pl.BlockSpec(memory_space=pltpu.HBM), pl.BlockSpec(memory_space=pltpu.HBM)],
        out_specs=(pl.BlockSpec(memory_space=pltpu.VMEM), pl.BlockSpec(memory_space=pltpu.VMEM)),
        scratch_shapes=[
            pltpu.VMEM((rows + 2 * TOP, cols + 2 * LANE), f32),
            pltpu.VMEM((2, third, LANE), f32),
            pltpu.VMEM((2, third, LANE), f32),
            pltpu.VMEM((halves_n, LANE), jnp.int32),
            pltpu.VMEM((halves_n, LANE), f32),
            pltpu.VMEM((n_slots, halves_n, LANE), f32),
            pltpu.VMEM((near_offs, halves_n, LANE), f32),
            pltpu.VMEM((halves_n, LANE), f32),
            pltpu.VMEM((far_offs, n_slots, halves_n, LANE), f32),
            pltpu.VMEM((n_slots, halves_n, LANE), f32),
            pltpu.VMEM((rows + 2 * TOP, LANE), f32),
            pltpu.VMEM((LANE // 8, 8, reach), f32),
            pltpu.VMEM((inner, vecs, LANE), f32),
            pltpu.VMEM((outer, vecs, LANE), f32),
            pltpu.VMEM((inner, vecs, LANE), f32),
            pltpu.VMEM((outer, vecs, LANE), f32),
            dma,
            dma,
            dma((near_offs,)),
            dma((near_offs,)),
            dma((8,)),
            dma((8,)),
            dma((n_slots,)),
            dma((n_slots,)),
            dma((far_offs, n_slots)),
            dma((far_offs, n_slots)),
            dma((inner,)),
            dma((inner,)),
            dma((outer,)),
            dma((outer,)),
            dma((inner,)),
            dma((inner,)),
            dma((outer,)),
            dma((outer,)),
        ],
        compiler_params=pltpu.CompilerParams(
            collective_id=0, has_side_effects=True, vmem_limit_bytes=24 * 1024 * 1024
        ),
        name="comm",
    )(
        pltpu.with_memory_space_constraint(counts, pltpu.HBM),
        pltpu.with_memory_space_constraint(bin_mask.reshape(halves_n, LANE), pltpu.HBM),
    )
    return windows(normed, factor)


def solution(mesh):
    placed = (P("pos", "off"), P("pos"))
    return jax.shard_map(
        local,
        mesh=mesh,
        in_specs=placed,
        out_specs=(P("pos", "off"), P("pos", "off")),
        check_vma=False,
    )
```

```python
import functools

import jax
import jax.numpy as jnp
from jax import lax
from jax.experimental import pallas as pl
from jax.experimental.pallas import tpu as pltpu
from jax.sharding import PartitionSpec as P

W = 20
P_SIZE = 8
TOP = 24
LANE = 128
SIDE = 64
STEP = 64
SPAN = STEP + 2 * TOP
MESH = pl.DeviceIdType.MESH


def comm_kernel(
    sizes, counts_ref, mask_ref, normed_ref, factor_ref,
    cells, strips_out, strips_in, mask, own_live, live, cov, own, wts, lines, row_w, tables, part, group, part_live, group_live,
    load_sem, mask_sem, cov_send, cov_recv, halo_send, halo_recv, live_send, live_recv, wts_send, wts_recv,
    part_send, part_recv, group_send, group_recv, part_live_send, part_live_recv, group_live_send, group_live_recv,
):
    n_pos, n_off = sizes
    rows, cols = counts_ref.shape
    width = cols + LANE
    blocks = cols // LANE
    ratio = cols // rows
    near_offs = cov.shape[0]
    far_offs = n_off // near_offs
    inner = part.shape[0]
    outer = group.shape[0]
    pos = lax.axis_index("pos")
    off = lax.axis_index("off")
    total_bins = rows * n_pos
    band = cols * n_off
    row_halves = rows // LANE
    third = strips_in.shape[1]

    def at_pos(k):
        return lax.rem(pos + (k + n_pos), n_pos)

    def at_off(k):
        return lax.rem(off + (k + n_off), n_off)

    first = ratio * off
    far = off // near_offs
    near = off - far * near_offs
    quot = pos // inner
    rank = pos - quot * inner
    cov_peers = [(pos, far * near_offs + lax.rem(near + r, near_offs)) for r in range(1, near_offs)]

    def cov_source(r):
        return far * near_offs + lax.rem(near - r + near_offs, near_offs)

    def counts_of(r):
        return pos + ratio * cov_source(r) < n_pos

    halo_moves = [(0, -1), (0, 1), (-1, 0), (1, 0), (-1, -1), (-1, 1), (1, -1), (1, 1)]
    steps = list(range(-1, ratio + 2))
    n_steps = len(steps)
    self_step = steps.index(0)
    own_slot = n_steps
    n_slots = n_steps + 3
    part_peers = [(quot * inner + lax.rem(rank + r, inner), off) for r in range(1, inner)]
    group_peers = [(lax.rem(quot + r, outer) * inner + rank, off) for r in range(1, outer)]

    def wts_target(t, slot):
        there = lax.rem(far + t, far_offs) * near_offs + near
        if slot < n_steps:
            return (lax.rem(pos - ratio * there - steps[slot] + n_pos, n_pos), there)
        return (at_pos((0, 1, -1)[slot - n_steps]), there)

    def wts_source(t, slot):
        there = lax.rem(far - t + far_offs, far_offs) * near_offs + near
        if slot < n_steps:
            return (lax.rem(pos + first + steps[slot] + n_pos, n_pos), there)
        return (at_pos((0, -1, 1)[slot - n_steps]), there)

    meets = pos + first + steps[0] < n_pos

    def within(place):
        return (place >= 0) & (place < n_pos)

    def wts_sends(t, slot):
        there = lax.rem(far + t, far_offs) * near_offs + near
        if slot < n_steps:
            valid = within(pos - ratio * there - steps[slot])
            return valid & (off > 0) if t == 0 and slot == self_step else valid
        to = pos + (0, 1, -1)[slot - n_steps]
        return within(to) & (to + ratio * there + steps[0] < n_pos)

    def wts_receives(t, slot):
        if slot < n_steps:
            valid = within(pos + first + steps[slot])
            return valid & (off > 0) if t == 0 and slot == self_step else valid
        return within(pos + (0, -1, 1)[slot - n_steps]) & meets

    moves = []
    for t in list(range(1, far_offs)) + [0]:
        for slot in range(n_slots):
            if t or slot != own_slot:
                moves.append((t, slot))
    live_slots = [slot for slot in range(n_slots) if slot != own_slot]

    load = pltpu.make_async_copy(counts_ref, cells.at[pl.ds(TOP, rows), pl.ds(0, cols)], load_sem)
    load.start()
    load_mask = pltpu.make_async_copy(mask_ref, mask, mask_sem)
    load_mask.start()

    def sends(b):
        return off > 0 if b < 0 else off < n_off - 1

    barrier = pltpu.get_barrier_semaphore()

    def greet(device):
        pl.semaphore_signal(barrier, inc=1, device_id=device, device_id_type=MESH)

    for t, slot in moves:
        pl.when(wts_receives(t, slot))(functools.partial(greet, wts_source(t, slot)))
    for r in range(1, near_offs):
        pl.when(counts_of(r))(functools.partial(greet, (pos, cov_source(r))))
    for a, b in halo_moves:
        source = (at_pos(-a), at_off(-b))
        if b == 0:
            greet(source)
        else:
            pl.when(sends(-b))(functools.partial(greet, source))
    for device in part_peers + group_peers:
        greet(device)

    @pl.when(off == 0)
    def _():
        strips_in[1] = jnp.zeros(strips_in.shape[1:], jnp.float32)
        for place in (0, TOP + rows):
            cells[place : place + TOP, cols + LANE :] = jnp.zeros((TOP, LANE), jnp.float32)

    @pl.when(off == n_off - 1)
    def _():
        strips_in[0] = jnp.zeros(strips_in.shape[1:], jnp.float32)
        for place in (0, TOP + rows):
            cells[place : place + TOP, cols : cols + LANE] = jnp.zeros((TOP, LANE), jnp.float32)

    load.wait()

    base = pos * rows + off * cols
    acc = None
    for b in range(blocks):
        row_i = lax.broadcasted_iota(jnp.int32, (rows, LANE), 0)
        col_i = lax.broadcasted_iota(jnp.int32, (rows, LANE), 1)
        piece = cells[TOP : TOP + rows, b * LANE : (b + 1) * LANE]
        piece = jnp.where(row_i + col_i < total_bins - base - b * LANE, piece, 0.0)
        acc = piece if acc is None else acc + piece
    for h in range(row_halves):
        turned = acc[h * LANE : (h + 1) * LANE, :].T
        cov[0, h : h + 1, :] = jnp.sum(turned, axis=0, keepdims=True)
    load_mask.wait()
    own_live[...] = mask[...].astype(jnp.float32)

    n_greet = len(part_peers) + len(group_peers) + jnp.where(pos + first < n_pos, len(cov_peers), 0)
    for _, b in halo_moves:
        n_greet = n_greet + (jnp.where(sends(b), 1, 0) if b else 1)
    for t, slot in moves:
        n_greet = n_greet + jnp.where(wts_sends(t, slot), 1, 0)
    pl.semaphore_wait(barrier, n_greet)

    def remote(src, dst, send, recv, device):
        return pltpu.make_async_remote_copy(
            src_ref=src, dst_ref=dst, send_sem=send, recv_sem=recv, device_id=device, device_id_type=MESH
        )

    cov_copies = [
        remote(cov.at[0], cov.at[r], cov_send.at[r], cov_recv.at[r], cov_peers[r - 1]) for r in range(1, near_offs)
    ]
    for copy in cov_copies:
        pl.when(pos + first < n_pos)(copy.start)

    live_copies = [
        remote(own_live, live.at[k], live_send.at[k], live_recv.at[k], wts_target(0, k)) for k in live_slots
    ]

    def each_live(act):
        valid = wts_receives if act == "wait_recv" else wts_sends
        for k, copy in zip(live_slots, live_copies):
            pl.when(valid(0, k))(getattr(copy, act))

    each_live("start")
    live[own_slot] = own_live[...]

    @pl.when(off == 0)
    def _():
        live[self_step] = own_live[...]

    spans = {-1: (pl.ds(0, TOP), pl.ds(TOP + rows, TOP)), 1: (pl.ds(rows - TOP, TOP), pl.ds(0, TOP))}
    strips = {
        -1: (pl.ds(0, LANE), pl.ds(cols, LANE)),
        1: (pl.ds(cols - LANE, LANE), pl.ds(cols + LANE, LANE)),
        0: (pl.ds(0, cols), pl.ds(0, cols)),
    }
    halo_copies = []
    for k, (a, b) in enumerate(halo_moves):
        if a == 0:
            side = 0 if b < 0 else 1
            ends = strips_out.at[side], strips_in.at[side]
        else:
            ends = counts_ref.at[spans[a][0], strips[b][0]], cells.at[spans[a][1], strips[b][1]]
        halo_copies.append(remote(*ends, halo_send.at[k], halo_recv.at[k], (at_pos(a), at_off(b))))

    def each_halo(copies, act):
        for (a, b), copy in copies:
            if b == 0:
                getattr(copy, act)()
            elif act == "wait_recv":
                pl.when(sends(-b))(copy.wait_recv)
            else:
                pl.when(sends(b))(getattr(copy, act))

    halos = list(zip(halo_moves, halo_copies))
    each_halo(halos[2:], "start")

    spare = LANE // 3
    lane_t = lax.broadcasted_iota(jnp.int32, (third, LANE), 1)
    for side in (0, 1):
        packed = None
        for k in range(3):
            low = TOP + k * third
            high = min(low + third, TOP + rows)
            piece = cells[low:high, 0:LANE] if side == 0 else cells[low:high, cols - LANE : cols]
            if high - low < third:
                piece = jnp.concatenate([piece, jnp.zeros((third - high + low, LANE), jnp.float32)], axis=0)
            if side == 0:
                piece = pltpu.roll(piece, k * spare, 1) if k else piece
                here = (lane_t >= k * spare) & (lane_t < (k + 1) * spare)
            else:
                piece = pltpu.roll(piece, LANE - k * spare, 1) if k else piece
                here = (lane_t < LANE - k * spare) & (lane_t >= LANE - (k + 1) * spare)
            packed = jnp.where(here, piece, 0.0 if packed is None else packed)
        strips_out[side] = packed

    each_halo(halos[:2], "start")

    for r, copy in enumerate(cov_copies, 1):
        pl.when(counts_of(r))(copy.wait_recv)
    coverage = cov[0]
    for r in range(1, near_offs):
        coverage = coverage + jnp.where(counts_of(r), cov[r], 0.0)
    own[...] = coverage

    wts_copies = [
        remote(own, wts.at[t, slot], wts_send.at[t, slot], wts_recv.at[t, slot], wts_target(t, slot))
        for t, slot in moves
    ]

    def each_wts(act, side):
        valid = wts_receives if act == "wait_recv" else wts_sends
        for (t, slot), copy in zip(moves, wts_copies):
            if side != (slot > own_slot):
                continue
            pl.when(valid(t, slot))(getattr(copy, act))

    each_wts("start", False)
    wts[0, own_slot] = own[...]

    @pl.when(off == 0)
    def _():
        wts[0, self_step] = own[...]

    def down(vector):
        return jnp.broadcast_to(vector, (LANE, LANE)).T

    phases = LANE // 8

    def spread(source):
        pieces = []
        for k, d in enumerate(steps):
            block = pos + first + d
            inside = (block >= 0) & (block < n_pos)
            for h in range(row_halves):
                pieces.append(jnp.where(inside, source[k, h : h + 1, :], 0.0))
        line = jnp.concatenate(pieces, axis=1)
        reach = line.shape[1]
        line = jnp.broadcast_to(line, (8, reach))
        line = pltpu.roll(line, reach - 7, 1, stride=1, stride_axis=0)
        flip = 7 - lax.broadcasted_iota(jnp.int32, (8, reach), 0)
        line = jnp.take_along_axis(line, flip, axis=0)
        for h in range(phases):
            tables[h] = line if h == 0 else pltpu.roll(line, reach - 8 * h, 1)

    lane_8 = lax.broadcasted_iota(jnp.int32, (8, LANE), 1)
    low_lanes = lane_8 < SIDE

    def column(g, b):
        place = 8 * g + rows - TOP
        h, shift = (place % LANE) // 8, place // LANE * LANE
        if b < blocks:
            return tables[h, :, shift + b * LANE : shift + (b + 1) * LANE]
        after = tables[h, :, shift + cols : shift + cols + LANE]
        return jnp.where(low_lanes, after, tables[h, :, shift - LANE : shift])

    own_groups = range(TOP // 8, (TOP + rows) // 8)

    def column_sums(to, terms_of):
        sums = [None] * (blocks + 1)
        for g in own_groups:
            for b, term in enumerate(terms_of(g)):
                sums[b] = term if sums[b] is None else sums[b] + term
        for b, total in enumerate(sums):
            to[0, b : b + 1, :] = jnp.sum(total, axis=0, keepdims=True)

    def share(buffer, send, recv, peers):
        copies = [
            remote(buffer.at[0], buffer.at[r], send.at[r], recv.at[r], peers[r - 1]) for r in range(1, buffer.shape[0])
        ]
        for copy in copies:
            copy.start()
        return copies

    def gather(copies, buffer):
        for copy in copies:
            copy.wait_recv()
        total = buffer[0]
        for r in range(1, buffer.shape[0]):
            total = total + buffer[r]
        return total

    each_live("wait_recv")
    for h in range(row_halves):
        row_w[TOP + h * LANE : TOP + (h + 1) * LANE, :] = down(own_live[h : h + 1, :])
    spread(live)

    def live_terms(g):
        row = row_w[8 * g : 8 * g + 8, :]
        return [row * column(g, b) for b in range(blocks + 1)]

    column_sums(part_live, live_terms)
    part_live_copies = share(part_live, part_live_send, part_live_recv, part_peers)

    def weigh(low, high):
        gathered = wts[0, low:high]
        for t in range(1, far_offs):
            gathered = gathered + wts[t, low:high]
        lines[low:high] = live[low:high] / jnp.sqrt(gathered)

    each_wts("wait_recv", False)
    weigh(0, own_slot + 1)
    for h in range(row_halves):
        row_w[TOP + h * LANE : TOP + (h + 1) * LANE, :] = down(jnp.where(meets, lines[own_slot, h : h + 1, :], 0.0))
    spread(lines)

    def row_group(g):
        rows_g = slice(8 * g, 8 * g + 8)
        weight = row_w[rows_g, :]
        outs = []
        for b in range(blocks + 1):
            if b < blocks:
                count = cells[rows_g, b * LANE : (b + 1) * LANE]
            else:
                own_row = 8 * g - TOP
                if 0 <= own_row < rows:
                    k, at = own_row // third, own_row % third
                    after, before = strips_in[0, at : at + 8, :], strips_in[1, at : at + 8, :]
                    if k:
                        after = pltpu.roll(after, LANE - k * spare, 1)
                        before = pltpu.roll(before, k * spare, 1)
                else:
                    after, before = cells[rows_g, cols : cols + LANE], cells[rows_g, cols + LANE : cols + 2 * LANE]
                count = jnp.where(low_lanes, after, before)
            value = count * weight * column(g, b)
            normed_ref[rows_g, b * LANE : (b + 1) * LANE] = value
            outs.append(value)
        return outs

    each_halo(halos[:2], "wait_recv")
    column_sums(part, row_group)
    part_copies = share(part, part_send, part_recv, part_peers)

    each_wts("start", True)

    group_live[0] = gather(part_live_copies, part_live)
    group_live_copies = share(group_live, group_live_send, group_live_recv, group_peers)
    group[0] = gather(part_copies, part)
    group_copies = share(group, group_send, group_recv, group_peers)

    each_halo(halos[2:], "wait_recv")
    each_wts("wait_recv", True)
    weigh(own_slot + 1, n_slots)
    for side, h, low, place in ((0, row_halves - 1, LANE - TOP, 0), (1, 0, 0, TOP + rows)):
        block = pos + (1 if side else -1)
        inside = (block >= 0) & (block < n_pos)
        weight = jnp.where(inside & meets, lines[own_slot + 1 + side, h : h + 1, :], 0.0)
        row_w[place : place + TOP, :] = down(weight)[low : low + TOP, :]
    for g in list(range(TOP // 8)) + list(range((TOP + rows) // 8, (2 * TOP + rows) // 8)):
        row_group(g)

    for copy in cov_copies:
        pl.when(pos + first < n_pos)(copy.wait_send)
    for copy in part_copies + part_live_copies:
        copy.wait_send()
    each_halo(halos, "wait_send")
    each_wts("wait_send", False)
    each_wts("wait_send", True)
    each_live("wait_send")
    pairs = gather(group_live_copies, group_live)
    expected = gather(group_copies, group)
    lane = lax.broadcasted_iota(jnp.int32, expected.shape, 1)
    place = lax.broadcasted_iota(jnp.int32, expected.shape, 0) * LANE + lane
    needed = (place < cols + 2 * W) | (place >= width - 2 * W)
    place = off * cols + jnp.where(place < cols + SIDE, place, place - width)
    factor = pairs / jnp.where(expected > 0, expected, 1.0)
    factor_ref[...] = jnp.where(needed & (place >= 0) & (place < band), factor, 0.0)
    for copy in group_copies + group_live_copies:
        copy.wait_send()


def near(distance, lowest, highest):
    return (distance >= lowest) & (distance <= highest)


def both(mask_a, mask_b):
    return jnp.where(mask_a | mask_b, 1.0, 0.0).astype(jnp.bfloat16)


def halves(values):
    high = values.astype(jnp.bfloat16)
    return high, (values - high.astype(jnp.float32)).astype(jnp.bfloat16)


def window_kernel(normed_ref, factor_ref, donut_ref, lower_ref, donut, lower, sems):
    width = normed_ref.shape[1]
    rows, cols = donut_ref.shape
    blocks = width // LANE

    out_row = lax.broadcasted_iota(jnp.int32, (STEP, 2 * SPAN), 0)
    out_row = (out_row // 8) * 8 + 7 - lax.rem(out_row, 8)
    in_row = lax.broadcasted_iota(jnp.int32, (STEP, 2 * SPAN), 1)
    in_row = jnp.where(in_row < SPAN, in_row, in_row - SPAN)
    a = in_row - TOP - out_row
    down_table = jnp.concatenate(
        [
            both(near(a, P_SIZE + 1, W), near(a, -W, -P_SIZE - 1)),
            both(near(a, 1, P_SIZE), near(a, -P_SIZE, -1)),
            both(near(a, P_SIZE + 1, W), near(a, P_SIZE + 1, W)),
            both(near(a, 1, P_SIZE), near(a, 1, P_SIZE)),
        ],
        axis=0,
    )
    def side_tables(depth, wide, split):
        shape = (depth, wide)
        at = lax.broadcasted_iota(jnp.int32, shape, 0)
        if split:
            at = jnp.where(at < SIDE, at + wide, at - LANE)
        b = at - lax.broadcasted_iota(jnp.int32, shape, 1)
        return [
            both(near(b, 1, W), near(b, -W, -1)),
            both(near(b, P_SIZE + 1, W), near(b, -W, -P_SIZE - 1)),
            both(near(b, -W, -1), near(b, -W, -1)),
            both(near(b, -W, -P_SIZE - 1), near(b, -W, -P_SIZE - 1)),
        ]

    main_t, rim_t = side_tables(2 * LANE, 2 * LANE, False), side_tables(LANE, 2 * LANE, True)
    mid_t, edge_t = side_tables(LANE, LANE, False), side_tables(LANE, LANE, True)
    pair_table, last_table = [], []
    for k in (0, 2):
        pair_table.append(jnp.concatenate([main_t[k]] * 2 + [main_t[k + 1]] * 2 + [rim_t[k]] * 2 + [rim_t[k + 1]] * 2, axis=0))
        last_table.append(jnp.concatenate([mid_t[k], edge_t[k]] * 2 + [mid_t[k + 1], edge_t[k + 1]] * 2, axis=0))
    flip = 7 - lax.broadcasted_iota(jnp.int32, (8, cols), 0)
    cells_donut = (2 * W + 1) ** 2 - (2 * P_SIZE + 1) ** 2 - 4 * (W - P_SIZE)
    cells_lower = W * W - P_SIZE * P_SIZE
    factor = jnp.concatenate([factor_ref[b : b + 1, :] for b in range(blocks)], axis=1)

    copies = []

    def upright(start):
        ratios = normed_ref[start : start + SPAN, :] * factor
        level = pltpu.roll(ratios, 0, 1, stride=1, stride_axis=0)
        stacked = jnp.concatenate(halves(level), axis=0)
        summed = jnp.dot(down_table, stacked, preferred_element_type=jnp.float32)
        return ratios[TOP : TOP + STEP, :cols], summed

    lanes = lax.broadcasted_iota(jnp.int32, (STEP, LANE), 1)

    def sideways(summed, k):
        mains, rims = [], []
        x = summed[k * STEP : (k + 1) * STEP, :]
        pieces = [x[:, b * LANE : (b + 1) * LANE] for b in range(blocks)]
        rim = jnp.concatenate(
            [jnp.where(lanes < SIDE, pieces[(2 * c + 2) % blocks], pieces[(2 * c - 1) % blocks]) for c in range(blocks // 2)],
            axis=0,
        )
        last = jnp.concatenate([pieces[-1], jnp.where(lanes < SIDE, pieces[0], pieces[-2])], axis=1)
        main = jnp.concatenate([x[:, 2 * c * LANE : (2 * c + 2) * LANE] for c in range(blocks // 2)], axis=0)
        return halves(main), halves(rim), halves(last)

    def level_out(start, here, summed):
        for to, out_ref, out, k, cell_count in (
            (0, donut_ref, donut, 0, cells_donut),
            (1, lower_ref, lower, 2, cells_lower),
        ):
            (m0, r0, l0), (m1, r1, l1) = sideways(summed, k), sideways(summed, k + 1)
            tall = jnp.dot(jnp.concatenate(m0 + m1 + r0 + r1, axis=1), pair_table[k // 2], preferred_element_type=jnp.float32)
            end = jnp.dot(jnp.concatenate(l0 + l1, axis=1), last_table[k // 2], preferred_element_type=jnp.float32)
            flat = jnp.concatenate([tall[c * STEP : (c + 1) * STEP, :] for c in range(blocks // 2)] + [end], axis=1)
            for g in range(STEP // 8):
                rows_g = slice(8 * g, 8 * g + 8)
                back = pltpu.roll(flat[rows_g, :], width - TOP - 8 * g - 7, 1, stride=1, stride_axis=0)[:, :cols]
                back = jnp.take_along_axis(back, flip, axis=0)
                out[start + 8 * g : start + 8 * g + 8, :] = here[rows_g, :] / jnp.maximum(back / cell_count, 0.25)
            span = pl.ds(start, STEP)
            copies.append(pltpu.make_async_copy(out.at[span, :], out_ref.at[span, :], sems.at[to, start // STEP]))
            copies[-1].start()

    for start in range(0, rows, STEP):
        level_out(start, *upright(start))
    for copy in copies:
        copy.wait()


def windows(normed, factor):
    rows, cols = normed.shape[0] - 2 * TOP, normed.shape[1] - LANE
    out = jax.ShapeDtypeStruct((rows, cols), jnp.float32)
    return pl.pallas_call(
        window_kernel,
        out_shape=(out, out),
        in_specs=[pl.BlockSpec(memory_space=pltpu.VMEM), pl.BlockSpec(memory_space=pltpu.VMEM)],
        out_specs=(pl.BlockSpec(memory_space=pltpu.HBM), pl.BlockSpec(memory_space=pltpu.HBM)),
        scratch_shapes=[
            pltpu.VMEM((rows, cols), jnp.float32),
            pltpu.VMEM((rows, cols), jnp.float32),
            pltpu.SemaphoreType.DMA((2, rows // STEP)),
        ],
        compiler_params=pltpu.CompilerParams(vmem_limit_bytes=32 * 1024 * 1024),
        name="windows",
    )(normed, factor)


def local(counts, bin_mask):
    rows, cols = counts.shape
    n_pos = lax.axis_size("pos")
    n_off = lax.axis_size("off")
    inner = 8
    outer = n_pos // inner
    near_offs = 4
    far_offs = n_off // near_offs
    width = cols + LANE
    vecs = cols // LANE + 1
    n_slots = cols // rows + 6
    reach = (cols // rows + 3) * rows
    halves_n = rows // LANE
    third = -(-rows // 24) * 8
    dma = pltpu.SemaphoreType.DMA
    f32 = jnp.float32
    normed, factor = pl.pallas_call(
        functools.partial(comm_kernel, (n_pos, n_off)),
        out_shape=(
            pltpu.VMEM((rows + 2 * TOP, width), f32),
            pltpu.VMEM((vecs, LANE), f32),
        ),
        in_specs=[pl.BlockSpec(memory_space=pltpu.HBM), pl.BlockSpec(memory_space=pltpu.HBM)],
        out_specs=(pl.BlockSpec(memory_space=pltpu.VMEM), pl.BlockSpec(memory_space=pltpu.VMEM)),
        scratch_shapes=[
            pltpu.VMEM((rows + 2 * TOP, cols + 2 * LANE), f32),
            pltpu.VMEM((2, third, LANE), f32),
            pltpu.VMEM((2, third, LANE), f32),
            pltpu.VMEM((halves_n, LANE), jnp.int32),
            pltpu.VMEM((halves_n, LANE), f32),
            pltpu.VMEM((n_slots, halves_n, LANE), f32),
            pltpu.VMEM((near_offs, halves_n, LANE), f32),
            pltpu.VMEM((halves_n, LANE), f32),
            pltpu.VMEM((far_offs, n_slots, halves_n, LANE), f32),
            pltpu.VMEM((n_slots, halves_n, LANE), f32),
            pltpu.VMEM((rows + 2 * TOP, LANE), f32),
            pltpu.VMEM((LANE // 8, 8, reach), f32),
            pltpu.VMEM((inner, vecs, LANE), f32),
            pltpu.VMEM((outer, vecs, LANE), f32),
            pltpu.VMEM((inner, vecs, LANE), f32),
            pltpu.VMEM((outer, vecs, LANE), f32),
            dma,
            dma,
            dma((near_offs,)),
            dma((near_offs,)),
            dma((8,)),
            dma((8,)),
            dma((n_slots,)),
            dma((n_slots,)),
            dma((far_offs, n_slots)),
            dma((far_offs, n_slots)),
            dma((inner,)),
            dma((inner,)),
            dma((outer,)),
            dma((outer,)),
            dma((inner,)),
            dma((inner,)),
            dma((outer,)),
            dma((outer,)),
        ],
        compiler_params=pltpu.CompilerParams(
            collective_id=0, has_side_effects=True, vmem_limit_bytes=24 * 1024 * 1024
        ),
        name="comm",
    )(
        pltpu.with_memory_space_constraint(counts, pltpu.HBM),
        pltpu.with_memory_space_constraint(bin_mask.reshape(halves_n, LANE), pltpu.HBM),
    )
    return windows(normed, factor)


def solution(mesh):
    placed = (P("pos", "off"), P("pos"))
    return jax.shard_map(
        local,
        mesh=mesh,
        in_specs=placed,
        out_specs=(P("pos", "off"), P("pos", "off")),
        check_vma=False,
    )
```

```python
import functools

import jax
import jax.numpy as jnp
from jax import lax
from jax.experimental import pallas as pl
from jax.experimental.pallas import tpu as pltpu
from jax.sharding import PartitionSpec as P

W = 20
P_SIZE = 8
TOP = 24
LANE = 128
SIDE = 64
STEP = 64
SPAN = STEP + 2 * TOP
MESH = pl.DeviceIdType.MESH


def comm_kernel(
    sizes, counts_ref, mask_ref, normed_ref, factor_ref,
    cells, strips_out, strips_in, mask, own_live, live, cov, own, wts, lines, row_w, tables, part, group, part_live, group_live,
    load_sem, mask_sem, cov_send, cov_recv, halo_send, halo_recv, live_send, live_recv, wts_send, wts_recv,
    part_send, part_recv, group_send, group_recv, part_live_send, part_live_recv, group_live_send, group_live_recv,
):
    n_pos, n_off = sizes
    rows, cols = counts_ref.shape
    width = cols + LANE
    blocks = cols // LANE
    ratio = cols // rows
    near_offs = cov.shape[0]
    far_offs = n_off // near_offs
    inner = part.shape[0]
    outer = group.shape[0]
    pos = lax.axis_index("pos")
    off = lax.axis_index("off")
    total_bins = rows * n_pos
    band = cols * n_off
    row_halves = rows // LANE
    third = strips_in.shape[1]

    def at_pos(k):
        return lax.rem(pos + (k + n_pos), n_pos)

    def at_off(k):
        return lax.rem(off + (k + n_off), n_off)

    first = ratio * off
    far = off // near_offs
    near = off - far * near_offs
    quot = pos // inner
    rank = pos - quot * inner
    cov_peers = [(pos, far * near_offs + lax.rem(near + r, near_offs)) for r in range(1, near_offs)]
    halo_moves = [(0, -1), (0, 1), (-1, 0), (1, 0), (-1, -1), (-1, 1), (1, -1), (1, 1)]
    steps = list(range(-1, ratio + 2))
    n_steps = len(steps)
    self_step = steps.index(0)
    own_slot = n_steps
    n_slots = n_steps + 3
    part_peers = [(quot * inner + lax.rem(rank + r, inner), off) for r in range(1, inner)]
    group_peers = [(lax.rem(quot + r, outer) * inner + rank, off) for r in range(1, outer)]

    def wts_target(t, slot):
        there = lax.rem(far + t, far_offs) * near_offs + near
        if slot < n_steps:
            return (lax.rem(pos - ratio * there - steps[slot] + n_pos, n_pos), there)
        return (at_pos((0, 1, -1)[slot - n_steps]), there)

    def wts_source(t, slot):
        there = lax.rem(far - t + far_offs, far_offs) * near_offs + near
        if slot < n_steps:
            return (lax.rem(pos + first + steps[slot] + n_pos, n_pos), there)
        return (at_pos((0, -1, 1)[slot - n_steps]), there)

    meets = pos + first + steps[0] < n_pos

    def within(place):
        return (place >= 0) & (place < n_pos)

    def wts_sends(t, slot):
        there = lax.rem(far + t, far_offs) * near_offs + near
        if slot < n_steps:
            valid = within(pos - ratio * there - steps[slot])
            return valid & (off > 0) if t == 0 and slot == self_step else valid
        to = pos + (0, 1, -1)[slot - n_steps]
        return within(to) & (to + ratio * there + steps[0] < n_pos)

    def wts_receives(t, slot):
        if slot < n_steps:
            valid = within(pos + first + steps[slot])
            return valid & (off > 0) if t == 0 and slot == self_step else valid
        return within(pos + (0, -1, 1)[slot - n_steps]) & meets

    moves = []
    for t in list(range(1, far_offs)) + [0]:
        for slot in range(n_slots):
            if t or slot != own_slot:
                moves.append((t, slot))
    live_slots = [slot for slot in range(n_slots) if slot != own_slot]

    load = pltpu.make_async_copy(counts_ref, cells.at[pl.ds(TOP, rows), pl.ds(0, cols)], load_sem)
    load.start()
    load_mask = pltpu.make_async_copy(mask_ref, mask, mask_sem)
    load_mask.start()

    def sends(b):
        return off > 0 if b < 0 else off < n_off - 1

    barrier = pltpu.get_barrier_semaphore()

    def greet(device):
        pl.semaphore_signal(barrier, inc=1, device_id=device, device_id_type=MESH)

    for t, slot in moves:
        pl.when(wts_receives(t, slot))(functools.partial(greet, wts_source(t, slot)))
    for device in cov_peers:
        greet(device)
    for a, b in halo_moves:
        source = (at_pos(-a), at_off(-b))
        if b == 0:
            greet(source)
        else:
            pl.when(sends(-b))(functools.partial(greet, source))
    for device in part_peers + group_peers:
        greet(device)

    @pl.when(off == 0)
    def _():
        strips_in[1] = jnp.zeros(strips_in.shape[1:], jnp.float32)
        for place in (0, TOP + rows):
            cells[place : place + TOP, cols + LANE :] = jnp.zeros((TOP, LANE), jnp.float32)

    @pl.when(off == n_off - 1)
    def _():
        strips_in[0] = jnp.zeros(strips_in.shape[1:], jnp.float32)
        for place in (0, TOP + rows):
            cells[place : place + TOP, cols : cols + LANE] = jnp.zeros((TOP, LANE), jnp.float32)

    load.wait()

    base = pos * rows + off * cols
    acc = None
    for b in range(blocks):
        row_i = lax.broadcasted_iota(jnp.int32, (rows, LANE), 0)
        col_i = lax.broadcasted_iota(jnp.int32, (rows, LANE), 1)
        piece = cells[TOP : TOP + rows, b * LANE : (b + 1) * LANE]
        piece = jnp.where(row_i + col_i < total_bins - base - b * LANE, piece, 0.0)
        acc = piece if acc is None else acc + piece
    for h in range(row_halves):
        turned = acc[h * LANE : (h + 1) * LANE, :].T
        cov[0, h : h + 1, :] = jnp.sum(turned, axis=0, keepdims=True)
    load_mask.wait()
    own_live[...] = mask[...].astype(jnp.float32)

    n_greet = len(cov_peers) + len(part_peers) + len(group_peers)
    for _, b in halo_moves:
        n_greet = n_greet + (jnp.where(sends(b), 1, 0) if b else 1)
    for t, slot in moves:
        n_greet = n_greet + jnp.where(wts_sends(t, slot), 1, 0)
    pl.semaphore_wait(barrier, n_greet)

    def remote(src, dst, send, recv, device):
        return pltpu.make_async_remote_copy(
            src_ref=src, dst_ref=dst, send_sem=send, recv_sem=recv, device_id=device, device_id_type=MESH
        )

    cov_copies = [
        remote(cov.at[0], cov.at[r], cov_send.at[r], cov_recv.at[r], cov_peers[r - 1]) for r in range(1, near_offs)
    ]
    for copy in cov_copies:
        copy.start()

    live_copies = [
        remote(own_live, live.at[k], live_send.at[k], live_recv.at[k], wts_target(0, k)) for k in live_slots
    ]

    def each_live(act):
        valid = wts_receives if act == "wait_recv" else wts_sends
        for k, copy in zip(live_slots, live_copies):
            pl.when(valid(0, k))(getattr(copy, act))

    each_live("start")
    live[own_slot] = own_live[...]

    @pl.when(off == 0)
    def _():
        live[self_step] = own_live[...]

    spans = {-1: (pl.ds(0, TOP), pl.ds(TOP + rows, TOP)), 1: (pl.ds(rows - TOP, TOP), pl.ds(0, TOP))}
    strips = {
        -1: (pl.ds(0, LANE), pl.ds(cols, LANE)),
        1: (pl.ds(cols - LANE, LANE), pl.ds(cols + LANE, LANE)),
        0: (pl.ds(0, cols), pl.ds(0, cols)),
    }
    halo_copies = []
    for k, (a, b) in enumerate(halo_moves):
        if a == 0:
            side = 0 if b < 0 else 1
            ends = strips_out.at[side], strips_in.at[side]
        else:
            ends = counts_ref.at[spans[a][0], strips[b][0]], cells.at[spans[a][1], strips[b][1]]
        halo_copies.append(remote(*ends, halo_send.at[k], halo_recv.at[k], (at_pos(a), at_off(b))))

    def each_halo(copies, act):
        for (a, b), copy in copies:
            if b == 0:
                getattr(copy, act)()
            elif act == "wait_recv":
                pl.when(sends(-b))(copy.wait_recv)
            else:
                pl.when(sends(b))(getattr(copy, act))

    halos = list(zip(halo_moves, halo_copies))
    each_halo(halos[2:], "start")

    spare = LANE // 3
    lane_t = lax.broadcasted_iota(jnp.int32, (third, LANE), 1)
    for side in (0, 1):
        packed = None
        for k in range(3):
            low = TOP + k * third
            high = min(low + third, TOP + rows)
            piece = cells[low:high, 0:LANE] if side == 0 else cells[low:high, cols - LANE : cols]
            if high - low < third:
                piece = jnp.concatenate([piece, jnp.zeros((third - high + low, LANE), jnp.float32)], axis=0)
            if side == 0:
                piece = pltpu.roll(piece, k * spare, 1) if k else piece
                here = (lane_t >= k * spare) & (lane_t < (k + 1) * spare)
            else:
                piece = pltpu.roll(piece, LANE - k * spare, 1) if k else piece
                here = (lane_t < LANE - k * spare) & (lane_t >= LANE - (k + 1) * spare)
            packed = jnp.where(here, piece, 0.0 if packed is None else packed)
        strips_out[side] = packed

    each_halo(halos[:2], "start")

    for copy in cov_copies:
        copy.wait_recv()
    coverage = cov[0]
    for r in range(1, near_offs):
        coverage = coverage + cov[r]
    own[...] = coverage

    wts_copies = [
        remote(own, wts.at[t, slot], wts_send.at[t, slot], wts_recv.at[t, slot], wts_target(t, slot))
        for t, slot in moves
    ]

    def each_wts(act, side):
        valid = wts_receives if act == "wait_recv" else wts_sends
        for (t, slot), copy in zip(moves, wts_copies):
            if side != (slot > own_slot):
                continue
            pl.when(valid(t, slot))(getattr(copy, act))

    each_wts("start", False)
    wts[0, own_slot] = own[...]

    @pl.when(off == 0)
    def _():
        wts[0, self_step] = own[...]

    def down(vector):
        return jnp.broadcast_to(vector, (LANE, LANE)).T

    phases = LANE // 8

    def spread(source):
        pieces = []
        for k, d in enumerate(steps):
            block = pos + first + d
            inside = (block >= 0) & (block < n_pos)
            for h in range(row_halves):
                pieces.append(jnp.where(inside, source[k, h : h + 1, :], 0.0))
        line = jnp.concatenate(pieces, axis=1)
        reach = line.shape[1]
        line = jnp.broadcast_to(line, (8, reach))
        line = pltpu.roll(line, reach - 7, 1, stride=1, stride_axis=0)
        flip = 7 - lax.broadcasted_iota(jnp.int32, (8, reach), 0)
        line = jnp.take_along_axis(line, flip, axis=0)
        for h in range(phases):
            tables[h] = line if h == 0 else pltpu.roll(line, reach - 8 * h, 1)

    lane_8 = lax.broadcasted_iota(jnp.int32, (8, LANE), 1)
    low_lanes = lane_8 < SIDE

    def column(g, b):
        place = 8 * g + rows - TOP
        h, shift = (place % LANE) // 8, place // LANE * LANE
        if b < blocks:
            return tables[h, :, shift + b * LANE : shift + (b + 1) * LANE]
        after = tables[h, :, shift + cols : shift + cols + LANE]
        return jnp.where(low_lanes, after, tables[h, :, shift - LANE : shift])

    own_groups = range(TOP // 8, (TOP + rows) // 8)

    def column_sums(to, terms_of):
        sums = [None] * (blocks + 1)
        for g in own_groups:
            for b, term in enumerate(terms_of(g)):
                sums[b] = term if sums[b] is None else sums[b] + term
        for b, total in enumerate(sums):
            to[0, b : b + 1, :] = jnp.sum(total, axis=0, keepdims=True)

    def share(buffer, send, recv, peers):
        copies = [
            remote(buffer.at[0], buffer.at[r], send.at[r], recv.at[r], peers[r - 1]) for r in range(1, buffer.shape[0])
        ]
        for copy in copies:
            copy.start()
        return copies

    def gather(copies, buffer):
        for copy in copies:
            copy.wait_recv()
        total = buffer[0]
        for r in range(1, buffer.shape[0]):
            total = total + buffer[r]
        return total

    each_live("wait_recv")
    for h in range(row_halves):
        row_w[TOP + h * LANE : TOP + (h + 1) * LANE, :] = down(own_live[h : h + 1, :])
    spread(live)

    def live_terms(g):
        row = row_w[8 * g : 8 * g + 8, :]
        return [row * column(g, b) for b in range(blocks + 1)]

    column_sums(part_live, live_terms)
    part_live_copies = share(part_live, part_live_send, part_live_recv, part_peers)

    def weigh(low, high):
        gathered = wts[0, low:high]
        for t in range(1, far_offs):
            gathered = gathered + wts[t, low:high]
        lines[low:high] = live[low:high] / jnp.sqrt(gathered)

    each_wts("wait_recv", False)
    weigh(0, own_slot + 1)
    for h in range(row_halves):
        row_w[TOP + h * LANE : TOP + (h + 1) * LANE, :] = down(jnp.where(meets, lines[own_slot, h : h + 1, :], 0.0))
    spread(lines)

    def row_group(g):
        rows_g = slice(8 * g, 8 * g + 8)
        weight = row_w[rows_g, :]
        outs = []
        for b in range(blocks + 1):
            if b < blocks:
                count = cells[rows_g, b * LANE : (b + 1) * LANE]
            else:
                own_row = 8 * g - TOP
                if 0 <= own_row < rows:
                    k, at = own_row // third, own_row % third
                    after, before = strips_in[0, at : at + 8, :], strips_in[1, at : at + 8, :]
                    if k:
                        after = pltpu.roll(after, LANE - k * spare, 1)
                        before = pltpu.roll(before, k * spare, 1)
                else:
                    after, before = cells[rows_g, cols : cols + LANE], cells[rows_g, cols + LANE : cols + 2 * LANE]
                count = jnp.where(low_lanes, after, before)
            value = count * weight * column(g, b)
            normed_ref[rows_g, b * LANE : (b + 1) * LANE] = value
            outs.append(value)
        return outs

    each_halo(halos[:2], "wait_recv")
    column_sums(part, row_group)
    part_copies = share(part, part_send, part_recv, part_peers)

    each_wts("start", True)

    group_live[0] = gather(part_live_copies, part_live)
    group_live_copies = share(group_live, group_live_send, group_live_recv, group_peers)
    group[0] = gather(part_copies, part)
    group_copies = share(group, group_send, group_recv, group_peers)

    each_halo(halos[2:], "wait_recv")
    each_wts("wait_recv", True)
    weigh(own_slot + 1, n_slots)
    for side, h, low, place in ((0, row_halves - 1, LANE - TOP, 0), (1, 0, 0, TOP + rows)):
        block = pos + (1 if side else -1)
        inside = (block >= 0) & (block < n_pos)
        weight = jnp.where(inside & meets, lines[own_slot + 1 + side, h : h + 1, :], 0.0)
        row_w[place : place + TOP, :] = down(weight)[low : low + TOP, :]
    for g in list(range(TOP // 8)) + list(range((TOP + rows) // 8, (2 * TOP + rows) // 8)):
        row_group(g)

    for copy in cov_copies + part_copies + part_live_copies:
        copy.wait_send()
    each_halo(halos, "wait_send")
    each_wts("wait_send", False)
    each_wts("wait_send", True)
    each_live("wait_send")
    pairs = gather(group_live_copies, group_live)
    expected = gather(group_copies, group)
    lane = lax.broadcasted_iota(jnp.int32, expected.shape, 1)
    place = lax.broadcasted_iota(jnp.int32, expected.shape, 0) * LANE + lane
    needed = (place < cols + 2 * W) | (place >= width - 2 * W)
    place = off * cols + jnp.where(place < cols + SIDE, place, place - width)
    factor = pairs / jnp.where(expected > 0, expected, 1.0)
    factor_ref[...] = jnp.where(needed & (place >= 0) & (place < band), factor, 0.0)
    for copy in group_copies + group_live_copies:
        copy.wait_send()


def near(distance, lowest, highest):
    return (distance >= lowest) & (distance <= highest)


def both(mask_a, mask_b):
    return jnp.where(mask_a | mask_b, 1.0, 0.0).astype(jnp.bfloat16)


def halves(values):
    high = values.astype(jnp.bfloat16)
    return high, (values - high.astype(jnp.float32)).astype(jnp.bfloat16)


def window_kernel(normed_ref, factor_ref, donut_ref, lower_ref, donut, lower, sems):
    width = normed_ref.shape[1]
    rows, cols = donut_ref.shape
    blocks = width // LANE

    out_row = lax.broadcasted_iota(jnp.int32, (STEP, 2 * SPAN), 0)
    out_row = (out_row // 8) * 8 + 7 - lax.rem(out_row, 8)
    in_row = lax.broadcasted_iota(jnp.int32, (STEP, 2 * SPAN), 1)
    in_row = jnp.where(in_row < SPAN, in_row, in_row - SPAN)
    a = in_row - TOP - out_row
    down_table = jnp.concatenate(
        [
            both(near(a, P_SIZE + 1, W), near(a, -W, -P_SIZE - 1)),
            both(near(a, 1, P_SIZE), near(a, -P_SIZE, -1)),
            both(near(a, P_SIZE + 1, W), near(a, P_SIZE + 1, W)),
            both(near(a, 1, P_SIZE), near(a, 1, P_SIZE)),
        ],
        axis=0,
    )
    def side_tables(depth, wide, split):
        shape = (depth, wide)
        at = lax.broadcasted_iota(jnp.int32, shape, 0)
        if split:
            at = jnp.where(at < SIDE, at + wide, at - LANE)
        b = at - lax.broadcasted_iota(jnp.int32, shape, 1)
        return [
            both(near(b, 1, W), near(b, -W, -1)),
            both(near(b, P_SIZE + 1, W), near(b, -W, -P_SIZE - 1)),
            both(near(b, -W, -1), near(b, -W, -1)),
            both(near(b, -W, -P_SIZE - 1), near(b, -W, -P_SIZE - 1)),
        ]

    main_t, rim_t = side_tables(2 * LANE, 2 * LANE, False), side_tables(LANE, 2 * LANE, True)
    mid_t, edge_t = side_tables(LANE, LANE, False), side_tables(LANE, LANE, True)
    pair_table, last_table = [], []
    for k in (0, 2):
        pair_table.append(jnp.concatenate([main_t[k]] * 2 + [main_t[k + 1]] * 2 + [rim_t[k]] * 2 + [rim_t[k + 1]] * 2, axis=0))
        last_table.append(jnp.concatenate([mid_t[k], edge_t[k], mid_t[k + 1], edge_t[k + 1]], axis=0))
    flip = 7 - lax.broadcasted_iota(jnp.int32, (8, cols), 0)
    cells_donut = (2 * W + 1) ** 2 - (2 * P_SIZE + 1) ** 2 - 4 * (W - P_SIZE)
    cells_lower = W * W - P_SIZE * P_SIZE
    factor = jnp.concatenate([factor_ref[b : b + 1, :] for b in range(blocks)], axis=1)

    copies = []

    def upright(start):
        ratios = normed_ref[start : start + SPAN, :] * factor
        level = pltpu.roll(ratios, 0, 1, stride=1, stride_axis=0)
        stacked = jnp.concatenate(halves(level), axis=0)
        summed = jnp.dot(down_table, stacked, preferred_element_type=jnp.float32)
        return ratios[TOP : TOP + STEP, :cols], summed

    lanes = lax.broadcasted_iota(jnp.int32, (STEP, LANE), 1)

    def sideways(summed, k):
        mains, rims = [], []
        x = summed[k * STEP : (k + 1) * STEP, :]
        pieces = [x[:, b * LANE : (b + 1) * LANE] for b in range(blocks)]
        rim = jnp.concatenate(
            [jnp.where(lanes < SIDE, pieces[(2 * c + 2) % blocks], pieces[(2 * c - 1) % blocks]) for c in range(blocks // 2)],
            axis=0,
        )
        last = jnp.concatenate([pieces[-1], jnp.where(lanes < SIDE, pieces[0], pieces[-2])], axis=1)
        main = jnp.concatenate([x[:, 2 * c * LANE : (2 * c + 2) * LANE] for c in range(blocks // 2)], axis=0)
        return halves(main), halves(rim), halves(last)

    def level_out(start, here, summed):
        for to, out_ref, out, k, cell_count in (
            (0, donut_ref, donut, 0, cells_donut),
            (1, lower_ref, lower, 2, cells_lower),
        ):
            (m0, r0, l0), (m1, r1, l1) = sideways(summed, k), sideways(summed, k + 1)
            tall = jnp.dot(jnp.concatenate(m0 + m1 + r0 + r1, axis=1), pair_table[k // 2], preferred_element_type=jnp.float32)
            end = jnp.dot(
                jnp.concatenate([jnp.concatenate([l0[n], l1[n]], axis=1) for n in (0, 1)], axis=0),
                last_table[k // 2],
                preferred_element_type=jnp.float32,
            )
            end = end[:STEP] + end[STEP:]
            flat = jnp.concatenate([tall[c * STEP : (c + 1) * STEP, :] for c in range(blocks // 2)] + [end], axis=1)
            for g in range(STEP // 8):
                rows_g = slice(8 * g, 8 * g + 8)
                back = pltpu.roll(flat[rows_g, :], width - TOP - 8 * g - 7, 1, stride=1, stride_axis=0)[:, :cols]
                back = jnp.take_along_axis(back, flip, axis=0)
                out[start + 8 * g : start + 8 * g + 8, :] = here[rows_g, :] / jnp.maximum(back / cell_count, 0.25)
            span = pl.ds(start, STEP)
            copies.append(pltpu.make_async_copy(out.at[span, :], out_ref.at[span, :], sems.at[to, start // STEP]))
            copies[-1].start()

    for start in range(0, rows, STEP):
        level_out(start, *upright(start))
    for copy in copies:
        copy.wait()


def windows(normed, factor):
    rows, cols = normed.shape[0] - 2 * TOP, normed.shape[1] - LANE
    out = jax.ShapeDtypeStruct((rows, cols), jnp.float32)
    return pl.pallas_call(
        window_kernel,
        out_shape=(out, out),
        in_specs=[pl.BlockSpec(memory_space=pltpu.VMEM), pl.BlockSpec(memory_space=pltpu.VMEM)],
        out_specs=(pl.BlockSpec(memory_space=pltpu.HBM), pl.BlockSpec(memory_space=pltpu.HBM)),
        scratch_shapes=[
            pltpu.VMEM((rows, cols), jnp.float32),
            pltpu.VMEM((rows, cols), jnp.float32),
            pltpu.SemaphoreType.DMA((2, rows // STEP)),
        ],
        compiler_params=pltpu.CompilerParams(vmem_limit_bytes=32 * 1024 * 1024),
        name="windows",
    )(normed, factor)


def local(counts, bin_mask):
    rows, cols = counts.shape
    n_pos = lax.axis_size("pos")
    n_off = lax.axis_size("off")
    inner = 8
    outer = n_pos // inner
    near_offs = 4
    far_offs = n_off // near_offs
    width = cols + LANE
    vecs = cols // LANE + 1
    n_slots = cols // rows + 6
    reach = (cols // rows + 3) * rows
    halves_n = rows // LANE
    third = -(-rows // 24) * 8
    dma = pltpu.SemaphoreType.DMA
    f32 = jnp.float32
    normed, factor = pl.pallas_call(
        functools.partial(comm_kernel, (n_pos, n_off)),
        out_shape=(
            pltpu.VMEM((rows + 2 * TOP, width), f32),
            pltpu.VMEM((vecs, LANE), f32),
        ),
        in_specs=[pl.BlockSpec(memory_space=pltpu.HBM), pl.BlockSpec(memory_space=pltpu.HBM)],
        out_specs=(pl.BlockSpec(memory_space=pltpu.VMEM), pl.BlockSpec(memory_space=pltpu.VMEM)),
        scratch_shapes=[
            pltpu.VMEM((rows + 2 * TOP, cols + 2 * LANE), f32),
            pltpu.VMEM((2, third, LANE), f32),
            pltpu.VMEM((2, third, LANE), f32),
            pltpu.VMEM((halves_n, LANE), jnp.int32),
            pltpu.VMEM((halves_n, LANE), f32),
            pltpu.VMEM((n_slots, halves_n, LANE), f32),
            pltpu.VMEM((near_offs, halves_n, LANE), f32),
            pltpu.VMEM((halves_n, LANE), f32),
            pltpu.VMEM((far_offs, n_slots, halves_n, LANE), f32),
            pltpu.VMEM((n_slots, halves_n, LANE), f32),
            pltpu.VMEM((rows + 2 * TOP, LANE), f32),
            pltpu.VMEM((LANE // 8, 8, reach), f32),
            pltpu.VMEM((inner, vecs, LANE), f32),
            pltpu.VMEM((outer, vecs, LANE), f32),
            pltpu.VMEM((inner, vecs, LANE), f32),
            pltpu.VMEM((outer, vecs, LANE), f32),
            dma,
            dma,
            dma((near_offs,)),
            dma((near_offs,)),
            dma((8,)),
            dma((8,)),
            dma((n_slots,)),
            dma((n_slots,)),
            dma((far_offs, n_slots)),
            dma((far_offs, n_slots)),
            dma((inner,)),
            dma((inner,)),
            dma((outer,)),
            dma((outer,)),
            dma((inner,)),
            dma((inner,)),
            dma((outer,)),
            dma((outer,)),
        ],
        compiler_params=pltpu.CompilerParams(
            collective_id=0, has_side_effects=True, vmem_limit_bytes=24 * 1024 * 1024
        ),
        name="comm",
    )(
        pltpu.with_memory_space_constraint(counts, pltpu.HBM),
        pltpu.with_memory_space_constraint(bin_mask.reshape(halves_n, LANE), pltpu.HBM),
    )
    return windows(normed, factor)


def solution(mesh):
    placed = (P("pos", "off"), P("pos"))
    return jax.shard_map(
        local,
        mesh=mesh,
        in_specs=placed,
        out_specs=(P("pos", "off"), P("pos", "off")),
        check_vma=False,
    )
```
